128 devices in a mesh: section: 4 (over x_hi, core), tile: 32 (over x_lo, z, y).
Axes of the slice: x: 4 (x_hi: 2, x_lo: 2; x = x_hi * 2 + x_lo), y: 4, z: 4, core: 2. Of those that a mesh axis runs over, the one named last changes fastest.
Arguments:
- layer_input: bfloat16 [4, 3, 32, 16, 32, 128], P('section', None, 'tile'), may hold values from -6 to 6
- hidden_prev: bfloat16 [4, 3, 32, 16, 32, 128], P('section', None, 'tile'), may hold values from -0.8984375 to 0.8984375
- cell_prev: float32 [4, 3, 32, 16, 32, 128], P('section', None, 'tile'), may hold values from -6 to 6
- out_cot: bfloat16 [3, 32, 16, 32, 128], P(None, 'tile'), may hold values from -18 to 18
- bias: float32 [4, 512], P('section'), may hold values from -1 to 2
- master: float32 [4, 2304, 512], P('section', 'tile'), may hold values from -0.375 to 0.375
- moment1: float32 [4, 2304, 512], P('section', 'tile'), may hold values from -6 to 6
- moment2: float32 [4, 2304, 512], P('section', 'tile'), may hold values from 1 to 100
Outputs:
- input_cot: bfloat16 [4, 3, 32, 16, 32, 128], P('section', None, 'tile')
- new_master: float32 [4, 2304, 512], P('section', 'tile')
- new_moment1: float32 [4, 2304, 512], P('section', 'tile')
- new_moment2: float32 [4, 2304, 512], P('section', 'tile')
The draws below stay inside these ranges and needn't reach their ends.
All inputs are finite; a program needn't handle non-finite values.
Results may differ from the reference program's by a relative error of at most 0.012.
Values may be sent and summed in bfloat16 or wider, within the bound.
No kernel may reach another device: no remote copies, remote signals or barrier semaphores. Data moves between devices by JAX's collectives and lax.ppermute only.
A program may use at most 128 MiB of HBM per device.

```python
import math
import jax
import jax.numpy as jnp

C = 128
TH = 16
TW = 32
FRAMES = 3
TILE_ROWS = 4
LAYERS = 4
TILES = 32
G = 512
KW = 2304
N_SECTION = 4
N_TILE = 32


def level_of(key, extent, shards, low, top_value):
    factor_of = 1.0
    for dim, shards_of in shards:
        heights = jax.random.uniform(jax.random.fold_in(jax.random.fold_in(key, 6), dim), (shards_of,), jnp.float32, low / len(shards), top_value / len(shards))
        factor_of = factor_of * jnp.repeat(jnp.exp(heights), extent[dim] // shards_of).reshape((-1,) + (1,) * (len(extent) - 1 - dim))
    return factor_of


def noise(key, shape, scale, reach, shards=(), kind=jnp.bfloat16):
    gain = level_of(key, shape, shards, -0.22, 0.18) if shards else 1.0
    result = jax.random.normal(key, shape, jnp.float32) * scale * gain
    return jnp.minimum(jnp.maximum(result, -reach), reach).astype(kind)


def setup_inputs(seed: int = 0) -> dict:
    key_list = jax.random.split(jax.random.key(seed), 9)
    return {
        "layer_input": noise(key_list[0], (LAYERS, FRAMES, TILES, TH, TW, C), 1.0, 6.0, ((0, 4), (2, 32))),
        "hidden_prev": jnp.clip(jax.random.uniform(key_list[1], (LAYERS, FRAMES, TILES, TH, TW, C), jnp.float32, -0.8984375, 0.8984375) * level_of(key_list[1], (LAYERS, FRAMES, TILES, TH, TW, C), ((0, 4), (2, 32)), -0.4, 0.0), -0.8984375, 0.8984375).astype(jnp.bfloat16),
        "cell_prev": noise(key_list[2], (LAYERS, FRAMES, TILES, TH, TW, C), 1.0, 6.0, ((0, 4), (2, 32)), jnp.float32),
        "out_cot": noise(key_list[3], (FRAMES, TILES, TH, TW, C), 3.0, 18.0, ((1, 32),)),
        "bias": jnp.clip(-1.0 + 3.0 * jax.random.uniform(key_list[4], (LAYERS, G), jnp.float32) ** level_of(key_list[4], (LAYERS, G), ((0, 4),), -0.2, 0.2), -1.0, 2.0),
        "master": noise(key_list[5], (LAYERS, KW, G), (2 * C) ** -0.5, 0.375, ((0, 4), (1, 32)), jnp.float32),
        "moment1": noise(key_list[6], (LAYERS, KW, G), 1.0, 6.0, ((0, 4), (1, 32)), jnp.float32),
        "moment2": jnp.clip(jnp.exp(math.log(100.0) - 4.6051702 * jax.random.uniform(key_list[7], (LAYERS, KW, G), jnp.float32) ** level_of(key_list[7], (LAYERS, KW, G), ((0, 4), (1, 32)), -0.2, 0.2)), 1.0, 100.0),
    }


def to_grid(tiles):
    cols = N_TILE // TILE_ROWS
    width = tiles.shape[-1]
    shaped = tiles.reshape(TILE_ROWS, cols, TH, TW, width).transpose(0, 2, 1, 3, 4)
    return shaped.reshape(TILE_ROWS * TH, cols * TW, width)

def from_grid(flat):
    cols = N_TILE // TILE_ROWS
    width = flat.shape[-1]
    shaped = flat.reshape(TILE_ROWS, TH, cols, TW, width).transpose(0, 2, 1, 3, 4)
    return shaped.reshape(N_TILE, TH, TW, width)

def window_rows(field, flipped):
    rows_all, cols_all = (field.shape[0], field.shape[1])
    padded = jnp.pad(field, ((1, 1), (1, 1), (0, 0)))
    parts = []
    for shift_a in range(3):
        for shift_b in range(3):
            row0 = 2 - shift_a if flipped else shift_a
            col0 = 2 - shift_b if flipped else shift_b
            parts.append(padded[row0:row0 + rows_all, col0:col0 + cols_all, :])
    joined = jnp.concatenate(parts, -1)
    return joined.reshape(rows_all * cols_all, joined.shape[-1])

def reference(layer_input, hidden_prev, cell_prev, out_cot, bias, master, moment1, moment2):
    cells_all = N_TILE * TH * TW
    width = C
    grid_rows = TILE_ROWS * TH
    grid_cols = N_TILE // TILE_ROWS * TW
    layer_cots = [None] * N_SECTION
    grads = [None] * N_SECTION
    above_cots = [out_cot[frame] for frame in range(FRAMES)]
    for layer in reversed(range(N_SECTION)):
        kernel = master[layer].astype(jnp.bfloat16)
        kernel_t = kernel.reshape(9, 2 * width, 4 * width).transpose(0, 2, 1).reshape(9 * 4 * width, 2 * width)
        dh_rec = jnp.zeros((cells_all, width), jnp.float32)
        dc_rec = jnp.zeros((cells_all, width), jnp.float32)
        grad = jnp.zeros((18 * width, 4 * width), jnp.float32)
        cots = [None] * FRAMES
        for frame in reversed(range(FRAMES)):
            joined = jnp.concatenate([layer_input[layer, frame], hidden_prev[layer, frame]], -1)
            patches = window_rows(to_grid(joined), False)
            gates = jnp.dot(patches, kernel, preferred_element_type=jnp.float32) + bias[layer]
            gate_i = jax.nn.sigmoid(gates[:, :width])
            gate_f = jax.nn.sigmoid(gates[:, width:2 * width])
            gate_g = jnp.tanh(gates[:, 2 * width:3 * width])
            gate_o = jax.nn.sigmoid(gates[:, 3 * width:])
            c_prev = to_grid(cell_prev[layer, frame]).reshape(cells_all, width)
            cell = gate_f * c_prev + gate_i * gate_g
            tanh_cell = jnp.tanh(cell)
            above = to_grid(above_cots[frame]).reshape(cells_all, width).astype(jnp.float32)
            dh = above + dh_rec
            dc = dc_rec + dh * gate_o * (1.0 - tanh_cell * tanh_cell)
            dgates = jnp.concatenate([dc * gate_g * gate_i * (1.0 - gate_i), dc * c_prev * gate_f * (1.0 - gate_f), dc * gate_i * (1.0 - gate_g * gate_g), dh * tanh_cell * gate_o * (1.0 - gate_o)], -1).astype(jnp.bfloat16)
            dc_rec = dc * gate_f
            spread = window_rows(dgates.reshape(grid_rows, grid_cols, 4 * width), True)
            dz = jnp.dot(spread, kernel_t, preferred_element_type=jnp.float32)
            dh_rec = dz[:, width:]
            cots[frame] = from_grid(dz[:, :width].astype(jnp.bfloat16))
            grad = grad + jnp.dot(patches.T, dgates, preferred_element_type=jnp.float32)
        layer_cots[layer] = jnp.stack(cots, 0)
        above_cots = cots
        grads[layer] = grad
    grad_all = jnp.stack(grads, 0)
    input_cot = jnp.stack(layer_cots, 0)
    new_moment1 = 0.9 * moment1 + 0.1 * grad_all
    new_moment2 = 0.999 * moment2 + 0.001 * grad_all * grad_all
    fix1 = 1.0 - 0.9 ** 10
    fix2 = 1.0 - 0.999 ** 10
    step_size = new_moment1 / fix1 / (jnp.sqrt(new_moment2 / fix2) + 1e-08)
    new_master = master - 0.001 * step_size - 0.0001 * master
    return (input_cot, new_master, new_moment1, new_moment2)
```

```python
import jax
import jax.numpy as jnp
from jax import lax
from jax.sharding import PartitionSpec as P

TILE_ROWS = 4


def shifted(array, axis, by):
    size = lax.axis_size(axis)
    pairs = [(i, i + by) for i in range(size) if 0 <= i + by < size]
    return lax.ppermute(array, axis, pairs)


def extend(block, ncols, column):
    left_col = block[..., :, :1, :]
    right_col = block[..., :, -1:, :]
    from_left = shifted(right_col, "tile", 1)
    from_right = shifted(left_col, "tile", -1)
    from_left = jnp.where(column > 0, from_left, jnp.zeros_like(from_left))
    from_right = jnp.where(column < ncols - 1, from_right, jnp.zeros_like(from_right))
    wide = jnp.concatenate([from_left, block, from_right], -2)
    from_above = shifted(wide[..., -1:, :, :], "tile", ncols)
    from_below = shifted(wide[..., :1, :, :], "tile", -ncols)
    return jnp.concatenate([from_above, wide, from_below], -3)


def window_patches(padded, rows_in, cols_in, flipped):
    parts = []
    for shift_a in range(3):
        for shift_b in range(3):
            row0 = 2 - shift_a if flipped else shift_a
            col0 = 2 - shift_b if flipped else shift_b
            parts.append(padded[..., row0 : row0 + rows_in, col0 : col0 + cols_in, :])
    return jnp.concatenate(parts, -1)


def on_device(layer_input, hidden_prev, cell_prev, out_cot, bias, master, moment1, moment2):
    frames = layer_input.shape[1]
    rows_in = layer_input.shape[3]
    cols_in = layer_input.shape[4]
    width = layer_input.shape[5]
    cells = rows_in * cols_in
    ngate = 4 * width
    layer_count = lax.axis_size("section")
    layer_index = lax.axis_index("section")
    ntile = lax.axis_size("tile")
    tile = lax.axis_index("tile")
    ncols = ntile // TILE_ROWS
    column = tile % ncols
    own_rows = master[0].astype(jnp.bfloat16)
    kernel = lax.all_to_all(jnp.tile(own_rows, (ntile, 1)), "tile", 0, 0, tiled=True)
    kernel_t = kernel.reshape(9, 2 * width, ngate).transpose(0, 2, 1).reshape(9 * ngate, 2 * width)
    joined = jnp.concatenate([layer_input[0, :, 0], hidden_prev[0, :, 0]], -1)
    padded = extend(joined, ncols, column)
    patches = window_patches(padded, rows_in, cols_in, False).reshape(frames * cells, 18 * width)
    gates_all = (jnp.dot(patches, kernel, preferred_element_type=jnp.float32) + bias[0]).reshape(
        frames, cells, ngate
    )
    saved_cells = cell_prev[0, :, 0].reshape(frames, cells, width)
    own_cots = out_cot[:, 0]
    is_top = layer_index == layer_count - 1
    sent = jnp.zeros((rows_in, cols_in, width), jnp.bfloat16)
    dh_rec = jnp.zeros((cells, width), jnp.float32)
    dc_rec = jnp.zeros((cells, width), jnp.float32)
    input_cot = jnp.zeros((frames, rows_in, cols_in, width), jnp.bfloat16)
    kept = jnp.zeros((frames, cells, ngate), jnp.bfloat16)
    frame_ids = jnp.arange(frames, dtype=jnp.int32)
    for step in range(layer_count + frames - 1):
        frame = frames - 1 - step + (layer_count - 1) - layer_index
        valid = (frame >= 0) & (frame < frames)
        pick = jnp.clip(frame, 0, frames - 1)
        incoming = shifted(sent, "section", -1)
        own = lax.dynamic_index_in_dim(own_cots, pick, 0, False)
        above = jnp.where(is_top, own, incoming).astype(jnp.float32).reshape(cells, width)
        gates = lax.dynamic_index_in_dim(gates_all, pick, 0, False)
        c_prev = lax.dynamic_index_in_dim(saved_cells, pick, 0, False)
        gate_i = jax.nn.sigmoid(gates[:, :width])
        gate_f = jax.nn.sigmoid(gates[:, width : 2 * width])
        gate_g = jnp.tanh(gates[:, 2 * width : 3 * width])
        gate_o = jax.nn.sigmoid(gates[:, 3 * width :])
        tanh_cell = jnp.tanh(gate_f * c_prev + gate_i * gate_g)
        dh = above + dh_rec
        dc = dc_rec + dh * gate_o * (1.0 - tanh_cell * tanh_cell)
        dgates = jnp.concatenate(
            [
                dc * gate_g * gate_i * (1.0 - gate_i),
                dc * c_prev * gate_f * (1.0 - gate_f),
                dc * gate_i * (1.0 - gate_g * gate_g),
                dh * tanh_cell * gate_o * (1.0 - gate_o),
            ],
            -1,
        )
        dgates = jnp.where(valid, dgates, jnp.zeros_like(dgates)).astype(jnp.bfloat16)
        dc_rec = jnp.where(valid, dc * gate_f, dc_rec)
        spread_in = extend(dgates.reshape(1, rows_in, cols_in, ngate), ncols, column)
        spread = window_patches(spread_in, rows_in, cols_in, True).reshape(cells, 9 * ngate)
        dz = jnp.dot(spread, kernel_t, preferred_element_type=jnp.float32)
        dh_rec = jnp.where(valid, dz[:, width:], dh_rec)
        dx_frame = dz[:, :width].astype(jnp.bfloat16).reshape(rows_in, cols_in, width)
        sent = dx_frame
        slot = frame_ids == frame
        input_cot = jnp.where(slot[:, None, None, None], dx_frame[None], input_cot)
        kept = jnp.where(slot[:, None, None], dgates[None], kept)
    flat_dgates = kept.reshape(frames * cells, ngate)
    partial = lax.dot_general(
        patches, flat_dgates, (((0,), (0,)), ((), ())), preferred_element_type=jnp.float32
    ).astype(jnp.bfloat16)
    arrived = lax.all_to_all(partial, "tile", 0, 0, tiled=True)
    grad_rows = jnp.sum(arrived.reshape(ntile, -1, ngate).astype(jnp.float32), 0)
    new_moment1 = 0.9 * moment1[0] + 0.1 * grad_rows
    new_moment2 = 0.999 * moment2[0] + 0.001 * grad_rows * grad_rows
    fix1 = 1.0 - 0.9**10
    fix2 = 1.0 - 0.999**10
    step_size = new_moment1 / fix1 / (jnp.sqrt(new_moment2 / fix2) + 1e-08)
    new_master = master[0] - 0.001 * step_size - 0.0001 * master[0]
    return (input_cot[None, :, None], new_master[None], new_moment1[None], new_moment2[None])


def solution(mesh):
    return jax.shard_map(
        on_device,
        mesh=mesh,
        in_specs=(
            P("section", None, "tile", None, None, None),
            P("section", None, "tile", None, None, None),
            P("section", None, "tile", None, None, None),
            P(None, "tile", None, None, None),
            P("section", None),
            P("section", "tile", None),
            P("section", "tile", None),
            P("section", "tile", None),
        ),
        out_specs=(
            P("section", None, "tile", None, None, None),
            P("section", "tile", None),
            P("section", "tile", None),
            P("section", "tile", None),
        ),
        check_vma=False,
    )
```

```python
import functools

import jax
import jax.numpy as jnp
from jax import lax
from jax.experimental import pallas as pl
from jax.experimental.pallas import tpu as pltpu
from jax.sharding import PartitionSpec as P

TILE_ROWS = 4
BF = jnp.bfloat16
F32 = jnp.float32
SIDE = 8
LEAD = 16
VMEM_LIMIT = 56 * 1024 * 1024


def chunks(size, most):
    units = size // 16
    count = -(-units * 16 // most)
    out, at = [], 0
    for i in range(count):
        end = units * (i + 1) // count
        out.append((at * 16, (end - at) * 16))
        at = end
    return out


def in_vmem(shape, dtype):
    return pltpu.VMEM(shape, dtype)


def sigmoid(x):
    return 0.5 * jnp.tanh(0.5 * x) + 0.5


def gates_kernel(pitch, cells, width, zs_ref, ext_ref, mask_ref, kernel_ref, bias_ref, fac_ref):
    depth = 6 * width
    for start, size in chunks(cells, 480):
        total = bias_ref[...]
        for a in range(3):
            total = total + jnp.dot(
                zs_ref[pl.ds(start + a * pitch, size), :],
                kernel_ref[a * depth : (a + 1) * depth, :],
                preferred_element_type=F32,
            )
        here = pl.ds(start, size)
        mask = mask_ref[here, :].astype(F32)
        c_prev = ext_ref[pl.ds(start + pitch, size), 2 * width : 3 * width].astype(F32)
        i = sigmoid(total[:, :width])
        f = sigmoid(total[:, width : 2 * width])
        g = jnp.tanh(total[:, 2 * width : 3 * width])
        o = sigmoid(total[:, 3 * width :])
        tc = jnp.tanh(f * c_prev + i * g)
        fac_ref[here, 0:width] = o * (1.0 - tc * tc)
        fac_ref[here, width : 2 * width] = mask * g * i * (1.0 - i)
        fac_ref[here, 2 * width : 3 * width] = mask * c_prev * f * (1.0 - f)
        fac_ref[here, 3 * width : 4 * width] = mask * i * (1.0 - g * g)
        fac_ref[here, 4 * width : 5 * width] = mask * tc * o * (1.0 - o)
        fac_ref[here, 5 * width : 6 * width] = f


def step_kernel(step, layers, frames, pitch, rows, cols, width, *refs):
    ids_ref, kernel_t_ref = refs[0], refs[1]
    picks = [f for f in range(frames) if 0 <= frames - 1 - step + layers - 1 - f <= layers - 1]
    fac_refs = refs[2 : 2 + len(picks)]
    at = 2 + len(picks)
    first, tops = step == 0, step < frames
    ext_ref = refs[at] if tops else None
    at += 1 if tops else 0
    if not first:
        inc_ref, dh_ref, dc_ref = refs[at : at + 3]
        at += 3
    dx_ref, dxi_ref, dgi_ref, dhn_ref, dcn_ref, d_ref, p_ref = refs[at:]
    margin = frames + layers - 1 - step
    size_d = LEAD + (rows + 2 * margin) * pitch
    size_z = LEAD + (rows + 2 * margin - 2) * pitch
    frame = ids_ref[0] - step
    ngate = 4 * width

    def point(fac_ref, top_frame, pick):
        start_frame = pick == frames - 1
        for start, size in chunks(size_d, 256):
            here = pl.ds(start, size)
            there = pl.ds(start + step * pitch, size)
            if tops and pick == top_frame:
                own = ext_ref[pl.ds(start + (step + 1) * pitch, size), 3 * width :]
                above = own.astype(F32)
            else:
                above = inc_ref[here, :].astype(F32)
            dh = above
            if not start_frame:
                dh = dh + dh_ref[here, :]
            dc = dh * fac_ref[there, 0:width]
            if not start_frame:
                dc = dc + dc_ref[here, :]
            d_ref[here, 0:width] = (dc * fac_ref[there, width : 2 * width]).astype(BF)
            d_ref[here, width : 2 * width] = (dc * fac_ref[there, 2 * width : 3 * width]).astype(BF)
            d_ref[here, 2 * width : 3 * width] = (dc * fac_ref[there, 3 * width : 4 * width]).astype(BF)
            d_ref[here, 3 * width :] = (dh * fac_ref[there, 4 * width : 5 * width]).astype(BF)
            lo, hi = max(start, pitch), min(start + size, pitch + size_z)
            if hi > lo:
                rec = dc * fac_ref[there, 5 * width :]
                dcn_ref[lo - pitch : hi - pitch, :] = rec[lo - start : hi - start, :]

    top_frame = frames - 1 - step
    for number, pick in enumerate(picks):
        pl.when(frame == pick)(functools.partial(point, fac_refs[number], top_frame, pick))

    @pl.when((frame >= 0) & (frame < frames))
    def _():
        for row in range(rows):
            dgi_ref[row * cols : (row + 1) * cols, :] = d_ref[
                pl.ds(LEAD + (row + margin) * pitch, cols), :
            ]
        for side in range(3):
            p_ref[0:8, side * 2 * width : (side + 1) * 2 * width] = jnp.zeros((8, 2 * width), F32)
            p_ref[8 + size_z : 16 + size_z, side * 2 * width : (side + 1) * 2 * width] = jnp.zeros(
                (8, 2 * width), F32
            )
        for start, size in chunks(size_z, 448):
            total = None
            for a in range(3):
                part = jnp.dot(
                    d_ref[pl.ds(start + (2 - a) * pitch, size), :],
                    kernel_t_ref[a * ngate : (a + 1) * ngate, :],
                    preferred_element_type=F32,
                )
                total = part if total is None else total + part
            p_ref[pl.ds(8 + start, size), :] = total
        for start, size in chunks(size_z, 256):
            dz = (
                p_ref[pl.ds(8 + start, size), 2 * width : 4 * width]
                + p_ref[pl.ds(9 + start, size), 0 : 2 * width]
                + p_ref[pl.ds(7 + start, size), 4 * width :]
            )
            dx_ref[pl.ds(start, size), :] = dz[:, :width].astype(BF)
            dhn_ref[pl.ds(start, size), :] = dz[:, width:]
        for row in range(rows):
            dxi_ref[row * cols : (row + 1) * cols, :] = dx_ref[
                pl.ds(LEAD + (row + margin - 1) * pitch, cols), :
            ]


def spec_v():
    return pl.BlockSpec(memory_space=pltpu.VMEM)


def spec_s():
    return pl.BlockSpec(memory_space=pltpu.SMEM)


def row_pairs(ntile, ncols, by):
    return [(i, i + by * ncols) for i in range(ntile) if 0 <= i + by * ncols < ntile]


def col_pairs(ntile, ncols, by):
    return [(i, i + by) for i in range(ntile) if 0 <= i % ncols + by < ncols]


def on_device(layer_input, hidden_prev, cell_prev, out_cot, bias, master, moment1, moment2):
    frames, rows, cols, width = (layer_input.shape[i] for i in (1, 3, 4, 5))
    ngate = 4 * width
    layers = lax.axis_size("section")
    layer = lax.axis_index("section")
    ntile = lax.axis_size("tile")
    tile = lax.axis_index("tile")
    ncols = ntile // TILE_ROWS
    pitch = cols + 2 * SIDE
    edge = frames + layers - 1

    own_rows = master[0].astype(BF)
    kernel = lax.all_to_all(jnp.tile(own_rows, (ntile, 1)), "tile", 0, 0, tiled=True)
    kernel_t = kernel.reshape(3, 6 * width, ngate).transpose(0, 2, 1).reshape(3 * ngate, 6 * width)

    packed = jnp.concatenate(
        [layer_input[0, :, 0], hidden_prev[0, :, 0], cell_prev[0, :, 0].astype(BF), out_cot[:, 0]], -1
    )
    ext = [None] * frames
    for f in reversed(range(frames)):
        deep = edge + 1 - (frames - 1 - f)
        block = packed[f]
        above = lax.ppermute(block[rows - deep :], "tile", row_pairs(ntile, ncols, 1))
        below = lax.ppermute(block[:deep], "tile", row_pairs(ntile, ncols, -1))
        tall = jnp.concatenate([above, block, below], 0)
        left = lax.ppermute(tall[:, cols - SIDE :], "tile", col_pairs(ntile, ncols, 1))
        right = lax.ppermute(tall[:, :SIDE], "tile", col_pairs(ntile, ncols, -1))
        wide = jnp.concatenate([left, tall, right], 1)
        gap = edge + 1 - deep
        flat = wide.reshape(-1, 4 * width)
        ext[f] = jnp.pad(
            flat, ((LEAD - SIDE + gap * pitch, SIDE + gap * pitch), (0, 0))
        )
    size_e = LEAD + (rows + 2 * edge + 2) * pitch
    size_d = LEAD + (rows + 2 * edge) * pitch

    at = jnp.arange(size_d, dtype=jnp.int32) - LEAD + SIDE
    row_at = at // pitch - edge + (tile // ncols) * rows
    col_at = at % pitch - SIDE + (tile % ncols) * cols
    inside = (row_at >= 0) & (row_at < TILE_ROWS * rows) & (col_at >= 0) & (col_at < ncols * cols)
    mask = jnp.broadcast_to(inside[:, None], (size_d, width)).astype(BF)

    params = pltpu.CompilerParams(vmem_limit_bytes=VMEM_LIMIT)
    facs, patches = [None] * frames, [None] * frames
    for f in reversed(range(frames)):
        z = ext[f][:, : 2 * width]
        none = jnp.zeros((1, 2 * width), BF)
        zs = jnp.concatenate(
            [jnp.concatenate([none, z[:-1]], 0), z, jnp.concatenate([z[1:], none], 0)], -1
        )
        inner = zs[LEAD:].reshape(rows + 2 * edge + 2, pitch, 6 * width)[edge : edge + rows + 2, :cols]
        patches[f] = jnp.concatenate(
            [inner[a : a + rows].reshape(rows * cols, 6 * width) for a in range(3)], -1
        )
        facs[f] = pl.pallas_call(
            functools.partial(gates_kernel, pitch, size_d, width),
            out_shape=in_vmem((size_d, 6 * width), F32),
            in_specs=[spec_v()] * 5,
            out_specs=spec_v(),
            compiler_params=params,
            cost_estimate=pl.CostEstimate(
                flops=2 * size_d * 18 * width * ngate, bytes_accessed=10 << 20, transcendentals=size_d * 5 * width
            ),
        )(zs, ext[f], mask, kernel, bias)

    ids = (frames - 1 + layers - 1 - layer).astype(jnp.int32).reshape(1)
    state = []
    sent_dx, kept = [], []
    steps = layers + frames - 1
    for step in range(steps):
        margin = edge - step
        size_z = LEAD + (rows + 2 * margin - 2) * pitch
        picks = [f for f in range(frames) if 0 <= frames - 1 - step + layers - 1 - f <= layers - 1]
        args = [ids, kernel_t] + [facs[f] for f in picks]
        if step < frames:
            args.append(ext[frames - 1 - step])
        args += state
        dx, dxi, dgi, dh_rec, dc_rec = pl.pallas_call(
            functools.partial(step_kernel, step, layers, frames, pitch, rows, cols, width),
            out_shape=(
                jax.ShapeDtypeStruct((size_z, width), BF),
                jax.ShapeDtypeStruct((rows * cols, width), BF),
                jax.ShapeDtypeStruct((rows * cols, ngate), BF),
                in_vmem((size_z, width), F32),
                in_vmem((size_z, width), F32),
            ),
            in_specs=[spec_s()] + [spec_v()] * (len(args) - 1),
            out_specs=(spec_v(),) * 5,
            scratch_shapes=[
                pltpu.VMEM((size_z + 2 * pitch, ngate), BF),
                pltpu.VMEM((size_z + 16, 6 * width), F32),
            ],
            compiler_params=params,
            cost_estimate=pl.CostEstimate(
                flops=2 * size_z * 18 * width * ngate, bytes_accessed=10 << 20, transcendentals=0
            ),
        )(*args)
        sent_dx.append(dxi)
        kept.append(dgi)
        if step < steps - 1:
            pairs = [
                (i, i - 1)
                for i in range(1, layers)
                if 0 <= frames - 1 - step + layers - 1 - i < frames
            ]
            state = [lax.ppermute(dx, "section", pairs), dh_rec, dc_rec]

    first = layers - 1 - layer
    late = lax.dynamic_slice_in_dim(jnp.stack(kept), first, frames, 0)
    flat_dgates = late.reshape(frames * rows * cols, ngate)
    all_patches = jnp.concatenate([patches[f] for f in reversed(range(frames))], 0)
    partial = lax.dot_general(
        all_patches, flat_dgates, (((0,), (0,)), ((), ())), preferred_element_type=F32
    ).astype(BF)
    arrived = lax.all_to_all(partial, "tile", 0, 0, tiled=True)
    cots = lax.dynamic_slice_in_dim(jnp.stack(sent_dx), first, frames, 0)
    input_cot = jnp.flip(cots, 0).reshape(frames, rows, cols, width)
    grad_rows = jnp.sum(arrived.reshape(ntile, -1, ngate).astype(F32), 0)
    new_moment1 = 0.9 * moment1[0] + 0.1 * grad_rows
    new_moment2 = 0.999 * moment2[0] + 0.001 * grad_rows * grad_rows
    fix1 = 1.0 - 0.9**10
    fix2 = 1.0 - 0.999**10
    step_size = new_moment1 / fix1 / (jnp.sqrt(new_moment2 / fix2) + 1e-08)
    new_master = master[0] - 0.001 * step_size - 0.0001 * master[0]
    return (input_cot[None, :, None], new_master[None], new_moment1[None], new_moment2[None])


def solution(mesh):
    return jax.shard_map(
        on_device,
        mesh=mesh,
        in_specs=(
            P("section", None, "tile", None, None, None),
            P("section", None, "tile", None, None, None),
            P("section", None, "tile", None, None, None),
            P(None, "tile", None, None, None),
            P("section", None),
            P("section", "tile", None),
            P("section", "tile", None),
            P("section", "tile", None),
        ),
        out_specs=(
            P("section", None, "tile", None, None, None),
            P("section", "tile", None),
            P("section", "tile", None),
            P("section", "tile", None),
        ),
        check_vma=False,
    )
```

```python
import functools

import jax
import jax.numpy as jnp
from jax import lax
from jax.experimental import pallas as pl
from jax.experimental.pallas import tpu as pltpu
from jax.sharding import PartitionSpec as P

TILE_ROWS = 4
BF = jnp.bfloat16
F32 = jnp.float32
SIDE = 8
LEAD = 16


def params(mib):
    return pltpu.CompilerParams(vmem_limit_bytes=mib << 20)


def chunks(size, most):
    units = size // 16
    count = -(-units * 16 // most)
    out, at = [], 0
    for i in range(count):
        end = units * (i + 1) // count
        out.append((at * 16, (end - at) * 16))
        at = end
    return out


def in_vmem(shape, dtype):
    return pltpu.VMEM(shape, dtype)


def sigmoid(x):
    return 0.5 * jnp.tanh(0.5 * x) + 0.5


def gates_kernel(pitch, cells, width, zs_ref, ext_ref, mask_ref, kernel_ref, bias_ref, fac_ref):
    depth = 6 * width
    for start, size in chunks(cells, 480):
        total = bias_ref[...]
        for a in range(3):
            total = total + jnp.dot(
                zs_ref[pl.ds(start + a * pitch, size), :],
                kernel_ref[a * depth : (a + 1) * depth, :],
                preferred_element_type=F32,
            )
        here = pl.ds(start, size)
        mask = mask_ref[here, :].astype(F32)
        c_prev = ext_ref[pl.ds(start + pitch, size), 2 * width : 3 * width].astype(F32)
        i = sigmoid(total[:, :width])
        f = sigmoid(total[:, width : 2 * width])
        g = jnp.tanh(total[:, 2 * width : 3 * width])
        o = sigmoid(total[:, 3 * width :])
        tc = jnp.tanh(f * c_prev + i * g)
        fac_ref[here, 0:width] = o * (1.0 - tc * tc)
        fac_ref[here, width : 2 * width] = mask * g * i * (1.0 - i)
        fac_ref[here, 2 * width : 3 * width] = mask * c_prev * f * (1.0 - f)
        fac_ref[here, 3 * width : 4 * width] = mask * i * (1.0 - g * g)
        fac_ref[here, 4 * width : 5 * width] = mask * tc * o * (1.0 - o)
        fac_ref[here, 5 * width : 6 * width] = f


def step_kernel(step, layers, frames, pitch, rows, cols, width, *refs):
    ids_ref, kernel_t_ref = refs[0], refs[1]
    picks = picks_of(step, layers, frames)
    fac_refs = refs[2 : 2 + len(picks)]
    at = 2 + len(picks)
    first, tops = step == 0, step < frames
    ext_ref = refs[at] if tops else None
    at += 1 if tops else 0
    if not first:
        inc_ref, dh_ref, dc_ref = refs[at : at + 3]
        at += 5
    dx_ref, dxi_ref, dgi_ref, dhn_ref, dcn_ref, d_ref, p_ref = refs[at:]
    margin = frames + layers - 1 - step
    size_d = LEAD + (rows + 2 * margin) * pitch
    size_z = LEAD + (rows + 2 * margin - 2) * pitch
    frame = ids_ref[0] - step
    ngate = 4 * width

    def point(fac_ref, top_frame, pick):
        start_frame = pick == frames - 1
        for start, size in chunks(size_d, 256):
            here = pl.ds(start, size)
            there = pl.ds(start + step * pitch, size)
            if tops and pick == top_frame:
                above = ext_ref[pl.ds(start + (step + 1) * pitch, size), 3 * width :].astype(F32)
            else:
                above = inc_ref[here, :].astype(F32)
            dh = above
            if not start_frame:
                dh = dh + dh_ref[here, :]
            dc = dh * fac_ref[there, 0:width]
            if not start_frame:
                dc = dc + dc_ref[here, :]
            d_ref[here, 0:width] = (dc * fac_ref[there, width : 2 * width]).astype(BF)
            d_ref[here, width : 2 * width] = (dc * fac_ref[there, 2 * width : 3 * width]).astype(BF)
            d_ref[here, 2 * width : 3 * width] = (dc * fac_ref[there, 3 * width : 4 * width]).astype(BF)
            d_ref[here, 3 * width :] = (dh * fac_ref[there, 4 * width : 5 * width]).astype(BF)
            lo, hi = max(start, pitch), min(start + size, pitch + size_z)
            if hi > lo:
                rec = dc * fac_ref[there, 5 * width :]
                dcn_ref[lo - pitch : hi - pitch, :] = rec[lo - start : hi - start, :]

    top_frame = frames - 1 - step
    for number, pick in enumerate(picks):
        pl.when(frame == pick)(functools.partial(point, fac_refs[number], top_frame, pick))

    @pl.when((frame >= 0) & (frame < frames))
    def _():
        slot = pl.multiple_of(frame * (rows * cols), rows * cols)
        for row in range(rows):
            dgi_ref[pl.ds(slot + row * cols, cols), :] = d_ref[
                pl.ds(LEAD + (row + margin) * pitch, cols), :
            ]
        p_ref[0:8, :] = jnp.zeros((8, 6 * width), F32)
        p_ref[8 + size_z : 16 + size_z, :] = jnp.zeros((8, 6 * width), F32)
        for start, size in chunks(size_z, 448):
            total = None
            for a in range(3):
                part = jnp.dot(
                    d_ref[pl.ds(start + (2 - a) * pitch, size), :],
                    kernel_t_ref[a * ngate : (a + 1) * ngate, :],
                    preferred_element_type=F32,
                )
                total = part if total is None else total + part
            p_ref[pl.ds(8 + start, size), :] = total
        for start, size in chunks(size_z, 256):
            dz = (
                p_ref[pl.ds(8 + start, size), 2 * width : 4 * width]
                + p_ref[pl.ds(9 + start, size), 0 : 2 * width]
                + p_ref[pl.ds(7 + start, size), 4 * width :]
            )
            dx_ref[pl.ds(start, size), :] = dz[:, :width].astype(BF)
            dhn_ref[pl.ds(start, size), :] = dz[:, width:]
        for row in range(rows):
            dxi_ref[pl.ds(slot + row * cols, cols), :] = dx_ref[
                pl.ds(LEAD + (row + margin - 1) * pitch, cols), :
            ]


def picks_of(step, layers, frames):
    return [f for f in range(frames) if 0 <= frames - 1 - step + layers - 1 - f <= layers - 1]


def patch_kernel(pitch, rows, cols, edge, zs_ref, pt_ref, flat_ref):
    depth = zs_ref.shape[1]
    for a in range(3):
        for row in range(rows):
            flat_ref[row * cols : (row + 1) * cols, :] = zs_ref[
                pl.ds(LEAD + (edge + row + a) * pitch, cols), :
            ]
        pt_ref[a * depth : (a + 1) * depth, :] = flat_ref[...].T


def grad_kernel(cells, frame, count, begin, end, *refs):
    pts, dg_ref = refs[:count], refs[count]
    total_ref = None if begin else refs[count + 1]
    out_ref = refs[-1]
    block = 256
    for at in range(0, out_ref.shape[0], block):
        here = pl.ds(at, block)
        total = None if begin else total_ref[here, :]
        part = jnp.dot(
            pts[0][here, :], dg_ref[frame * cells : (frame + 1) * cells, :], preferred_element_type=F32
        )
        total = part if begin else total + part
        out_ref[here, :] = total.astype(out_ref.dtype)


def spec_v():
    return pl.BlockSpec(memory_space=pltpu.VMEM)


def spec_s():
    return pl.BlockSpec(memory_space=pltpu.SMEM)


def on_device(layer_input, hidden_prev, cell_prev, out_cot, bias, master, moment1, moment2):
    frames, rows, cols, width = (layer_input.shape[i] for i in (1, 3, 4, 5))
    ngate = 4 * width
    layers = lax.axis_size("section")
    layer = lax.axis_index("section")
    ntile = lax.axis_size("tile")
    tile = lax.axis_index("tile")
    ncols = ntile // TILE_ROWS
    pitch = cols + 2 * SIDE
    edge = frames + layers - 1

    own_rows = master[0].astype(BF)
    kernel = lax.all_to_all(jnp.tile(own_rows, (ntile, 1)), "tile", 0, 0, tiled=True)
    kernel_t = kernel.reshape(3, 6 * width, ngate).transpose(0, 2, 1).reshape(3 * ngate, 6 * width)

    packed = jnp.concatenate(
        [layer_input[0, :, 0], hidden_prev[0, :, 0], cell_prev[0, :, 0].astype(BF), out_cot[:, 0]], -1
    )
    deeps = [edge + 1 - (frames - 1 - f) for f in range(frames)]
    grid_row, grid_col = tile // ncols, tile % ncols

    def around(by, strip, keep):
        got = lax.ppermute(strip, "tile", [(i, by(i)) for i in range(ntile)])
        return jnp.where(keep, got, jnp.zeros_like(got))

    downs = jnp.concatenate([packed[f, rows - deeps[f] :] for f in range(frames)], 0)
    ups = jnp.concatenate([packed[f, : deeps[f]] for f in range(frames)], 0)
    above = around(lambda i: (i + ncols) % ntile, downs, grid_row > 0)
    below = around(lambda i: (i - ncols) % ntile, ups, grid_row < TILE_ROWS - 1)
    talls, at = [], 0
    for f in range(frames):
        talls.append(jnp.concatenate([above[at : at + deeps[f]], packed[f], below[at : at + deeps[f]]], 0))
        at += deeps[f]
    rights = jnp.concatenate([t[:, cols - SIDE :] for t in talls], 0)
    lefts = jnp.concatenate([t[:, :SIDE] for t in talls], 0)
    left = around(lambda i: i // ncols * ncols + (i + 1) % ncols, rights, grid_col > 0)
    right = around(lambda i: i // ncols * ncols + (i - 1) % ncols, lefts, grid_col < ncols - 1)
    ext, at = [], 0
    for f in range(frames):
        tall = rows + 2 * deeps[f]
        wide = jnp.concatenate([left[at : at + tall], talls[f], right[at : at + tall]], 1)
        at += tall
        gap = edge + 1 - deeps[f]
        ext.append(
            jnp.pad(
                wide.reshape(-1, 4 * width), ((LEAD - SIDE + gap * pitch, SIDE + gap * pitch), (0, 0))
            )
        )
    size_e = LEAD + (rows + 2 * edge + 2) * pitch
    size_d = LEAD + (rows + 2 * edge) * pitch
    cells = rows * cols

    at = jnp.arange(size_d, dtype=jnp.int32) - LEAD + SIDE
    row_at = at // pitch - edge + grid_row * rows
    col_at = at % pitch - SIDE + grid_col * cols
    inside = (row_at >= 0) & (row_at < TILE_ROWS * rows) & (col_at >= 0) & (col_at < ncols * cols)
    mask = jnp.broadcast_to(inside[:, None], (size_d, width)).astype(BF)

    facs, pts = [None] * frames, [None] * frames
    for f in reversed(range(frames)):
        z = ext[f][:, : 2 * width]
        none = jnp.zeros((1, 2 * width), BF)
        zs = jnp.concatenate(
            [jnp.concatenate([none, z[:-1]], 0), z, jnp.concatenate([z[1:], none], 0)], -1
        )
        pts[f] = pl.pallas_call(
            functools.partial(patch_kernel, pitch, rows, cols, edge),
            out_shape=in_vmem((18 * width, cells), BF),
            in_specs=[spec_v()],
            out_specs=spec_v(),
            scratch_shapes=[pltpu.VMEM((cells, 6 * width), BF)],
            compiler_params=params(16),
            cost_estimate=pl.CostEstimate(flops=0, bytes_accessed=8 << 20, transcendentals=0),
        )(zs)
        facs[f] = pl.pallas_call(
            functools.partial(gates_kernel, pitch, size_d, width),
            out_shape=in_vmem((size_d, 6 * width), F32),
            in_specs=[spec_v()] * 5,
            out_specs=spec_v(),
            compiler_params=params(16),
            cost_estimate=pl.CostEstimate(
                flops=2 * size_d * 18 * width * ngate, bytes_accessed=10 << 20, transcendentals=size_d * 5 * width
            ),
        )(zs, ext[f], mask, kernel, bias)

    ids = (frames - 1 + layers - 1 - layer).astype(jnp.int32).reshape(1)
    state = []
    steps = layers + frames - 1
    total = None
    for step in range(steps):
        margin = edge - step
        size_z = LEAD + (rows + 2 * margin - 2) * pitch
        args = [ids, kernel_t] + [facs[f] for f in picks_of(step, layers, frames)]
        if step < frames:
            args.append(ext[frames - 1 - step])
        args += state
        dx, cots, dgates, dh_rec, dc_rec = pl.pallas_call(
            functools.partial(step_kernel, step, layers, frames, pitch, rows, cols, width),
            out_shape=(
                jax.ShapeDtypeStruct((size_z, width), BF),
                in_vmem((frames * cells, width), BF),
                in_vmem((frames * cells, ngate), BF),
                in_vmem((size_z, width), F32),
                in_vmem((size_z, width), F32),
            ),
            in_specs=[spec_s()] + [spec_v()] * (len(args) - 1),
            out_specs=(spec_v(),) * 5,
            scratch_shapes=[
                pltpu.VMEM((size_z + 2 * pitch, ngate), BF),
                pltpu.VMEM((size_z + 16, 6 * width), F32),
            ],
            input_output_aliases={len(args) - 2: 1, len(args) - 1: 2} if step else {},
            compiler_params=params(20),
            cost_estimate=pl.CostEstimate(
                flops=2 * size_z * 18 * width * ngate, bytes_accessed=10 << 20, transcendentals=0
            ),
        )(*args)
        if step < steps - 1:
            pairs = [
                (i, i - 1)
                for i in range(1, layers)
                if 0 <= frames - 1 - step + layers - 1 - i < frames
            ]
            state = [lax.ppermute(dx, "section", pairs), dh_rec, dc_rec, cots, dgates]
        if step >= layers - 1:
            f = frames - 1 - (step - layers + 1)
            end = step == steps - 1
            args = [pts[f], dgates] + ([] if total is None else [total])
            total = pl.pallas_call(
                functools.partial(grad_kernel, cells, f, 1, total is None, end),
                out_shape=jax.ShapeDtypeStruct((18 * width, ngate), BF) if end else in_vmem((18 * width, ngate), F32),
                in_specs=[spec_v()] * len(args),
                out_specs=spec_v(),
                compiler_params=params(16),
                cost_estimate=pl.CostEstimate(
                    flops=2 * cells * 18 * width * ngate, bytes_accessed=4 << 20, transcendentals=0
                ),
            )(*args)

    total, cots = lax.optimization_barrier((total, cots))
    arrived = lax.all_to_all(total, "tile", 0, 0, tiled=True)
    arrived, cots = lax.optimization_barrier((arrived, cots))
    input_cot = cots.reshape(frames, rows, cols, width)
    grad_rows = jnp.sum(arrived.reshape(ntile, -1, ngate).astype(F32), 0)
    new_moment1 = 0.9 * moment1[0] + 0.1 * grad_rows
    new_moment2 = 0.999 * moment2[0] + 0.001 * grad_rows * grad_rows
    fix1 = 1.0 - 0.9**10
    fix2 = 1.0 - 0.999**10
    step_size = new_moment1 / fix1 / (jnp.sqrt(new_moment2 / fix2) + 1e-08)
    new_master = master[0] - 0.001 * step_size - 0.0001 * master[0]
    return (input_cot[None, :, None], new_master[None], new_moment1[None], new_moment2[None])


def solution(mesh):
    return jax.shard_map(
        on_device,
        mesh=mesh,
        in_specs=(
            P("section", None, "tile", None, None, None),
            P("section", None, "tile", None, None, None),
            P("section", None, "tile", None, None, None),
            P(None, "tile", None, None, None),
            P("section", None),
            P("section", "tile", None),
            P("section", "tile", None),
            P("section", "tile", None),
        ),
        out_specs=(
            P("section", None, "tile", None, None, None),
            P("section", "tile", None),
            P("section", "tile", None),
            P("section", "tile", None),
        ),
        check_vma=False,
    )
```

```python
import functools

import jax
import jax.numpy as jnp
from jax import lax
from jax.experimental import pallas as pl
from jax.experimental.pallas import tpu as pltpu
from jax.sharding import PartitionSpec as P

TILE_ROWS = 4
BF = jnp.bfloat16
F32 = jnp.float32
SIDE = 8
LEAD = 16


def params(mib):
    return pltpu.CompilerParams(vmem_limit_bytes=mib << 20)


def chunks(size, most):
    units = size // 16
    count = -(-units * 16 // most)
    out, at = [], 0
    for i in range(count):
        end = units * (i + 1) // count
        out.append((at * 16, (end - at) * 16))
        at = end
    return out


def in_vmem(shape, dtype):
    return pltpu.VMEM(shape, dtype)


def sigmoid(x):
    return 0.5 * jnp.tanh(0.5 * x) + 0.5


def gates_kernel(pitch, width, deep, gap, at_row, at_side, ids_ref, mid_ref, above_ref, below_ref, side_ref, mask_ref, kernel_ref, bias_ref, fac_ref, zs_ref, own_ref, flat_ref, z_ref):
    depth = 6 * width
    rows = mid_ref.shape[0]
    cols = pitch - 2 * SIDE
    tall = rows + 2 * deep
    size_e = zs_ref.shape[0]
    begin = gap * pitch
    stop = begin + LEAD + tall * pitch
    if gap:
        for lo, hi in ((0, begin), (stop, size_e)):
            z_ref[8 + lo : 8 + hi, :] = jnp.zeros((hi - lo, 2 * width), F32)
            flat_ref[lo:hi, :] = jnp.zeros((hi - lo, 2 * width), BF)
    z_ref[0:8, :] = jnp.zeros((8, 2 * width), F32)
    z_ref[8 + size_e :, :] = jnp.zeros((8, 2 * width), F32)

    def put(at, value):
        size = value.shape[0]
        z_ref[8 + at : 8 + at + size, :] = value[:, : 2 * width].astype(F32)
        flat_ref[at : at + size, :] = value[:, 2 * width :]

    for row in range(tall + 1):
        put(begin + row * pitch, side_ref[at_side + row])
    for row in range(tall):
        at = begin + LEAD + row * pitch
        if row < deep:
            put(at, above_ref[at_row + row])
        elif row < deep + rows:
            put(at, mid_ref[row - deep])
        else:
            put(at, below_ref[at_row + row - deep - rows])
    for start, size in chunks(size_e, 256):
        here = pl.ds(start, size)
        own_ref[here, :] = flat_ref[here, width:]
        for b in range(3):
            zs_ref[here, b * 2 * width : (b + 1) * 2 * width] = z_ref[
                7 + b + start : 7 + b + start + size, :
            ].astype(BF)
    cells = fac_ref.shape[0] - 2 * begin
    for start, size in chunks(cells, 480):
        start = start + begin
        total = bias_ref[...]
        for a in range(3):
            total = total + jnp.dot(
                zs_ref[pl.ds(start + a * pitch, size), :],
                kernel_ref[a * depth : (a + 1) * depth, :],
                preferred_element_type=F32,
            )
        here = pl.ds(start, size)
        mask = mask_ref[here, :].astype(F32)
        c_prev = flat_ref[pl.ds(start + pitch, size), :width].astype(F32)
        i = sigmoid(total[:, :width])
        f = sigmoid(total[:, width : 2 * width])
        g = jnp.tanh(total[:, 2 * width : 3 * width])
        o = sigmoid(total[:, 3 * width :])
        tc = jnp.tanh(f * c_prev + i * g)
        fac_ref[here, 0:width] = o * (1.0 - tc * tc)
        fac_ref[here, width : 2 * width] = mask * g * i * (1.0 - i)
        fac_ref[here, 2 * width : 3 * width] = mask * c_prev * f * (1.0 - f)
        fac_ref[here, 3 * width : 4 * width] = mask * i * (1.0 - g * g)
        fac_ref[here, 4 * width : 5 * width] = mask * tc * o * (1.0 - o)
        fac_ref[here, 5 * width : 6 * width] = f


def turn_kernel(kernel_ref, turned_ref):
    depth, ngate = kernel_ref.shape[0] // 3, kernel_ref.shape[1]
    for a in range(3):
        turned_ref[a * ngate : (a + 1) * ngate, :] = kernel_ref[a * depth : (a + 1) * depth, :].T


def step_kernel(step, group, layers, frames, pitch, rows, cols, width, *refs):
    ids_ref, kernel_t_ref = refs[0], refs[1]
    picks = picks_of(step, group, layers, frames)
    fac_refs = refs[2 : 2 + len(picks)]
    at = 2 + len(picks)
    tops = layers - 1 in group and step < frames
    own_ref = refs[at] if tops else None
    at += 1 if tops else 0
    has_inc, has_state, has_kept = needs_of(step, group, layers, frames)
    inc_refs = {}
    for f in picks:
        if frames - 1 - step + layers - f < layers:
            inc_refs[f] = refs[at]
            at += 1
    if has_state:
        dh_ref, dc_ref = refs[at : at + 2]
        at += 2
    if has_kept:
        at += 2
    dx_ref, dxi_ref, dgi_ref, dhn_ref, dcn_ref, d_ref, p_ref = refs[at:]
    margin = frames + layers - 1 - step
    size_d = LEAD + (rows + 2 * margin) * pitch
    size_z = LEAD + (rows + 2 * margin - 2) * pitch
    frame = ids_ref[0] - step
    ngate = 4 * width

    def point(fac_ref, top_frame, pick):
        start_frame = pick == frames - 1
        for start, size in chunks(size_d, 256):
            here = pl.ds(start, size)
            there = pl.ds(start + step * pitch, size)
            if tops and pick == top_frame:
                above = own_ref[pl.ds(start + (step + 1) * pitch, size), :].astype(F32)
            else:
                above = inc_refs[pick][here, :].astype(F32)
            dh = above
            if not start_frame:
                dh = dh + dh_ref[here, :]
            dc = dh * fac_ref[there, 0:width]
            if not start_frame:
                dc = dc + dc_ref[here, :]
            d_ref[here, 0:width] = (dc * fac_ref[there, width : 2 * width]).astype(BF)
            d_ref[here, width : 2 * width] = (dc * fac_ref[there, 2 * width : 3 * width]).astype(BF)
            d_ref[here, 2 * width : 3 * width] = (dc * fac_ref[there, 3 * width : 4 * width]).astype(BF)
            d_ref[here, 3 * width :] = (dh * fac_ref[there, 4 * width : 5 * width]).astype(BF)
            lo, hi = max(start, pitch), min(start + size, pitch + size_z)
            if hi > lo:
                rec = dc * fac_ref[there, 5 * width :]
                dcn_ref[lo - pitch : hi - pitch, :] = rec[lo - start : hi - start, :]

    top_frame = frames - 1 - step
    for number, pick in enumerate(picks):
        pl.when(frame == pick)(functools.partial(point, fac_refs[number], top_frame, pick))

    active = (frame >= picks[0]) & (frame <= picks[-1])

    @pl.when(active)
    def _():
        slot = pl.multiple_of(frame * (rows * cols), rows * cols)
        for row in range(rows):
            dgi_ref[pl.ds(slot + row * cols, cols), :] = d_ref[
                pl.ds(LEAD + (row + margin) * pitch, cols), :
            ]
        p_ref[0:8, :] = jnp.zeros((8, 6 * width), F32)
        p_ref[8 + size_z : 16 + size_z, :] = jnp.zeros((8, 6 * width), F32)
        for start, size in chunks(size_z, 448):
            total = None
            for a in range(3):
                part = jnp.dot(
                    d_ref[pl.ds(start + (2 - a) * pitch, size), :],
                    kernel_t_ref[a * ngate : (a + 1) * ngate, :],
                    preferred_element_type=F32,
                )
                total = part if total is None else total + part
            p_ref[pl.ds(8 + start, size), :] = total
        for start, size in chunks(size_z, 256):
            dz = (
                p_ref[pl.ds(8 + start, size), 2 * width : 4 * width]
                + p_ref[pl.ds(9 + start, size), 0 : 2 * width]
                + p_ref[pl.ds(7 + start, size), 4 * width :]
            )
            dx_ref[pl.ds(start, size), :] = dz[:, :width].astype(BF)
            dhn_ref[pl.ds(start, size), :] = dz[:, width:]
        for row in range(rows):
            dxi_ref[pl.ds(slot + row * cols, cols), :] = dx_ref[
                pl.ds(LEAD + (row + margin - 1) * pitch, cols), :
            ]


def picks_of(step, group, layers, frames):
    now = [frames - 1 - step + layers - 1 - layer for layer in group]
    return sorted(f for f in now if 0 <= f < frames)


def needs_of(step, group, layers, frames):
    has_inc = any(
        0 <= frames - 1 - step + layers - 1 - layer < frames for layer in group if layer < layers - 1
    )
    has_state = any(f < frames - 1 for f in picks_of(step, group, layers, frames))
    return has_inc, has_state, step > 0


def patch_kernel(pitch, rows, cols, edge, zs_ref, pt_ref, flat_ref):
    depth = zs_ref.shape[1]
    for a in range(3):
        for row in range(rows):
            flat_ref[row * cols : (row + 1) * cols, :] = zs_ref[
                pl.ds(LEAD + (edge + row + a) * pitch, cols), :
            ]
        pt_ref[a * depth : (a + 1) * depth, :] = flat_ref[...].T


def grad_kernel(cells, frame, count, begin, end, *refs):
    pts, dg_ref = refs[:count], refs[count]
    total_ref = None if begin else refs[count + 1]
    out_ref = refs[-1]
    block = 256
    for at in range(0, out_ref.shape[0], block):
        here = pl.ds(at, block)
        total = None if begin else total_ref[here, :]
        part = jnp.dot(
            pts[0][here, :], dg_ref[frame * cells : (frame + 1) * cells, :], preferred_element_type=F32
        )
        total = part if begin else total + part
        out_ref[here, :] = total.astype(out_ref.dtype)


def spec_v():
    return pl.BlockSpec(memory_space=pltpu.VMEM)


def spec_s():
    return pl.BlockSpec(memory_space=pltpu.SMEM)


def on_device(layer_input, hidden_prev, cell_prev, out_cot, bias, master, moment1, moment2):
    frames, rows, cols, width = (layer_input.shape[i] for i in (1, 3, 4, 5))
    ngate = 4 * width
    layers = lax.axis_size("section")
    layer = lax.axis_index("section")
    ntile = lax.axis_size("tile")
    tile = lax.axis_index("tile")
    ncols = ntile // TILE_ROWS
    pitch = cols + 2 * SIDE
    edge = frames + layers - 1

    own_rows = master[0].astype(BF)
    kernel = lax.all_to_all(jnp.tile(own_rows, (ntile, 1)), "tile", 0, 0, tiled=True)

    ids = (frames - 1 + layers - 1 - layer).astype(jnp.int32).reshape(1)
    packed = jnp.concatenate(
        [layer_input[0, :, 0], hidden_prev[0, :, 0], cell_prev[0, :, 0].astype(BF), out_cot[:, 0]], -1
    )
    deeps = [edge + 1 - (frames - 1 - f) for f in range(frames)]
    grid_row, grid_col = tile // ncols, tile % ncols

    def around(by, strip, keep):
        got = lax.ppermute(strip, "tile", [(i, by(i)) for i in range(ntile)])
        return jnp.where(keep, got, jnp.zeros_like(got))

    downs = jnp.concatenate([packed[f, rows - deeps[f] :] for f in range(frames)], 0)
    ups = jnp.concatenate([packed[f, : deeps[f]] for f in range(frames)], 0)
    above = around(lambda i: (i + ncols) % ntile, downs, grid_row > 0)
    below = around(lambda i: (i - ncols) % ntile, ups, grid_row < TILE_ROWS - 1)
    talls, at = [], 0
    for f in range(frames):
        talls.append(jnp.concatenate([above[at : at + deeps[f]], packed[f], below[at : at + deeps[f]]], 0))
        at += deeps[f]
    deepest = max(deeps)
    rights = jnp.concatenate([t[:, cols - d :].reshape(-1, 4 * width) for t, d in zip(talls, deeps)], 0)
    lefts = jnp.concatenate([t[:, :d].reshape(-1, 4 * width) for t, d in zip(talls, deeps)], 0)
    left = around(lambda i: i // ncols * ncols + (i + 1) % ncols, rights, grid_col > 0)
    right = around(lambda i: i // ncols * ncols + (i - 1) % ncols, lefts, grid_col < ncols - 1)
    sides, at = [], 0
    for f, d in enumerate(deeps):
        tall = rows + 2 * d
        right_f = right[at : at + tall * d].reshape(tall, d, 4 * width)
        left_f = left[at : at + tall * d].reshape(tall, d, 4 * width)
        at += tall * d
        sides.append(
            jnp.concatenate(
                [
                    jnp.pad(right_f, ((1, 0), (0, SIDE - d), (0, 0))),
                    jnp.pad(left_f, ((0, 1), (SIDE - d, 0), (0, 0))),
                ],
                1,
            )
        )
    side = jnp.concatenate(sides, 0)
    size_e = LEAD + (rows + 2 * edge + 2) * pitch
    size_d = LEAD + (rows + 2 * edge) * pitch
    cells = rows * cols

    at = jnp.arange(size_d, dtype=jnp.int32) - LEAD + SIDE
    row_at = at // pitch - edge + grid_row * rows
    col_at = at % pitch - SIDE + grid_col * cols
    inside = (row_at >= 0) & (row_at < TILE_ROWS * rows) & (col_at >= 0) & (col_at < ncols * cols)
    mask = jnp.broadcast_to(inside[:, None], (size_d, width)).astype(BF)

    facs, pts, owns = [None] * frames, [None] * frames, [None] * frames
    for f in reversed(range(frames)):
        gap = edge + 1 - deeps[f]
        facs[f], zs, owns[f] = pl.pallas_call(
            functools.partial(
                gates_kernel, pitch, width, deeps[f], gap, sum(deeps[:f]),
                sum(rows + 2 * d + 1 for d in deeps[:f]),
            ),
            out_shape=(
                in_vmem((size_d, 6 * width), F32),
                in_vmem((size_e, 6 * width), BF),
                in_vmem((size_e, width), BF),
            ),
            in_specs=[spec_s()] + [spec_v()] * 7,
            out_specs=(spec_v(),) * 3,
            scratch_shapes=[pltpu.VMEM((size_e, 2 * width), BF), pltpu.VMEM((size_e + 16, 2 * width), F32)],
            compiler_params=params(20),
            cost_estimate=pl.CostEstimate(
                flops=2 * size_d * 18 * width * ngate, bytes_accessed=10 << 20, transcendentals=size_d * 5 * width
            ),
        )(ids, packed[f], above, below, side, mask, kernel, bias)
        pts[f] = pl.pallas_call(
            functools.partial(patch_kernel, pitch, rows, cols, edge),
            out_shape=in_vmem((18 * width, cells), BF),
            in_specs=[spec_v()],
            out_specs=spec_v(),
            scratch_shapes=[pltpu.VMEM((cells, 6 * width), BF)],
            compiler_params=params(16),
            cost_estimate=pl.CostEstimate(flops=0, bytes_accessed=8 << 20, transcendentals=0),
        )(zs)
    kernel_t = pl.pallas_call(
        turn_kernel,
        out_shape=in_vmem((3 * ngate, 6 * width), BF),
        in_specs=[spec_v()],
        out_specs=spec_v(),
        compiler_params=params(16),
        cost_estimate=pl.CostEstimate(flops=0, bytes_accessed=4 << 20, transcendentals=0),
    )(kernel)

    steps = layers + frames - 1
    upper, lower = tuple(range(layers // 2, layers)), tuple(range(layers // 2))
    states = {upper: None, lower: None}
    sent = {}
    kept = None
    total = None
    for step in range(steps):
        margin = edge - step
        size_z = LEAD + (rows + 2 * margin - 2) * pitch
        fresh = {}
        for group in (upper, lower):
            picks = picks_of(step, group, layers, frames)
            if not picks:
                continue
            has_inc, has_state, has_kept = needs_of(step, group, layers, frames)
            args = [ids, kernel_t] + [facs[f] for f in picks]
            if layers - 1 in group and step < frames:
                args.append(owns[frames - 1 - step])
            if has_inc:
                above_of = [frames - 1 - step + layers - f for f in picks]
                args += [sent[i] for i in above_of if i < layers]
            if has_state:
                args += list(states[group])
            if has_kept:
                args += list(kept)
            dx, cots, dgates, dh_rec, dc_rec = pl.pallas_call(
                functools.partial(step_kernel, step, group, layers, frames, pitch, rows, cols, width),
                out_shape=(
                    jax.ShapeDtypeStruct((size_z, width), BF),
                    in_vmem((frames * cells, width), BF),
                    in_vmem((frames * cells, ngate), BF),
                    in_vmem((size_z, width), F32),
                    in_vmem((size_z, width), F32),
                ),
                in_specs=[spec_s()] + [spec_v()] * (len(args) - 1),
                out_specs=(spec_v(),) * 5,
                scratch_shapes=[
                    pltpu.VMEM((size_z + 2 * pitch, ngate), BF),
                    pltpu.VMEM((size_z + 16, 6 * width), F32),
                ],
                input_output_aliases={len(args) - 2: 1, len(args) - 1: 2} if has_kept else {},
                compiler_params=params(20),
                cost_estimate=pl.CostEstimate(
                    flops=2 * size_z * 18 * width * ngate, bytes_accessed=10 << 20, transcendentals=0
                ),
            )(*args)
            kept = (cots, dgates)
            states[group] = (dh_rec, dc_rec)
            for i in group:
                if i > 0 and 0 <= frames - 1 - step + layers - 1 - i < frames:
                    fresh[i] = lax.ppermute(dx, "section", [(i, i - 1)])
        sent = fresh
        if step >= layers - 1:
            f = frames - 1 - (step - layers + 1)
            end = step == steps - 1
            args = [pts[f], kept[1]] + ([] if total is None else [total])
            total = pl.pallas_call(
                functools.partial(grad_kernel, cells, f, 1, total is None, end),
                out_shape=in_vmem((18 * width, ngate), BF if end else F32),
                in_specs=[spec_v()] * len(args),
                out_specs=spec_v(),
                compiler_params=params(16),
                cost_estimate=pl.CostEstimate(
                    flops=2 * cells * 18 * width * ngate, bytes_accessed=4 << 20, transcendentals=0
                ),
            )(*args)
    cots = kept[0]
    total, cots = lax.optimization_barrier((total, cots))
    arrived = lax.all_to_all(total, "tile", 0, 0, tiled=True)
    arrived, cots = lax.optimization_barrier((arrived, cots))
    input_cot = cots.reshape(frames, rows, cols, width)
    grad_rows = jnp.sum(arrived.reshape(ntile, -1, ngate).astype(F32), 0)
    new_moment1 = 0.9 * moment1[0] + 0.1 * grad_rows
    new_moment2 = 0.999 * moment2[0] + 0.001 * grad_rows * grad_rows
    fix1 = 1.0 - 0.9**10
    fix2 = 1.0 - 0.999**10
    step_size = new_moment1 / fix1 / (jnp.sqrt(new_moment2 / fix2) + 1e-08)
    new_master = master[0] - 0.001 * step_size - 0.0001 * master[0]
    return (input_cot[None, :, None], new_master[None], new_moment1[None], new_moment2[None])


def solution(mesh):
    return jax.shard_map(
        on_device,
        mesh=mesh,
        in_specs=(
            P("section", None, "tile", None, None, None),
            P("section", None, "tile", None, None, None),
            P("section", None, "tile", None, None, None),
            P(None, "tile", None, None, None),
            P("section", None),
            P("section", "tile", None),
            P("section", "tile", None),
            P("section", "tile", None),
        ),
        out_specs=(
            P("section", None, "tile", None, None, None),
            P("section", "tile", None),
            P("section", "tile", None),
            P("section", "tile", None),
        ),
        check_vma=False,
    )
```

```python
import functools

import jax
import jax.numpy as jnp
from jax import lax
from jax.experimental import pallas as pl
from jax.experimental.pallas import tpu as pltpu
from jax.sharding import PartitionSpec as P

TILE_ROWS = 4
BF = jnp.bfloat16
F32 = jnp.float32
SIDE = 8
LEAD = 16


def params(mib):
    return pltpu.CompilerParams(vmem_limit_bytes=mib << 20)


def chunks(size, most):
    units = size // 16
    count = -(-units * 16 // most)
    out, at = [], 0
    for i in range(count):
        end = units * (i + 1) // count
        out.append((at * 16, (end - at) * 16))
        at = end
    return out


def in_vmem(shape, dtype):
    return pltpu.VMEM(shape, dtype)


def sigmoid(x):
    return 0.5 * jnp.tanh(0.5 * x) + 0.5


def gates_kernel(pitch, width, deep, gap, at_row, at_side, ids_ref, mid_ref, above_ref, below_ref, left_ref, right_ref, mask_ref, kernel_ref, bias_ref, fac_ref, zs_ref, own_ref, flat_ref, z_ref):
    depth = 6 * width
    rows = mid_ref.shape[0]
    cols = pitch - 2 * SIDE
    tall = rows + 2 * deep
    size_e = zs_ref.shape[0]
    begin = gap * pitch
    stop = begin + LEAD + tall * pitch
    if gap:
        for lo, hi in ((0, begin), (stop, size_e)):
            z_ref[8 + lo : 8 + hi, :] = jnp.zeros((hi - lo, 2 * width), F32)
            flat_ref[lo:hi, :] = jnp.zeros((hi - lo, 2 * width), BF)
    z_ref[0:8, :] = jnp.zeros((8, 2 * width), F32)
    z_ref[8 + size_e :, :] = jnp.zeros((8, 2 * width), F32)

    def put(at, value):
        size = value.shape[0]
        z_ref[8 + at : 8 + at + size, :] = value[:, : 2 * width].astype(F32)
        flat_ref[at : at + size, :] = value[:, 2 * width :]

    none = jnp.zeros((SIDE, 4 * width), BF)
    for row in range(tall + 1):
        before = none if row == 0 else right_ref[at_side + row - 1]
        after = none if row == tall else left_ref[at_side + row]
        put(begin + row * pitch, jnp.concatenate([before, after], 0))
    for row in range(tall):
        at = begin + LEAD + row * pitch
        if row < deep:
            put(at, above_ref[at_row + row])
        elif row < deep + rows:
            put(at, mid_ref[row - deep])
        else:
            put(at, below_ref[at_row + row - deep - rows])
    for start, size in chunks(size_e, 256):
        here = pl.ds(start, size)
        own_ref[here, :] = flat_ref[here, width:]
        for b in range(3):
            zs_ref[here, b * 2 * width : (b + 1) * 2 * width] = z_ref[
                7 + b + start : 7 + b + start + size, :
            ].astype(BF)
    cells = fac_ref.shape[0] - 2 * begin
    for start, size in chunks(cells, 480):
        start = start + begin
        total = bias_ref[...]
        for a in range(3):
            total = total + jnp.dot(
                zs_ref[pl.ds(start + a * pitch, size), :],
                kernel_ref[a * depth : (a + 1) * depth, :],
                preferred_element_type=F32,
            )
        here = pl.ds(start, size)
        mask = mask_ref[here, :].astype(F32)
        c_prev = flat_ref[pl.ds(start + pitch, size), :width].astype(F32)
        i = sigmoid(total[:, :width])
        f = sigmoid(total[:, width : 2 * width])
        g = jnp.tanh(total[:, 2 * width : 3 * width])
        o = sigmoid(total[:, 3 * width :])
        tc = jnp.tanh(f * c_prev + i * g)
        fac_ref[here, 0:width] = o * (1.0 - tc * tc)
        fac_ref[here, width : 2 * width] = mask * g * i * (1.0 - i)
        fac_ref[here, 2 * width : 3 * width] = mask * c_prev * f * (1.0 - f)
        fac_ref[here, 3 * width : 4 * width] = mask * i * (1.0 - g * g)
        fac_ref[here, 4 * width : 5 * width] = mask * tc * o * (1.0 - o)
        fac_ref[here, 5 * width : 6 * width] = f


def turn_kernel(kernel_ref, turned_ref):
    depth, ngate = kernel_ref.shape[0] // 3, kernel_ref.shape[1]
    for a in range(3):
        turned_ref[a * ngate : (a + 1) * ngate, :] = kernel_ref[a * depth : (a + 1) * depth, :].T


def step_kernel(step, group, layers, frames, pitch, rows, cols, width, *refs):
    ids_ref, kernel_t_ref = refs[0], refs[1]
    picks = picks_of(step, group, layers, frames)
    fac_refs = refs[2 : 2 + len(picks)]
    at = 2 + len(picks)
    tops = layers - 1 in group and step < frames
    own_ref = refs[at] if tops else None
    at += 1 if tops else 0
    has_inc, has_state, has_kept = needs_of(step, group, layers, frames)
    inc_refs = {}
    for f in picks:
        if frames - 1 - step + layers - f < layers:
            inc_refs[f] = refs[at]
            at += 1
    if has_state:
        dh_ref, dc_ref = refs[at : at + 2]
        at += 2
    if has_kept:
        at += 2
    dx_ref, dxi_ref, dgi_ref, dhn_ref, dcn_ref, d_ref, p_ref = refs[at:]
    margin = frames + layers - 1 - step
    size_d = LEAD + (rows + 2 * margin) * pitch
    size_z = LEAD + (rows + 2 * margin - 2) * pitch
    frame = ids_ref[0] - step
    ngate = 4 * width

    def point(fac_ref, top_frame, pick):
        start_frame = pick == frames - 1
        for start, size in chunks(size_d, 256):
            here = pl.ds(start, size)
            there = pl.ds(start + step * pitch, size)
            if tops and pick == top_frame:
                above = own_ref[pl.ds(start + (step + 1) * pitch, size), :].astype(F32)
            else:
                above = inc_refs[pick][here, :].astype(F32)
            dh = above
            if not start_frame:
                dh = dh + dh_ref[here, :]
            dc = dh * fac_ref[there, 0:width]
            if not start_frame:
                dc = dc + dc_ref[here, :]
            d_ref[here, 0:width] = (dc * fac_ref[there, width : 2 * width]).astype(BF)
            d_ref[here, width : 2 * width] = (dc * fac_ref[there, 2 * width : 3 * width]).astype(BF)
            d_ref[here, 2 * width : 3 * width] = (dc * fac_ref[there, 3 * width : 4 * width]).astype(BF)
            d_ref[here, 3 * width :] = (dh * fac_ref[there, 4 * width : 5 * width]).astype(BF)
            lo, hi = max(start, pitch), min(start + size, pitch + size_z)
            if hi > lo:
                rec = dc * fac_ref[there, 5 * width :]
                dcn_ref[lo - pitch : hi - pitch, :] = rec[lo - start : hi - start, :]

    top_frame = frames - 1 - step
    for number, pick in enumerate(picks):
        pl.when(frame == pick)(functools.partial(point, fac_refs[number], top_frame, pick))

    active = (frame >= picks[0]) & (frame <= picks[-1])

    @pl.when(active)
    def _():
        slot = pl.multiple_of(frame * (rows * cols), rows * cols)
        for row in range(rows):
            dgi_ref[pl.ds(slot + row * cols, cols), :] = d_ref[
                pl.ds(LEAD + (row + margin) * pitch, cols), :
            ]
        p_ref[0:8, :] = jnp.zeros((8, 6 * width), F32)
        p_ref[8 + size_z : 16 + size_z, :] = jnp.zeros((8, 6 * width), F32)
        for start, size in chunks(size_z, 448):
            total = None
            for a in range(3):
                part = jnp.dot(
                    d_ref[pl.ds(start + (2 - a) * pitch, size), :],
                    kernel_t_ref[a * ngate : (a + 1) * ngate, :],
                    preferred_element_type=F32,
                )
                total = part if total is None else total + part
            p_ref[pl.ds(8 + start, size), :] = total
        for start, size in chunks(size_z, 256):
            dz = (
                p_ref[pl.ds(8 + start, size), 2 * width : 4 * width]
                + p_ref[pl.ds(9 + start, size), 0 : 2 * width]
                + p_ref[pl.ds(7 + start, size), 4 * width :]
            )
            dx_ref[pl.ds(start, size), :] = dz[:, :width].astype(BF)
            dhn_ref[pl.ds(start, size), :] = dz[:, width:]
        for row in range(rows):
            dxi_ref[pl.ds(slot + row * cols, cols), :] = dx_ref[
                pl.ds(LEAD + (row + margin - 1) * pitch, cols), :
            ]


def picks_of(step, group, layers, frames):
    now = [frames - 1 - step + layers - 1 - layer for layer in group]
    return sorted(f for f in now if 0 <= f < frames)


def needs_of(step, group, layers, frames):
    has_inc = any(
        0 <= frames - 1 - step + layers - 1 - layer < frames for layer in group if layer < layers - 1
    )
    has_state = any(f < frames - 1 for f in picks_of(step, group, layers, frames))
    return has_inc, has_state, step > 0


def patch_kernel(pitch, rows, cols, edge, zs_ref, pt_ref, flat_ref):
    depth = zs_ref.shape[1]
    for a in range(3):
        for row in range(rows):
            flat_ref[row * cols : (row + 1) * cols, :] = zs_ref[
                pl.ds(LEAD + (edge + row + a) * pitch, cols), :
            ]
        pt_ref[a * depth : (a + 1) * depth, :] = flat_ref[...].T


def grad_kernel(cells, frame, count, begin, end, *refs):
    pts, dg_ref = refs[:count], refs[count]
    total_ref = None if begin else refs[count + 1]
    out_ref = refs[-1]
    block = 256
    for at in range(0, out_ref.shape[0], block):
        here = pl.ds(at, block)
        total = None if begin else total_ref[here, :]
        part = jnp.dot(
            pts[0][here, :], dg_ref[frame * cells : (frame + 1) * cells, :], preferred_element_type=F32
        )
        total = part if begin else total + part
        out_ref[here, :] = total.astype(out_ref.dtype)


def spec_v():
    return pl.BlockSpec(memory_space=pltpu.VMEM)


def spec_s():
    return pl.BlockSpec(memory_space=pltpu.SMEM)


def on_device(layer_input, hidden_prev, cell_prev, out_cot, bias, master, moment1, moment2):
    frames, rows, cols, width = (layer_input.shape[i] for i in (1, 3, 4, 5))
    ngate = 4 * width
    layers = lax.axis_size("section")
    layer = lax.axis_index("section")
    ntile = lax.axis_size("tile")
    tile = lax.axis_index("tile")
    ncols = ntile // TILE_ROWS
    pitch = cols + 2 * SIDE
    edge = frames + layers - 1

    own_rows = master[0].astype(BF)
    kernel = lax.all_to_all(jnp.tile(own_rows, (ntile, 1)), "tile", 0, 0, tiled=True)

    ids = (frames - 1 + layers - 1 - layer).astype(jnp.int32).reshape(1)
    packed = jnp.concatenate(
        [layer_input[0, :, 0], hidden_prev[0, :, 0], cell_prev[0, :, 0].astype(BF), out_cot[:, 0]], -1
    )
    deeps = [edge + 1 - (frames - 1 - f) for f in range(frames)]
    grid_row, grid_col = tile // ncols, tile % ncols

    def around(by, strip, keep):
        got = lax.ppermute(strip, "tile", [(i, by(i)) for i in range(ntile)])
        return jnp.where(keep, got, jnp.zeros_like(got))

    downs = jnp.concatenate([packed[f, rows - deeps[f] :] for f in range(frames)], 0)
    ups = jnp.concatenate([packed[f, : deeps[f]] for f in range(frames)], 0)
    above = around(lambda i: (i + ncols) % ntile, downs, grid_row > 0)
    below = around(lambda i: (i - ncols) % ntile, ups, grid_row < TILE_ROWS - 1)
    talls, at = [], 0
    for f in range(frames):
        talls.append(jnp.concatenate([above[at : at + deeps[f]], packed[f], below[at : at + deeps[f]]], 0))
        at += deeps[f]
    rights = jnp.concatenate([t[:, cols - SIDE :] for t in talls], 0)
    lefts = jnp.concatenate([t[:, :SIDE] for t in talls], 0)
    left = around(lambda i: i // ncols * ncols + (i + 1) % ncols, rights, grid_col > 0)
    right = around(lambda i: i // ncols * ncols + (i - 1) % ncols, lefts, grid_col < ncols - 1)

    size_e = LEAD + (rows + 2 * edge + 2) * pitch
    size_d = LEAD + (rows + 2 * edge) * pitch
    cells = rows * cols

    at = jnp.arange(size_d, dtype=jnp.int32) - LEAD + SIDE
    row_at = at // pitch - edge + grid_row * rows
    col_at = at % pitch - SIDE + grid_col * cols
    inside = (row_at >= 0) & (row_at < TILE_ROWS * rows) & (col_at >= 0) & (col_at < ncols * cols)
    mask = jnp.broadcast_to(inside[:, None], (size_d, width)).astype(BF)

    facs, pts, owns = [None] * frames, [None] * frames, [None] * frames
    for f in reversed(range(frames)):
        gap = edge + 1 - deeps[f]
        facs[f], zs, owns[f] = pl.pallas_call(
            functools.partial(
                gates_kernel, pitch, width, deeps[f], gap, sum(deeps[:f]),
                sum(rows + 2 * d for d in deeps[:f]),
            ),
            out_shape=(
                in_vmem((size_d, 6 * width), F32),
                in_vmem((size_e, 6 * width), BF),
                in_vmem((size_e, width), BF),
            ),
            in_specs=[spec_s()] + [spec_v()] * 8,
            out_specs=(spec_v(),) * 3,
            scratch_shapes=[pltpu.VMEM((size_e, 2 * width), BF), pltpu.VMEM((size_e + 16, 2 * width), F32)],
            compiler_params=params(20),
            cost_estimate=pl.CostEstimate(
                flops=2 * size_d * 18 * width * ngate, bytes_accessed=10 << 20, transcendentals=size_d * 5 * width
            ),
        )(ids, packed[f], above, below, left, right, mask, kernel, bias)
        pts[f] = pl.pallas_call(
            functools.partial(patch_kernel, pitch, rows, cols, edge),
            out_shape=in_vmem((18 * width, cells), BF),
            in_specs=[spec_v()],
            out_specs=spec_v(),
            scratch_shapes=[pltpu.VMEM((cells, 6 * width), BF)],
            compiler_params=params(16),
            cost_estimate=pl.CostEstimate(flops=0, bytes_accessed=8 << 20, transcendentals=0),
        )(zs)
    kernel_t = pl.pallas_call(
        turn_kernel,
        out_shape=in_vmem((3 * ngate, 6 * width), BF),
        in_specs=[spec_v()],
        out_specs=spec_v(),
        compiler_params=params(16),
        cost_estimate=pl.CostEstimate(flops=0, bytes_accessed=4 << 20, transcendentals=0),
    )(kernel)

    steps = layers + frames - 1
    upper, lower = tuple(range(layers // 2, layers)), tuple(range(layers // 2))
    states = {upper: None, lower: None}
    sent = {}
    kept = None
    total = None
    for step in range(steps):
        margin = edge - step
        size_z = LEAD + (rows + 2 * margin - 2) * pitch
        fresh = {}
        for group in (upper, lower):
            picks = picks_of(step, group, layers, frames)
            if not picks:
                continue
            has_inc, has_state, has_kept = needs_of(step, group, layers, frames)
            args = [ids, kernel_t] + [facs[f] for f in picks]
            if layers - 1 in group and step < frames:
                args.append(owns[frames - 1 - step])
            if has_inc:
                above_of = [frames - 1 - step + layers - f for f in picks]
                args += [sent[i] for i in above_of if i < layers]
            if has_state:
                args += list(states[group])
            if has_kept:
                args += list(kept)
            dx, cots, dgates, dh_rec, dc_rec = pl.pallas_call(
                functools.partial(step_kernel, step, group, layers, frames, pitch, rows, cols, width),
                out_shape=(
                    jax.ShapeDtypeStruct((size_z, width), BF),
                    in_vmem((frames * cells, width), BF),
                    in_vmem((frames * cells, ngate), BF),
                    in_vmem((size_z, width), F32),
                    in_vmem((size_z, width), F32),
                ),
                in_specs=[spec_s()] + [spec_v()] * (len(args) - 1),
                out_specs=(spec_v(),) * 5,
                scratch_shapes=[
                    pltpu.VMEM((size_z + 2 * pitch, ngate), BF),
                    pltpu.VMEM((size_z + 16, 6 * width), F32),
                ],
                input_output_aliases={len(args) - 2: 1, len(args) - 1: 2} if has_kept else {},
                compiler_params=params(20),
                cost_estimate=pl.CostEstimate(
                    flops=2 * size_z * 18 * width * ngate, bytes_accessed=10 << 20, transcendentals=0
                ),
            )(*args)
            kept = (cots, dgates)
            states[group] = (dh_rec, dc_rec)
            for i in group:
                if i > 0 and 0 <= frames - 1 - step + layers - 1 - i < frames:
                    fresh[i] = lax.ppermute(dx, "section", [(i, i - 1)])
        sent = fresh
        if step >= layers - 1:
            f = frames - 1 - (step - layers + 1)
            end = step == steps - 1
            args = [pts[f], kept[1]] + ([] if total is None else [total])
            total = pl.pallas_call(
                functools.partial(grad_kernel, cells, f, 1, total is None, end),
                out_shape=in_vmem((18 * width, ngate), BF if end else F32),
                in_specs=[spec_v()] * len(args),
                out_specs=spec_v(),
                compiler_params=params(16),
                cost_estimate=pl.CostEstimate(
                    flops=2 * cells * 18 * width * ngate, bytes_accessed=4 << 20, transcendentals=0
                ),
            )(*args)
    cots = kept[0]
    total, cots = lax.optimization_barrier((total, cots))
    arrived = lax.all_to_all(total, "tile", 0, 0, tiled=True)
    arrived, cots = lax.optimization_barrier((arrived, cots))
    input_cot = cots.reshape(frames, rows, cols, width)
    grad_rows = jnp.sum(arrived.reshape(ntile, -1, ngate).astype(F32), 0)
    new_moment1 = 0.9 * moment1[0] + 0.1 * grad_rows
    new_moment2 = 0.999 * moment2[0] + 0.001 * grad_rows * grad_rows
    fix1 = 1.0 - 0.9**10
    fix2 = 1.0 - 0.999**10
    step_size = new_moment1 / fix1 / (jnp.sqrt(new_moment2 / fix2) + 1e-08)
    new_master = master[0] - 0.001 * step_size - 0.0001 * master[0]
    return (input_cot[None, :, None], new_master[None], new_moment1[None], new_moment2[None])


def solution(mesh):
    return jax.shard_map(
        on_device,
        mesh=mesh,
        in_specs=(
            P("section", None, "tile", None, None, None),
            P("section", None, "tile", None, None, None),
            P("section", None, "tile", None, None, None),
            P(None, "tile", None, None, None),
            P("section", None),
            P("section", "tile", None),
            P("section", "tile", None),
            P("section", "tile", None),
        ),
        out_specs=(
            P("section", None, "tile", None, None, None),
            P("section", "tile", None),
            P("section", "tile", None),
            P("section", "tile", None),
        ),
        check_vma=False,
    )
```

```python
import functools

import jax
import jax.numpy as jnp
from jax import lax
from jax.experimental import pallas as pl
from jax.experimental.pallas import tpu as pltpu
from jax.sharding import PartitionSpec as P

TILE_ROWS = 4
BF = jnp.bfloat16
F32 = jnp.float32
SIDE = 8
LEAD = 16


def params(mib):
    return pltpu.CompilerParams(vmem_limit_bytes=mib << 20)


def chunks(size, most):
    units = size // 16
    count = -(-units * 16 // most)
    out, at = [], 0
    for i in range(count):
        end = units * (i + 1) // count
        out.append((at * 16, (end - at) * 16))
        at = end
    return out


def in_vmem(shape, dtype):
    return pltpu.VMEM(shape, dtype)


def sigmoid(x):
    return 0.5 * jnp.tanh(0.5 * x) + 0.5


def gates_kernel(pitch, width, deep, gap, at_row, at_side, ids_ref, mid_ref, above_ref, below_ref, left_ref, right_ref, mask_ref, kernel_ref, bias_ref, fac_ref, zs_ref, own_ref, flat_ref, z_ref):
    depth = 6 * width
    rows = mid_ref.shape[0]
    cols = pitch - 2 * SIDE
    tall = rows + 2 * deep
    size_e = zs_ref.shape[0]
    begin = gap * pitch
    stop = begin + LEAD + tall * pitch
    if gap:
        for lo, hi in ((0, begin), (stop, size_e)):
            z_ref[8 + lo : 8 + hi, :] = jnp.zeros((hi - lo, 2 * width), F32)
            flat_ref[lo:hi, :] = jnp.zeros((hi - lo, 2 * width), BF)
    z_ref[0:8, :] = jnp.zeros((8, 2 * width), F32)
    z_ref[8 + size_e :, :] = jnp.zeros((8, 2 * width), F32)

    def put(at, value):
        size = value.shape[0]
        z_ref[8 + at : 8 + at + size, :] = value[:, : 2 * width].astype(F32)
        flat_ref[at : at + size, :] = value[:, 2 * width :]

    none = jnp.zeros((SIDE, 4 * width), BF)
    for row in range(tall + 1):
        before = none if row == 0 else right_ref[at_side + row - 1]
        after = none if row == tall else left_ref[at_side + row]
        put(begin + row * pitch, jnp.concatenate([before, after], 0))
    for row in range(tall):
        at = begin + LEAD + row * pitch
        if row < deep:
            put(at, above_ref[at_row + row])
        elif row < deep + rows:
            put(at, mid_ref[row - deep])
        else:
            put(at, below_ref[at_row + row - deep - rows])
    for start, size in chunks(size_e, 256):
        here = pl.ds(start, size)
        own_ref[here, :] = flat_ref[here, width:]
        for b in range(3):
            zs_ref[here, b * 2 * width : (b + 1) * 2 * width] = z_ref[
                7 + b + start : 7 + b + start + size, :
            ].astype(BF)
    cells = fac_ref.shape[0] - 2 * begin
    for start, size in chunks(cells, 480):
        start = start + begin
        total = bias_ref[...]
        for a in range(3):
            total = total + jnp.dot(
                zs_ref[pl.ds(start + a * pitch, size), :],
                kernel_ref[a * depth : (a + 1) * depth, :],
                preferred_element_type=F32,
            )
        here = pl.ds(start, size)
        mask = mask_ref[here, :].astype(F32)
        c_prev = flat_ref[pl.ds(start + pitch, size), :width].astype(F32)
        i = sigmoid(total[:, :width])
        f = sigmoid(total[:, width : 2 * width])
        g = jnp.tanh(total[:, 2 * width : 3 * width])
        o = sigmoid(total[:, 3 * width :])
        tc = jnp.tanh(f * c_prev + i * g)
        fac_ref[here, 0:width] = o * (1.0 - tc * tc)
        fac_ref[here, width : 2 * width] = mask * g * i * (1.0 - i)
        fac_ref[here, 2 * width : 3 * width] = mask * c_prev * f * (1.0 - f)
        fac_ref[here, 3 * width : 4 * width] = mask * i * (1.0 - g * g)
        fac_ref[here, 4 * width : 5 * width] = mask * tc * o * (1.0 - o)
        fac_ref[here, 5 * width : 6 * width] = f


def turn_kernel(kernel_ref, turned_ref):
    depth, ngate = kernel_ref.shape[0] // 3, kernel_ref.shape[1]
    for a in range(3):
        turned_ref[a * ngate : (a + 1) * ngate, :] = kernel_ref[a * depth : (a + 1) * depth, :].T


def step_kernel(step, group, layers, frames, pitch, rows, cols, width, *refs):
    ids_ref, kernel_t_ref = refs[0], refs[1]
    picks = picks_of(step, group, layers, frames)
    fac_refs = refs[2 : 2 + len(picks)]
    at = 2 + len(picks)
    tops = layers - 1 in group and step < frames
    own_ref = refs[at] if tops else None
    at += 1 if tops else 0
    has_inc, has_state, has_kept = needs_of(step, group, layers, frames)
    inc_refs = {}
    for f in picks:
        if frames - 1 - step + layers - f < layers:
            inc_refs[f] = refs[at]
            at += 1
    if has_state:
        dh_ref, dc_ref = refs[at : at + 2]
        at += 2
    if has_kept:
        at += 2
    dx_ref, dxi_ref, dgi_ref, dhn_ref, dcn_ref, d_ref, p_ref = refs[at:]
    margin = frames + layers - 1 - step
    size_d = LEAD + (rows + 2 * margin) * pitch
    size_z = LEAD + (rows + 2 * margin - 2) * pitch
    frame = ids_ref[0] - step
    ngate = 4 * width

    def point(fac_ref, top_frame, pick):
        start_frame = pick == frames - 1
        for start, size in chunks(size_d, 256):
            here = pl.ds(start, size)
            there = pl.ds(start + step * pitch, size)
            if tops and pick == top_frame:
                above = own_ref[pl.ds(start + (step + 1) * pitch, size), :].astype(F32)
            else:
                above = inc_refs[pick][here, :].astype(F32)
            dh = above
            if not start_frame:
                dh = dh + dh_ref[here, :]
            dc = dh * fac_ref[there, 0:width]
            if not start_frame:
                dc = dc + dc_ref[here, :]
            d_ref[here, 0:width] = (dc * fac_ref[there, width : 2 * width]).astype(BF)
            d_ref[here, width : 2 * width] = (dc * fac_ref[there, 2 * width : 3 * width]).astype(BF)
            d_ref[here, 2 * width : 3 * width] = (dc * fac_ref[there, 3 * width : 4 * width]).astype(BF)
            d_ref[here, 3 * width :] = (dh * fac_ref[there, 4 * width : 5 * width]).astype(BF)
            lo, hi = max(start, pitch), min(start + size, pitch + size_z)
            if hi > lo:
                rec = dc * fac_ref[there, 5 * width :]
                dcn_ref[lo - pitch : hi - pitch, :] = rec[lo - start : hi - start, :]

    top_frame = frames - 1 - step
    for number, pick in enumerate(picks):
        pl.when(frame == pick)(functools.partial(point, fac_refs[number], top_frame, pick))

    active = (frame >= picks[0]) & (frame <= picks[-1])

    @pl.when(active)
    def _():
        slot = pl.multiple_of(frame * (rows * cols), rows * cols)
        for row in range(rows):
            dgi_ref[pl.ds(slot + row * cols, cols), :] = d_ref[
                pl.ds(LEAD + (row + margin) * pitch, cols), :
            ]
        p_ref[0:8, :] = jnp.zeros((8, 6 * width), F32)
        p_ref[8 + size_z : 16 + size_z, :] = jnp.zeros((8, 6 * width), F32)
        for start, size in chunks(size_z, 448):
            total = None
            for a in range(3):
                part = jnp.dot(
                    d_ref[pl.ds(start + (2 - a) * pitch, size), :],
                    kernel_t_ref[a * ngate : (a + 1) * ngate, :],
                    preferred_element_type=F32,
                )
                total = part if total is None else total + part
            p_ref[pl.ds(8 + start, size), :] = total
        for start, size in chunks(size_z, 256):
            dz = (
                p_ref[pl.ds(8 + start, size), 2 * width : 4 * width]
                + p_ref[pl.ds(9 + start, size), 0 : 2 * width]
                + p_ref[pl.ds(7 + start, size), 4 * width :]
            )
            dx_ref[pl.ds(start, size), :] = dz[:, :width].astype(BF)
            dhn_ref[pl.ds(start, size), :] = dz[:, width:]
        for row in range(rows):
            dxi_ref[pl.ds(slot + row * cols, cols), :] = dx_ref[
                pl.ds(LEAD + (row + margin - 1) * pitch, cols), :
            ]


def picks_of(step, group, layers, frames):
    now = [frames - 1 - step + layers - 1 - layer for layer in group]
    return sorted(f for f in now if 0 <= f < frames)


def needs_of(step, group, layers, frames):
    has_inc = any(
        0 <= frames - 1 - step + layers - 1 - layer < frames for layer in group if layer < layers - 1
    )
    has_state = any(f < frames - 1 for f in picks_of(step, group, layers, frames))
    return has_inc, has_state, step > 0


def patch_kernel(pitch, rows, cols, edge, zs_ref, pt_ref, flat_ref):
    depth = zs_ref.shape[1]
    for a in range(3):
        for row in range(rows):
            flat_ref[row * cols : (row + 1) * cols, :] = zs_ref[
                pl.ds(LEAD + (edge + row + a) * pitch, cols), :
            ]
        pt_ref[a * depth : (a + 1) * depth, :] = flat_ref[...].T


def grad_kernel(cells, frame, count, begin, end, *refs):
    pts, dg_ref = refs[:count], refs[count]
    total_ref = None if begin else refs[count + 1]
    out_ref = refs[-1]
    block = 256
    for at in range(0, out_ref.shape[0], block):
        here = pl.ds(at, block)
        total = None if begin else total_ref[here, :]
        part = jnp.dot(
            pts[0][here, :], dg_ref[frame * cells : (frame + 1) * cells, :], preferred_element_type=F32
        )
        total = part if begin else total + part
        out_ref[here, :] = total.astype(out_ref.dtype)


def spec_v():
    return pl.BlockSpec(memory_space=pltpu.VMEM)


def spec_s():
    return pl.BlockSpec(memory_space=pltpu.SMEM)


def place_kernel(at_ref, *refs):
    out_ref = refs[-1]
    count = refs[0].shape[0]
    for number, ref in enumerate(refs[:-1]):
        for j in range(count):
            out_ref[at_ref[number * count + j]] = ref[j]


def gather_rows(own, ntile, tile):
    ring = 4
    planes = ntile // (ring * ring)
    hops = (0, 1, -1, 2)

    def where(i):
        return i // (ring * ring), i // ring % ring, i % ring

    def index(plane, z, y):
        return (plane % planes * ring + z % ring) * ring + y % ring

    def move(x, by):
        pairs = []
        for i in range(ntile):
            plane, z, y = where(i)
            pairs.append((i, index(plane + by[0], z + by[1], y + by[2])))
        return lax.ppermute(x, "tile", pairs)

    other = move(own, (1, 0, 0))
    near = jnp.stack([own] + [move(own, (0, h, 0)) for h in hops[1:]])
    far = jnp.stack([other] + [move(other, (0, 0, h)) for h in hops[1:]])
    parts = [near] + [move(near, (0, 0, h)) for h in hops[1:]]
    parts += [far] + [move(far, (0, h, 0)) for h in hops[1:]]
    plane, z, y = where(tile)
    at = [index(plane, z - hz, y - hy) for hy in hops for hz in hops]
    at += [index(plane + 1, z - hz, y - hy) for hz in hops for hy in hops]
    return pl.pallas_call(
        place_kernel,
        out_shape=in_vmem((ntile,) + own.shape, BF),
        in_specs=[spec_s()] + [spec_v()] * len(parts),
        out_specs=spec_v(),
        compiler_params=params(16),
        cost_estimate=pl.CostEstimate(flops=0, bytes_accessed=4 << 20, transcendentals=0),
    )(jnp.stack(at).astype(jnp.int32), *parts)


def on_device(layer_input, hidden_prev, cell_prev, out_cot, bias, master, moment1, moment2):
    frames, rows, cols, width = (layer_input.shape[i] for i in (1, 3, 4, 5))
    ngate = 4 * width
    layers = lax.axis_size("section")
    layer = lax.axis_index("section")
    ntile = lax.axis_size("tile")
    tile = lax.axis_index("tile")
    ncols = ntile // TILE_ROWS
    pitch = cols + 2 * SIDE
    edge = frames + layers - 1

    own_rows = master[0].astype(BF)
    kernel = gather_rows(own_rows, ntile, tile).reshape(-1, ngate)

    ids = (frames - 1 + layers - 1 - layer).astype(jnp.int32).reshape(1)
    packed = jnp.concatenate(
        [layer_input[0, :, 0], hidden_prev[0, :, 0], cell_prev[0, :, 0].astype(BF), out_cot[:, 0]], -1
    )
    deeps = [edge + 1 - (frames - 1 - f) for f in range(frames)]
    grid_row, grid_col = tile // ncols, tile % ncols

    def around(by, strip, keep):
        got = lax.ppermute(strip, "tile", [(i, by(i)) for i in range(ntile)])
        return jnp.where(keep, got, jnp.zeros_like(got))

    downs = jnp.concatenate([packed[f, rows - deeps[f] :] for f in range(frames)], 0)
    ups = jnp.concatenate([packed[f, : deeps[f]] for f in range(frames)], 0)
    above = around(lambda i: (i + ncols) % ntile, downs, grid_row > 0)
    below = around(lambda i: (i - ncols) % ntile, ups, grid_row < TILE_ROWS - 1)
    talls, at = [], 0
    for f in range(frames):
        talls.append(jnp.concatenate([above[at : at + deeps[f]], packed[f], below[at : at + deeps[f]]], 0))
        at += deeps[f]
    rights = jnp.concatenate([t[:, cols - SIDE :] for t in talls], 0)
    lefts = jnp.concatenate([t[:, :SIDE] for t in talls], 0)
    left = around(lambda i: i // ncols * ncols + (i + 1) % ncols, rights, grid_col > 0)
    right = around(lambda i: i // ncols * ncols + (i - 1) % ncols, lefts, grid_col < ncols - 1)

    size_e = LEAD + (rows + 2 * edge + 2) * pitch
    size_d = LEAD + (rows + 2 * edge) * pitch
    cells = rows * cols

    at = jnp.arange(size_d, dtype=jnp.int32) - LEAD + SIDE
    row_at = at // pitch - edge + grid_row * rows
    col_at = at % pitch - SIDE + grid_col * cols
    inside = (row_at >= 0) & (row_at < TILE_ROWS * rows) & (col_at >= 0) & (col_at < ncols * cols)
    mask = jnp.broadcast_to(inside[:, None], (size_d, width)).astype(BF)

    facs, pts, owns = [None] * frames, [None] * frames, [None] * frames
    for f in reversed(range(frames)):
        gap = edge + 1 - deeps[f]
        facs[f], zs, owns[f] = pl.pallas_call(
            functools.partial(
                gates_kernel, pitch, width, deeps[f], gap, sum(deeps[:f]),
                sum(rows + 2 * d for d in deeps[:f]),
            ),
            out_shape=(
                in_vmem((size_d, 6 * width), F32),
                in_vmem((size_e, 6 * width), BF),
                in_vmem((size_e, width), BF),
            ),
            in_specs=[spec_s()] + [spec_v()] * 8,
            out_specs=(spec_v(),) * 3,
            scratch_shapes=[pltpu.VMEM((size_e, 2 * width), BF), pltpu.VMEM((size_e + 16, 2 * width), F32)],
            compiler_params=params(20),
            cost_estimate=pl.CostEstimate(
                flops=2 * size_d * 18 * width * ngate, bytes_accessed=10 << 20, transcendentals=size_d * 5 * width
            ),
        )(ids, packed[f], above, below, left, right, mask, kernel, bias)
        pts[f] = pl.pallas_call(
            functools.partial(patch_kernel, pitch, rows, cols, edge),
            out_shape=in_vmem((18 * width, cells), BF),
            in_specs=[spec_v()],
            out_specs=spec_v(),
            scratch_shapes=[pltpu.VMEM((cells, 6 * width), BF)],
            compiler_params=params(16),
            cost_estimate=pl.CostEstimate(flops=0, bytes_accessed=8 << 20, transcendentals=0),
        )(zs)
    kernel_t = pl.pallas_call(
        turn_kernel,
        out_shape=in_vmem((3 * ngate, 6 * width), BF),
        in_specs=[spec_v()],
        out_specs=spec_v(),
        compiler_params=params(16),
        cost_estimate=pl.CostEstimate(flops=0, bytes_accessed=4 << 20, transcendentals=0),
    )(kernel)

    steps = layers + frames - 1
    upper, lower = tuple(range(layers // 2, layers)), tuple(range(layers // 2))
    states = {upper: None, lower: None}
    sent = {}
    kept = None
    total = None
    for step in range(steps):
        margin = edge - step
        size_z = LEAD + (rows + 2 * margin - 2) * pitch
        fresh = {}
        for group in (upper, lower):
            picks = picks_of(step, group, layers, frames)
            if not picks:
                continue
            has_inc, has_state, has_kept = needs_of(step, group, layers, frames)
            args = [ids, kernel_t] + [facs[f] for f in picks]
            if layers - 1 in group and step < frames:
                args.append(owns[frames - 1 - step])
            if has_inc:
                above_of = [frames - 1 - step + layers - f for f in picks]
                args += [sent[i] for i in above_of if i < layers]
            if has_state:
                args += list(states[group])
            if has_kept:
                args += list(kept)
            dx, cots, dgates, dh_rec, dc_rec = pl.pallas_call(
                functools.partial(step_kernel, step, group, layers, frames, pitch, rows, cols, width),
                out_shape=(
                    jax.ShapeDtypeStruct((size_z, width), BF),
                    in_vmem((frames * cells, width), BF),
                    in_vmem((frames * cells, ngate), BF),
                    in_vmem((size_z, width), F32),
                    in_vmem((size_z, width), F32),
                ),
                in_specs=[spec_s()] + [spec_v()] * (len(args) - 1),
                out_specs=(spec_v(),) * 5,
                scratch_shapes=[
                    pltpu.VMEM((size_z + 2 * pitch, ngate), BF),
                    pltpu.VMEM((size_z + 16, 6 * width), F32),
                ],
                input_output_aliases={len(args) - 2: 1, len(args) - 1: 2} if has_kept else {},
                compiler_params=params(20),
                cost_estimate=pl.CostEstimate(
                    flops=2 * size_z * 18 * width * ngate, bytes_accessed=10 << 20, transcendentals=0
                ),
            )(*args)
            kept = (cots, dgates)
            states[group] = (dh_rec, dc_rec)
            for i in group:
                if i > 0 and 0 <= frames - 1 - step + layers - 1 - i < frames:
                    fresh[i] = lax.ppermute(dx, "section", [(i, i - 1)])
        sent = fresh
        if step >= layers - 1:
            f = frames - 1 - (step - layers + 1)
            end = step == steps - 1
            args = [pts[f], kept[1]] + ([] if total is None else [total])
            total = pl.pallas_call(
                functools.partial(grad_kernel, cells, f, 1, total is None, end),
                out_shape=in_vmem((18 * width, ngate), BF if end else F32),
                in_specs=[spec_v()] * len(args),
                out_specs=spec_v(),
                compiler_params=params(16),
                cost_estimate=pl.CostEstimate(
                    flops=2 * cells * 18 * width * ngate, bytes_accessed=4 << 20, transcendentals=0
                ),
            )(*args)
    cots = kept[0]
    total, cots = lax.optimization_barrier((total, cots))
    arrived = lax.all_to_all(total, "tile", 0, 0, tiled=True)
    arrived, cots = lax.optimization_barrier((arrived, cots))
    input_cot = cots.reshape(frames, rows, cols, width)
    grad_rows = jnp.sum(arrived.reshape(ntile, -1, ngate).astype(F32), 0)
    new_moment1 = 0.9 * moment1[0] + 0.1 * grad_rows
    new_moment2 = 0.999 * moment2[0] + 0.001 * grad_rows * grad_rows
    fix1 = 1.0 - 0.9**10
    fix2 = 1.0 - 0.999**10
    step_size = new_moment1 / fix1 / (jnp.sqrt(new_moment2 / fix2) + 1e-08)
    new_master = master[0] - 0.001 * step_size - 0.0001 * master[0]
    return (input_cot[None, :, None], new_master[None], new_moment1[None], new_moment2[None])


def solution(mesh):
    return jax.shard_map(
        on_device,
        mesh=mesh,
        in_specs=(
            P("section", None, "tile", None, None, None),
            P("section", None, "tile", None, None, None),
            P("section", None, "tile", None, None, None),
            P(None, "tile", None, None, None),
            P("section", None),
            P("section", "tile", None),
            P("section", "tile", None),
            P("section", "tile", None),
        ),
        out_specs=(
            P("section", None, "tile", None, None, None),
            P("section", "tile", None),
            P("section", "tile", None),
            P("section", "tile", None),
        ),
        check_vma=False,
    )
```

```python
import functools

import jax
import jax.numpy as jnp
from jax import lax
from jax.experimental import pallas as pl
from jax.experimental.pallas import tpu as pltpu
from jax.sharding import PartitionSpec as P

TILE_ROWS = 4
BF = jnp.bfloat16
F32 = jnp.float32
SIDE = 8
LEAD = 16


def params(mib):
    return pltpu.CompilerParams(vmem_limit_bytes=mib << 20)


def chunks(size, most):
    units = size // 16
    count = -(-units * 16 // most)
    out, at = [], 0
    for i in range(count):
        end = units * (i + 1) // count
        out.append((at * 16, (end - at) * 16))
        at = end
    return out


def in_vmem(shape, dtype):
    return pltpu.VMEM(shape, dtype)


def sigmoid(x):
    return 0.5 * jnp.tanh(0.5 * x) + 0.5


def gates_kernel(pitch, width, deep, gap, at_row, at_side, ids_ref, mid_ref, above_ref, below_ref, left_ref, right_ref, mask_ref, kernel_ref, bias_ref, fac_ref, zs_ref, own_ref, flat_ref, z_ref):
    depth = 6 * width
    rows = mid_ref.shape[0]
    cols = pitch - 2 * SIDE
    tall = rows + 2 * deep
    size_e = zs_ref.shape[0]
    begin = gap * pitch
    stop = begin + LEAD + tall * pitch
    if gap:
        for lo, hi in ((0, begin), (stop, size_e)):
            z_ref[8 + lo : 8 + hi, :] = jnp.zeros((hi - lo, 2 * width), F32)
            flat_ref[lo:hi, :] = jnp.zeros((hi - lo, 2 * width), BF)
    z_ref[0:8, :] = jnp.zeros((8, 2 * width), F32)
    z_ref[8 + size_e :, :] = jnp.zeros((8, 2 * width), F32)

    def put(at, value):
        size = value.shape[0]
        z_ref[8 + at : 8 + at + size, :] = value[:, : 2 * width].astype(F32)
        flat_ref[at : at + size, :] = value[:, 2 * width :]

    none = jnp.zeros((SIDE, 4 * width), BF)
    for row in range(tall + 1):
        before = none if row == 0 else right_ref[at_side + row - 1]
        after = none if row == tall else left_ref[at_side + row]
        put(begin + row * pitch, jnp.concatenate([before, after], 0))
    for row in range(tall):
        at = begin + LEAD + row * pitch
        if row < deep:
            put(at, above_ref[at_row + row])
        elif row < deep + rows:
            put(at, mid_ref[row - deep])
        else:
            put(at, below_ref[at_row + row - deep - rows])
    for start, size in chunks(size_e, 256):
        here = pl.ds(start, size)
        own_ref[here, :] = flat_ref[here, width:]
        for b in range(3):
            zs_ref[here, b * 2 * width : (b + 1) * 2 * width] = z_ref[
                7 + b + start : 7 + b + start + size, :
            ].astype(BF)
    cells = fac_ref.shape[0] - 2 * begin
    for start, size in chunks(cells, 480):
        start = start + begin
        total = bias_ref[...]
        for a in range(3):
            total = total + jnp.dot(
                zs_ref[pl.ds(start + a * pitch, size), :],
                kernel_ref[a * depth : (a + 1) * depth, :],
                preferred_element_type=F32,
            )
        here = pl.ds(start, size)
        mask = mask_ref[here, :].astype(F32)
        c_prev = flat_ref[pl.ds(start + pitch, size), :width].astype(F32)
        i = sigmoid(total[:, :width])
        f = sigmoid(total[:, width : 2 * width])
        g = jnp.tanh(total[:, 2 * width : 3 * width])
        o = sigmoid(total[:, 3 * width :])
        tc = jnp.tanh(f * c_prev + i * g)
        fac_ref[here, 0:width] = o * (1.0 - tc * tc)
        fac_ref[here, width : 2 * width] = mask * g * i * (1.0 - i)
        fac_ref[here, 2 * width : 3 * width] = mask * c_prev * f * (1.0 - f)
        fac_ref[here, 3 * width : 4 * width] = mask * i * (1.0 - g * g)
        fac_ref[here, 4 * width : 5 * width] = mask * tc * o * (1.0 - o)
        fac_ref[here, 5 * width : 6 * width] = f


def turn_kernel(kernel_ref, turned_ref):
    depth, ngate = kernel_ref.shape[0] // 3, kernel_ref.shape[1]
    for a in range(3):
        turned_ref[a * ngate : (a + 1) * ngate, :] = kernel_ref[a * depth : (a + 1) * depth, :].T


def step_kernel(step, group, layers, frames, pitch, rows, cols, width, *refs):
    ids_ref, kernel_t_ref = refs[0], refs[1]
    picks = picks_of(step, group, layers, frames)
    fac_refs = refs[2 : 2 + len(picks)]
    at = 2 + len(picks)
    tops = layers - 1 in group and step < frames
    own_ref = refs[at] if tops else None
    at += 1 if tops else 0
    has_inc, has_state, has_kept = needs_of(step, group, layers, frames)
    inc_refs = {}
    for f in picks:
        if frames - 1 - step + layers - f < layers:
            inc_refs[f] = refs[at]
            at += 1
    if has_state:
        dh_ref, dc_ref = refs[at : at + 2]
        at += 2
    if has_kept:
        at += 2
    dx_ref, dxi_ref, dgi_ref, dhn_ref, dcn_ref, d_ref, p_ref = refs[at:]
    margin = frames + layers - 1 - step
    size_d = LEAD + (rows + 2 * margin) * pitch
    size_z = LEAD + (rows + 2 * margin - 2) * pitch
    frame = ids_ref[0] - step
    ngate = 4 * width

    def point(fac_ref, top_frame, pick):
        start_frame = pick == frames - 1
        for start, size in chunks(size_d, 256):
            here = pl.ds(start, size)
            there = pl.ds(start + step * pitch, size)
            if tops and pick == top_frame:
                above = own_ref[pl.ds(start + (step + 1) * pitch, size), :].astype(F32)
            else:
                above = inc_refs[pick][here, :].astype(F32)
            dh = above
            if not start_frame:
                dh = dh + dh_ref[here, :]
            dc = dh * fac_ref[there, 0:width]
            if not start_frame:
                dc = dc + dc_ref[here, :]
            d_ref[here, 0:width] = (dc * fac_ref[there, width : 2 * width]).astype(BF)
            d_ref[here, width : 2 * width] = (dc * fac_ref[there, 2 * width : 3 * width]).astype(BF)
            d_ref[here, 2 * width : 3 * width] = (dc * fac_ref[there, 3 * width : 4 * width]).astype(BF)
            d_ref[here, 3 * width :] = (dh * fac_ref[there, 4 * width : 5 * width]).astype(BF)
            lo, hi = max(start, pitch), min(start + size, pitch + size_z)
            if hi > lo:
                rec = dc * fac_ref[there, 5 * width :]
                dcn_ref[lo - pitch : hi - pitch, :] = rec[lo - start : hi - start, :]

    top_frame = frames - 1 - step
    for number, pick in enumerate(picks):
        pl.when(frame == pick)(functools.partial(point, fac_refs[number], top_frame, pick))

    active = (frame >= picks[0]) & (frame <= picks[-1])

    @pl.when(active)
    def _():
        slot = pl.multiple_of(frame * (rows * cols), rows * cols)
        for row in range(rows):
            dgi_ref[pl.ds(slot + row * cols, cols), :] = d_ref[
                pl.ds(LEAD + (row + margin) * pitch, cols), :
            ]
        p_ref[0:8, :] = jnp.zeros((8, 6 * width), F32)
        p_ref[8 + size_z : 16 + size_z, :] = jnp.zeros((8, 6 * width), F32)
        for start, size in chunks(size_z, 448):
            total = None
            for a in range(3):
                part = jnp.dot(
                    d_ref[pl.ds(start + (2 - a) * pitch, size), :],
                    kernel_t_ref[a * ngate : (a + 1) * ngate, :],
                    preferred_element_type=F32,
                )
                total = part if total is None else total + part
            p_ref[pl.ds(8 + start, size), :] = total
        for start, size in chunks(size_z, 256):
            dz = (
                p_ref[pl.ds(8 + start, size), 2 * width : 4 * width]
                + p_ref[pl.ds(9 + start, size), 0 : 2 * width]
                + p_ref[pl.ds(7 + start, size), 4 * width :]
            )
            dx_ref[pl.ds(start, size), :] = dz[:, :width].astype(BF)
            dhn_ref[pl.ds(start, size), :] = dz[:, width:]
        for row in range(rows):
            dxi_ref[pl.ds(slot + row * cols, cols), :] = dx_ref[
                pl.ds(LEAD + (row + margin - 1) * pitch, cols), :
            ]


def picks_of(step, group, layers, frames):
    now = [frames - 1 - step + layers - 1 - layer for layer in group]
    return sorted(f for f in now if 0 <= f < frames)


def needs_of(step, group, layers, frames):
    has_inc = any(
        0 <= frames - 1 - step + layers - 1 - layer < frames for layer in group if layer < layers - 1
    )
    has_state = any(f < frames - 1 for f in picks_of(step, group, layers, frames))
    return has_inc, has_state, step > 0


def patch_kernel(pitch, rows, cols, edge, zs_ref, pt_ref, flat_ref):
    depth = zs_ref.shape[1]
    for a in range(3):
        for row in range(rows):
            flat_ref[row * cols : (row + 1) * cols, :] = zs_ref[
                pl.ds(LEAD + (edge + row + a) * pitch, cols), :
            ]
        pt_ref[a * depth : (a + 1) * depth, :] = flat_ref[...].T


def grad_kernel(cells, frame, count, begin, end, *refs):
    pts, dg_ref = refs[:count], refs[count]
    total_ref = None if begin else refs[count + 1]
    out_ref = refs[-1]
    block = 256
    for at in range(0, out_ref.shape[0], block):
        here = pl.ds(at, block)
        total = None if begin else total_ref[here, :]
        part = jnp.dot(
            pts[0][here, :], dg_ref[frame * cells : (frame + 1) * cells, :], preferred_element_type=F32
        )
        total = part if begin else total + part
        out_ref[here, :] = total.astype(out_ref.dtype)


def spec_v():
    return pl.BlockSpec(memory_space=pltpu.VMEM)


def spec_s():
    return pl.BlockSpec(memory_space=pltpu.SMEM)


def place_kernel(at_ref, come_ref, out_ref):
    for j in range(out_ref.shape[0]):
        out_ref[at_ref[j]] = come_ref[j]


RING = 4


def on_ring(own, ntile):
    def move(x, by):
        pairs = [(i, i // 16 * 16 + (i // RING + by) % RING * RING + i % RING) for i in range(ntile)]
        return lax.ppermute(x, "tile", pairs)

    return jnp.stack([own] + [move(own, h) for h in (1, -1, 2)])


def all_rows(near, ntile, tile):
    members = ntile // RING
    groups = [
        [plane * 16 + z * RING + y for plane in range(members // RING) for y in range(RING)] for z in range(RING)
    ]
    come = lax.all_to_all(
        jnp.tile(near, (members, 1, 1)), "tile", 0, 0, axis_index_groups=groups, tiled=True
    )
    z = tile // RING % RING
    at = [
        plane * 16 + (z - h) % RING * RING + y
        for plane in range(members // RING)
        for y in range(RING)
        for h in (0, 1, -1, 2)
    ]
    return pl.pallas_call(
        place_kernel,
        out_shape=in_vmem(come.shape, BF),
        in_specs=[spec_s(), spec_v()],
        out_specs=spec_v(),
        compiler_params=params(16),
        cost_estimate=pl.CostEstimate(flops=0, bytes_accessed=4 << 20, transcendentals=0),
    )(jnp.stack(at).astype(jnp.int32), come)


def on_device(layer_input, hidden_prev, cell_prev, out_cot, bias, master, moment1, moment2):
    frames, rows, cols, width = (layer_input.shape[i] for i in (1, 3, 4, 5))
    ngate = 4 * width
    layers = lax.axis_size("section")
    layer = lax.axis_index("section")
    ntile = lax.axis_size("tile")
    tile = lax.axis_index("tile")
    ncols = ntile // TILE_ROWS
    pitch = cols + 2 * SIDE
    edge = frames + layers - 1

    near = on_ring(master[0].astype(BF), ntile)
    kernel = all_rows(near, ntile, tile).reshape(-1, ngate)

    ids = (frames - 1 + layers - 1 - layer).astype(jnp.int32).reshape(1)
    packed = jnp.concatenate(
        [layer_input[0, :, 0], hidden_prev[0, :, 0], cell_prev[0, :, 0].astype(BF), out_cot[:, 0]], -1
    )
    deeps = [edge + 1 - (frames - 1 - f) for f in range(frames)]
    grid_row, grid_col = tile // ncols, tile % ncols

    def around(by, strip, keep):
        got = lax.ppermute(strip, "tile", [(i, by(i)) for i in range(ntile)])
        return jnp.where(keep, got, jnp.zeros_like(got))

    margins = {}
    before = near
    for part in ((frames - 1,), tuple(range(frames - 1))):
        downs = jnp.concatenate([packed[f, rows - deeps[f] :] for f in part], 0)
        ups = jnp.concatenate([packed[f, : deeps[f]] for f in part], 0)
        downs, ups, _ = lax.optimization_barrier((downs, ups, before))
        above = around(lambda i: (i + ncols) % ntile, downs, grid_row > 0)
        below = around(lambda i: (i - ncols) % ntile, ups, grid_row < TILE_ROWS - 1)
        before = (above, below)
        talls, at = [], 0
        for f in part:
            talls.append(jnp.concatenate([above[at : at + deeps[f]], packed[f], below[at : at + deeps[f]]], 0))
            at += deeps[f]
        rights = jnp.concatenate([t[:, cols - SIDE :] for t in talls], 0)
        lefts = jnp.concatenate([t[:, :SIDE] for t in talls], 0)
        left = around(lambda i: i // ncols * ncols + (i + 1) % ncols, rights, grid_col > 0)
        right = around(lambda i: i // ncols * ncols + (i - 1) % ncols, lefts, grid_col < ncols - 1)
        for number, f in enumerate(part):
            ahead = part[:number]
            margins[f] = (
                (above, below, left, right),
                sum(deeps[g] for g in ahead),
                sum(rows + 2 * deeps[g] for g in ahead),
            )

    size_e = LEAD + (rows + 2 * edge + 2) * pitch
    size_d = LEAD + (rows + 2 * edge) * pitch
    cells = rows * cols

    at = jnp.arange(size_d, dtype=jnp.int32) - LEAD + SIDE
    row_at = at // pitch - edge + grid_row * rows
    col_at = at % pitch - SIDE + grid_col * cols
    inside = (row_at >= 0) & (row_at < TILE_ROWS * rows) & (col_at >= 0) & (col_at < ncols * cols)
    mask = jnp.broadcast_to(inside[:, None], (size_d, width)).astype(BF)

    facs, pts, owns = [None] * frames, [None] * frames, [None] * frames
    for f in reversed(range(frames)):
        gap = edge + 1 - deeps[f]
        strips, at_row, at_side = margins[f]
        facs[f], zs, owns[f] = pl.pallas_call(
            functools.partial(
                gates_kernel, pitch, width, deeps[f], gap, at_row, at_side
            ),
            out_shape=(
                in_vmem((size_d, 6 * width), F32),
                in_vmem((size_e, 6 * width), BF),
                in_vmem((size_e, width), BF),
            ),
            in_specs=[spec_s()] + [spec_v()] * 8,
            out_specs=(spec_v(),) * 3,
            scratch_shapes=[pltpu.VMEM((size_e, 2 * width), BF), pltpu.VMEM((size_e + 16, 2 * width), F32)],
            compiler_params=params(20),
            cost_estimate=pl.CostEstimate(
                flops=2 * size_d * 18 * width * ngate, bytes_accessed=10 << 20, transcendentals=size_d * 5 * width
            ),
        )(ids, packed[f], *strips, mask, kernel, bias)
        pts[f] = pl.pallas_call(
            functools.partial(patch_kernel, pitch, rows, cols, edge),
            out_shape=in_vmem((18 * width, cells), BF),
            in_specs=[spec_v()],
            out_specs=spec_v(),
            scratch_shapes=[pltpu.VMEM((cells, 6 * width), BF)],
            compiler_params=params(16),
            cost_estimate=pl.CostEstimate(flops=0, bytes_accessed=8 << 20, transcendentals=0),
        )(zs)
    kernel_t = pl.pallas_call(
        turn_kernel,
        out_shape=in_vmem((3 * ngate, 6 * width), BF),
        in_specs=[spec_v()],
        out_specs=spec_v(),
        compiler_params=params(16),
        cost_estimate=pl.CostEstimate(flops=0, bytes_accessed=4 << 20, transcendentals=0),
    )(kernel)

    steps = layers + frames - 1
    upper, lower = tuple(range(layers // 2, layers)), tuple(range(layers // 2))
    states = {upper: None, lower: None}
    sent = {}
    kept = None
    total = None
    for step in range(steps):
        margin = edge - step
        size_z = LEAD + (rows + 2 * margin - 2) * pitch
        fresh = {}
        for group in (upper, lower):
            picks = picks_of(step, group, layers, frames)
            if not picks:
                continue
            has_inc, has_state, has_kept = needs_of(step, group, layers, frames)
            args = [ids, kernel_t] + [facs[f] for f in picks]
            if layers - 1 in group and step < frames:
                args.append(owns[frames - 1 - step])
            if has_inc:
                above_of = [frames - 1 - step + layers - f for f in picks]
                args += [sent[i] for i in above_of if i < layers]
            if has_state:
                args += list(states[group])
            if has_kept:
                args += list(kept)
            dx, cots, dgates, dh_rec, dc_rec = pl.pallas_call(
                functools.partial(step_kernel, step, group, layers, frames, pitch, rows, cols, width),
                out_shape=(
                    jax.ShapeDtypeStruct((size_z, width), BF),
                    in_vmem((frames * cells, width), BF),
                    in_vmem((frames * cells, ngate), BF),
                    in_vmem((size_z, width), F32),
                    in_vmem((size_z, width), F32),
                ),
                in_specs=[spec_s()] + [spec_v()] * (len(args) - 1),
                out_specs=(spec_v(),) * 5,
                scratch_shapes=[
                    pltpu.VMEM((size_z + 2 * pitch, ngate), BF),
                    pltpu.VMEM((size_z + 16, 6 * width), F32),
                ],
                input_output_aliases={len(args) - 2: 1, len(args) - 1: 2} if has_kept else {},
                compiler_params=params(20),
                cost_estimate=pl.CostEstimate(
                    flops=2 * size_z * 18 * width * ngate, bytes_accessed=10 << 20, transcendentals=0
                ),
            )(*args)
            kept = (cots, dgates)
            states[group] = (dh_rec, dc_rec)
            for i in group:
                if i > 0 and 0 <= frames - 1 - step + layers - 1 - i < frames:
                    fresh[i] = lax.ppermute(dx, "section", [(i, i - 1)])
        sent = fresh
        if step >= layers - 1:
            f = frames - 1 - (step - layers + 1)
            end = step == steps - 1
            args = [pts[f], kept[1]] + ([] if total is None else [total])
            total = pl.pallas_call(
                functools.partial(grad_kernel, cells, f, 1, total is None, end),
                out_shape=in_vmem((18 * width, ngate), BF if end else F32),
                in_specs=[spec_v()] * len(args),
                out_specs=spec_v(),
                compiler_params=params(16),
                cost_estimate=pl.CostEstimate(
                    flops=2 * cells * 18 * width * ngate, bytes_accessed=4 << 20, transcendentals=0
                ),
            )(*args)
    cots = kept[0]
    total, cots = lax.optimization_barrier((total, cots))
    arrived = lax.all_to_all(total, "tile", 0, 0, tiled=True)
    arrived, cots = lax.optimization_barrier((arrived, cots))
    input_cot = cots.reshape(frames, rows, cols, width)
    grad_rows = jnp.sum(arrived.reshape(ntile, -1, ngate).astype(F32), 0)
    new_moment1 = 0.9 * moment1[0] + 0.1 * grad_rows
    new_moment2 = 0.999 * moment2[0] + 0.001 * grad_rows * grad_rows
    fix1 = 1.0 - 0.9**10
    fix2 = 1.0 - 0.999**10
    step_size = new_moment1 / fix1 / (jnp.sqrt(new_moment2 / fix2) + 1e-08)
    new_master = master[0] - 0.001 * step_size - 0.0001 * master[0]
    return (input_cot[None, :, None], new_master[None], new_moment1[None], new_moment2[None])


def solution(mesh):
    return jax.shard_map(
        on_device,
        mesh=mesh,
        in_specs=(
            P("section", None, "tile", None, None, None),
            P("section", None, "tile", None, None, None),
            P("section", None, "tile", None, None, None),
            P(None, "tile", None, None, None),
            P("section", None),
            P("section", "tile", None),
            P("section", "tile", None),
            P("section", "tile", None),
        ),
        out_specs=(
            P("section", None, "tile", None, None, None),
            P("section", "tile", None),
            P("section", "tile", None),
            P("section", "tile", None),
        ),
        check_vma=False,
    )
```

```python
import functools

import jax
import jax.numpy as jnp
from jax import lax
from jax.experimental import pallas as pl
from jax.experimental.pallas import tpu as pltpu
from jax.sharding import PartitionSpec as P

TILE_ROWS = 4
BF = jnp.bfloat16
F32 = jnp.float32
SIDE = 8
LEAD = 16


def params(mib):
    return pltpu.CompilerParams(vmem_limit_bytes=mib << 20)


def chunks(size, most):
    units = size // 16
    count = -(-units * 16 // most)
    out, at = [], 0
    for i in range(count):
        end = units * (i + 1) // count
        out.append((at * 16, (end - at) * 16))
        at = end
    return out


def in_vmem(shape, dtype):
    return pltpu.VMEM(shape, dtype)


def sigmoid(x):
    return 0.5 * jnp.tanh(0.5 * x) + 0.5


def gates_kernel(pitch, width, deep, gap, at_row, at_side, ids_ref, mid_ref, above_ref, below_ref, left_ref, right_ref, mask_ref, kernel_ref, bias_ref, fac_ref, zs_ref, own_ref, flat_ref, z_ref):
    depth = 6 * width
    rows = mid_ref.shape[0]
    cols = pitch - 2 * SIDE
    tall = rows + 2 * deep
    size_e = zs_ref.shape[0]
    begin = gap * pitch
    stop = begin + LEAD + tall * pitch
    if gap:
        for lo, hi in ((0, begin), (stop, size_e)):
            z_ref[8 + lo : 8 + hi, :] = jnp.zeros((hi - lo, 2 * width), F32)
            flat_ref[lo:hi, :] = jnp.zeros((hi - lo, 2 * width), BF)
    z_ref[0:8, :] = jnp.zeros((8, 2 * width), F32)
    z_ref[8 + size_e :, :] = jnp.zeros((8, 2 * width), F32)

    def put(at, value):
        size = value.shape[0]
        z_ref[8 + at : 8 + at + size, :] = value[:, : 2 * width].astype(F32)
        flat_ref[at : at + size, :] = value[:, 2 * width :]

    none = jnp.zeros((SIDE, 4 * width), BF)
    for row in range(tall + 1):
        before = none if row == 0 else right_ref[at_side + row - 1]
        after = none if row == tall else left_ref[at_side + row]
        put(begin + row * pitch, jnp.concatenate([before, after], 0))
    for row in range(tall):
        at = begin + LEAD + row * pitch
        if row < deep:
            put(at, above_ref[at_row + row])
        elif row < deep + rows:
            put(at, mid_ref[row - deep])
        else:
            put(at, below_ref[at_row + row - deep - rows])
    for start, size in chunks(size_e, 256):
        here = pl.ds(start, size)
        own_ref[here, :] = flat_ref[here, width:]
        for b in range(3):
            zs_ref[here, b * 2 * width : (b + 1) * 2 * width] = z_ref[
                7 + b + start : 7 + b + start + size, :
            ].astype(BF)
    cells = fac_ref.shape[0] - 2 * begin
    for start, size in chunks(cells, 480):
        start = start + begin
        total = bias_ref[...]
        for a in range(3):
            total = total + jnp.dot(
                zs_ref[pl.ds(start + a * pitch, size), :],
                kernel_ref[a * depth : (a + 1) * depth, :],
                preferred_element_type=F32,
            )
        here = pl.ds(start, size)
        mask = mask_ref[here, :].astype(F32)
        c_prev = flat_ref[pl.ds(start + pitch, size), :width].astype(F32)
        i = sigmoid(total[:, :width])
        f = sigmoid(total[:, width : 2 * width])
        g = jnp.tanh(total[:, 2 * width : 3 * width])
        o = sigmoid(total[:, 3 * width :])
        tc = jnp.tanh(f * c_prev + i * g)
        fac_ref[here, 0:width] = o * (1.0 - tc * tc)
        fac_ref[here, width : 2 * width] = mask * g * i * (1.0 - i)
        fac_ref[here, 2 * width : 3 * width] = mask * c_prev * f * (1.0 - f)
        fac_ref[here, 3 * width : 4 * width] = mask * i * (1.0 - g * g)
        fac_ref[here, 4 * width : 5 * width] = mask * tc * o * (1.0 - o)
        fac_ref[here, 5 * width : 6 * width] = f


def turn_kernel(kernel_ref, turned_ref):
    depth, ngate = kernel_ref.shape[0] // 3, kernel_ref.shape[1]
    for a in range(3):
        turned_ref[a * ngate : (a + 1) * ngate, :] = kernel_ref[a * depth : (a + 1) * depth, :].T


def step_kernel(step, group, layers, frames, pitch, rows, cols, width, *refs):
    ids_ref, kernel_t_ref = refs[0], refs[1]
    picks = picks_of(step, group, layers, frames)
    fac_refs = refs[2 : 2 + len(picks)]
    at = 2 + len(picks)
    tops = layers - 1 in group and step < frames
    own_ref = refs[at] if tops else None
    at += 1 if tops else 0
    has_inc, has_state, has_kept = needs_of(step, group, layers, frames)
    inc_refs = {}
    for f in picks:
        if frames - 1 - step + layers - f < layers:
            inc_refs[f] = refs[at]
            at += 1
    if has_state:
        dh_ref, dc_ref = refs[at : at + 2]
        at += 2
    if has_kept:
        at += 2
    dx_ref, dxi_ref, dgi_ref, dhn_ref, dcn_ref, d_ref, p_ref = refs[at:]
    margin = frames + layers - 1 - step
    size_d = LEAD + (rows + 2 * margin) * pitch
    size_z = LEAD + (rows + 2 * margin - 2) * pitch
    frame = ids_ref[0] - step
    ngate = 4 * width

    def point(fac_ref, top_frame, pick):
        start_frame = pick == frames - 1
        for start, size in chunks(size_d, 256):
            here = pl.ds(start, size)
            there = pl.ds(start + step * pitch, size)
            if tops and pick == top_frame:
                above = own_ref[pl.ds(start + (step + 1) * pitch, size), :].astype(F32)
            else:
                above = inc_refs[pick][here, :].astype(F32)
            dh = above
            if not start_frame:
                dh = dh + dh_ref[here, :]
            dc = dh * fac_ref[there, 0:width]
            if not start_frame:
                dc = dc + dc_ref[here, :]
            d_ref[here, 0:width] = (dc * fac_ref[there, width : 2 * width]).astype(BF)
            d_ref[here, width : 2 * width] = (dc * fac_ref[there, 2 * width : 3 * width]).astype(BF)
            d_ref[here, 2 * width : 3 * width] = (dc * fac_ref[there, 3 * width : 4 * width]).astype(BF)
            d_ref[here, 3 * width :] = (dh * fac_ref[there, 4 * width : 5 * width]).astype(BF)
            lo, hi = max(start, pitch), min(start + size, pitch + size_z)
            if hi > lo:
                rec = dc * fac_ref[there, 5 * width :]
                dcn_ref[lo - pitch : hi - pitch, :] = rec[lo - start : hi - start, :]

    top_frame = frames - 1 - step
    for number, pick in enumerate(picks):
        pl.when(frame == pick)(functools.partial(point, fac_refs[number], top_frame, pick))

    active = (frame >= picks[0]) & (frame <= picks[-1])

    @pl.when(active)
    def _():
        slot = pl.multiple_of(frame * (rows * cols), rows * cols)
        for row in range(rows):
            dgi_ref[pl.ds(slot + row * cols, cols), :] = d_ref[
                pl.ds(LEAD + (row + margin) * pitch, cols), :
            ]
        p_ref[0:8, :] = jnp.zeros((8, 6 * width), F32)
        p_ref[8 + size_z : 16 + size_z, :] = jnp.zeros((8, 6 * width), F32)
        for start, size in chunks(size_z, 448):
            total = None
            for a in range(3):
                part = jnp.dot(
                    d_ref[pl.ds(start + (2 - a) * pitch, size), :],
                    kernel_t_ref[a * ngate : (a + 1) * ngate, :],
                    preferred_element_type=F32,
                )
                total = part if total is None else total + part
            p_ref[pl.ds(8 + start, size), :] = total
        for start, size in chunks(size_z, 256):
            dz = (
                p_ref[pl.ds(8 + start, size), 2 * width : 4 * width]
                + p_ref[pl.ds(9 + start, size), 0 : 2 * width]
                + p_ref[pl.ds(7 + start, size), 4 * width :]
            )
            dx_ref[pl.ds(start, size), :] = dz[:, :width].astype(BF)
            dhn_ref[pl.ds(start, size), :] = dz[:, width:]
        for row in range(rows):
            dxi_ref[pl.ds(slot + row * cols, cols), :] = dx_ref[
                pl.ds(LEAD + (row + margin - 1) * pitch, cols), :
            ]


def picks_of(step, group, layers, frames):
    now = [frames - 1 - step + layers - 1 - layer for layer in group]
    return sorted(f for f in now if 0 <= f < frames)


def needs_of(step, group, layers, frames):
    has_inc = any(
        0 <= frames - 1 - step + layers - 1 - layer < frames for layer in group if layer < layers - 1
    )
    has_state = any(f < frames - 1 for f in picks_of(step, group, layers, frames))
    return has_inc, has_state, step > 0


def patch_kernel(pitch, rows, cols, edge, zs_ref, pt_ref, flat_ref):
    depth = zs_ref.shape[1]
    for a in range(3):
        for row in range(rows):
            flat_ref[row * cols : (row + 1) * cols, :] = zs_ref[
                pl.ds(LEAD + (edge + row + a) * pitch, cols), :
            ]
        pt_ref[a * depth : (a + 1) * depth, :] = flat_ref[...].T


def grad_kernel(cells, frame, count, begin, end, *refs):
    pts, dg_ref = refs[:count], refs[count]
    total_ref = None if begin else refs[count + 1]
    out_ref = refs[-1]
    block = 256
    for at in range(0, out_ref.shape[0], block):
        here = pl.ds(at, block)
        total = None if begin else total_ref[here, :]
        part = jnp.dot(
            pts[0][here, :], dg_ref[frame * cells : (frame + 1) * cells, :], preferred_element_type=F32
        )
        total = part if begin else total + part
        out_ref[here, :] = total.astype(out_ref.dtype)


def spec_v():
    return pl.BlockSpec(memory_space=pltpu.VMEM)


def spec_s():
    return pl.BlockSpec(memory_space=pltpu.SMEM)


def place_kernel(at_ref, come_ref, out_ref):
    for j in range(out_ref.shape[0]):
        out_ref[at_ref[j]] = come_ref[j]


RING = 4


def on_ring(own, ntile):
    def move(x, by):
        pairs = [(i, i // 16 * 16 + (i // RING + by) % RING * RING + i % RING) for i in range(ntile)]
        return lax.ppermute(x, "tile", pairs)

    return jnp.stack([own] + [move(own, h) for h in (1, -1, 2)])


def all_rows(near, ntile, tile):
    members = ntile // RING
    groups = [
        [plane * 16 + z * RING + y for plane in range(members // RING) for y in range(RING)] for z in range(RING)
    ]
    come = lax.all_to_all(
        jnp.tile(near, (members, 1, 1)), "tile", 0, 0, axis_index_groups=groups, tiled=True
    )
    z = tile // RING % RING
    at = [
        plane * 16 + (z - h) % RING * RING + y
        for plane in range(members // RING)
        for y in range(RING)
        for h in (0, 1, -1, 2)
    ]
    return pl.pallas_call(
        place_kernel,
        out_shape=in_vmem(come.shape, BF),
        in_specs=[spec_s(), spec_v()],
        out_specs=spec_v(),
        compiler_params=params(16),
        cost_estimate=pl.CostEstimate(flops=0, bytes_accessed=4 << 20, transcendentals=0),
    )(jnp.stack(at).astype(jnp.int32), come)


def on_device(layer_input, hidden_prev, cell_prev, out_cot, bias, master, moment1, moment2):
    frames, rows, cols, width = (layer_input.shape[i] for i in (1, 3, 4, 5))
    ngate = 4 * width
    layers = lax.axis_size("section")
    layer = lax.axis_index("section")
    ntile = lax.axis_size("tile")
    tile = lax.axis_index("tile")
    ncols = ntile // TILE_ROWS
    pitch = cols + 2 * SIDE
    edge = frames + layers - 1

    near = on_ring(master[0].astype(BF), ntile)
    kernel = all_rows(near, ntile, tile).reshape(-1, ngate)

    ids = (frames - 1 + layers - 1 - layer).astype(jnp.int32).reshape(1)
    packed = jnp.concatenate(
        [layer_input[0, :, 0], hidden_prev[0, :, 0], cell_prev[0, :, 0].astype(BF), out_cot[:, 0]], -1
    )
    deeps = [edge + 1 - (frames - 1 - f) for f in range(frames)]
    grid_row, grid_col = tile // ncols, tile % ncols

    def around(by, strip, keep):
        got = lax.ppermute(strip, "tile", [(i, by(i)) for i in range(ntile)])
        return jnp.where(keep, got, jnp.zeros_like(got))

    margins = {}
    before = near
    for part in (tuple(range(frames)),):
        downs = jnp.concatenate([packed[f, rows - deeps[f] :] for f in part], 0)
        ups = jnp.concatenate([packed[f, : deeps[f]] for f in part], 0)
        downs, ups, _ = lax.optimization_barrier((downs, ups, before))
        above = around(lambda i: (i + ncols) % ntile, downs, grid_row > 0)
        below = around(lambda i: (i - ncols) % ntile, ups, grid_row < TILE_ROWS - 1)
        before = (above, below)
        talls, at = [], 0
        for f in part:
            talls.append(jnp.concatenate([above[at : at + deeps[f]], packed[f], below[at : at + deeps[f]]], 0))
            at += deeps[f]
        rights = jnp.concatenate([t[:, cols - SIDE :] for t in talls], 0)
        lefts = jnp.concatenate([t[:, :SIDE] for t in talls], 0)
        left = around(lambda i: i // ncols * ncols + (i + 1) % ncols, rights, grid_col > 0)
        right = around(lambda i: i // ncols * ncols + (i - 1) % ncols, lefts, grid_col < ncols - 1)
        for number, f in enumerate(part):
            ahead = part[:number]
            margins[f] = (
                (above, below, left, right),
                sum(deeps[g] for g in ahead),
                sum(rows + 2 * deeps[g] for g in ahead),
            )

    size_e = LEAD + (rows + 2 * edge + 2) * pitch
    size_d = LEAD + (rows + 2 * edge) * pitch
    cells = rows * cols

    at = jnp.arange(size_d, dtype=jnp.int32) - LEAD + SIDE
    row_at = at // pitch - edge + grid_row * rows
    col_at = at % pitch - SIDE + grid_col * cols
    inside = (row_at >= 0) & (row_at < TILE_ROWS * rows) & (col_at >= 0) & (col_at < ncols * cols)
    mask = jnp.broadcast_to(inside[:, None], (size_d, width)).astype(BF)

    facs, pts, owns = [None] * frames, [None] * frames, [None] * frames
    for f in reversed(range(frames)):
        gap = edge + 1 - deeps[f]
        strips, at_row, at_side = margins[f]
        facs[f], zs, owns[f] = pl.pallas_call(
            functools.partial(
                gates_kernel, pitch, width, deeps[f], gap, at_row, at_side
            ),
            out_shape=(
                in_vmem((size_d, 6 * width), F32),
                in_vmem((size_e, 6 * width), BF),
                in_vmem((size_e, width), BF),
            ),
            in_specs=[spec_s()] + [spec_v()] * 8,
            out_specs=(spec_v(),) * 3,
            scratch_shapes=[pltpu.VMEM((size_e, 2 * width), BF), pltpu.VMEM((size_e + 16, 2 * width), F32)],
            compiler_params=params(20),
            cost_estimate=pl.CostEstimate(
                flops=2 * size_d * 18 * width * ngate, bytes_accessed=10 << 20, transcendentals=size_d * 5 * width
            ),
        )(ids, packed[f], *strips, mask, kernel, bias)
        pts[f] = pl.pallas_call(
            functools.partial(patch_kernel, pitch, rows, cols, edge),
            out_shape=in_vmem((18 * width, cells), BF),
            in_specs=[spec_v()],
            out_specs=spec_v(),
            scratch_shapes=[pltpu.VMEM((cells, 6 * width), BF)],
            compiler_params=params(16),
            cost_estimate=pl.CostEstimate(flops=0, bytes_accessed=8 << 20, transcendentals=0),
        )(zs)
    kernel_t = pl.pallas_call(
        turn_kernel,
        out_shape=in_vmem((3 * ngate, 6 * width), BF),
        in_specs=[spec_v()],
        out_specs=spec_v(),
        compiler_params=params(16),
        cost_estimate=pl.CostEstimate(flops=0, bytes_accessed=4 << 20, transcendentals=0),
    )(kernel)

    steps = layers + frames - 1
    upper, lower = tuple(range(layers // 2, layers)), tuple(range(layers // 2))
    states = {upper: None, lower: None}
    sent = {}
    kept = None
    total = None
    for step in range(steps):
        margin = edge - step
        size_z = LEAD + (rows + 2 * margin - 2) * pitch
        fresh = {}
        for group in (upper, lower):
            picks = picks_of(step, group, layers, frames)
            if not picks:
                continue
            has_inc, has_state, has_kept = needs_of(step, group, layers, frames)
            args = [ids, kernel_t] + [facs[f] for f in picks]
            if layers - 1 in group and step < frames:
                args.append(owns[frames - 1 - step])
            if has_inc:
                above_of = [frames - 1 - step + layers - f for f in picks]
                args += [sent[i] for i in above_of if i < layers]
            if has_state:
                args += list(states[group])
            if has_kept:
                args += list(kept)
            dx, cots, dgates, dh_rec, dc_rec = pl.pallas_call(
                functools.partial(step_kernel, step, group, layers, frames, pitch, rows, cols, width),
                out_shape=(
                    jax.ShapeDtypeStruct((size_z, width), BF),
                    in_vmem((frames * cells, width), BF),
                    in_vmem((frames * cells, ngate), BF),
                    in_vmem((size_z, width), F32),
                    in_vmem((size_z, width), F32),
                ),
                in_specs=[spec_s()] + [spec_v()] * (len(args) - 1),
                out_specs=(spec_v(),) * 5,
                scratch_shapes=[
                    pltpu.VMEM((size_z + 2 * pitch, ngate), BF),
                    pltpu.VMEM((size_z + 16, 6 * width), F32),
                ],
                input_output_aliases={len(args) - 2: 1, len(args) - 1: 2} if has_kept else {},
                compiler_params=params(20),
                cost_estimate=pl.CostEstimate(
                    flops=2 * size_z * 18 * width * ngate, bytes_accessed=10 << 20, transcendentals=0
                ),
            )(*args)
            kept = (cots, dgates)
            states[group] = (dh_rec, dc_rec)
            for i in group:
                if i > 0 and 0 <= frames - 1 - step + layers - 1 - i < frames:
                    fresh[i] = lax.ppermute(dx, "section", [(i, i - 1)])
        sent = fresh
        if step >= layers - 1:
            f = frames - 1 - (step - layers + 1)
            end = step == steps - 1
            args = [pts[f], kept[1]] + ([] if total is None else [total])
            total = pl.pallas_call(
                functools.partial(grad_kernel, cells, f, 1, total is None, end),
                out_shape=in_vmem((18 * width, ngate), BF if end else F32),
                in_specs=[spec_v()] * len(args),
                out_specs=spec_v(),
                compiler_params=params(16),
                cost_estimate=pl.CostEstimate(
                    flops=2 * cells * 18 * width * ngate, bytes_accessed=4 << 20, transcendentals=0
                ),
            )(*args)
    cots = kept[0]
    total, cots = lax.optimization_barrier((total, cots))
    arrived = lax.all_to_all(total, "tile", 0, 0, tiled=True)
    arrived, cots = lax.optimization_barrier((arrived, cots))
    input_cot = cots.reshape(frames, rows, cols, width)
    grad_rows = jnp.sum(arrived.reshape(ntile, -1, ngate).astype(F32), 0)
    new_moment1 = 0.9 * moment1[0] + 0.1 * grad_rows
    new_moment2 = 0.999 * moment2[0] + 0.001 * grad_rows * grad_rows
    fix1 = 1.0 - 0.9**10
    fix2 = 1.0 - 0.999**10
    step_size = new_moment1 / fix1 / (jnp.sqrt(new_moment2 / fix2) + 1e-08)
    new_master = master[0] - 0.001 * step_size - 0.0001 * master[0]
    return (input_cot[None, :, None], new_master[None], new_moment1[None], new_moment2[None])


def solution(mesh):
    return jax.shard_map(
        on_device,
        mesh=mesh,
        in_specs=(
            P("section", None, "tile", None, None, None),
            P("section", None, "tile", None, None, None),
            P("section", None, "tile", None, None, None),
            P(None, "tile", None, None, None),
            P("section", None),
            P("section", "tile", None),
            P("section", "tile", None),
            P("section", "tile", None),
        ),
        out_specs=(
            P("section", None, "tile", None, None, None),
            P("section", "tile", None),
            P("section", "tile", None),
            P("section", "tile", None),
        ),
        check_vma=False,
    )
```

```python
import functools

import jax
import jax.numpy as jnp
from jax import lax
from jax.experimental import pallas as pl
from jax.experimental.pallas import tpu as pltpu
from jax.sharding import PartitionSpec as P

TILE_ROWS = 4
BF = jnp.bfloat16
F32 = jnp.float32
SIDE = 8
LEAD = 16


def params(mib):
    return pltpu.CompilerParams(vmem_limit_bytes=mib << 20)


def chunks(size, most):
    units = size // 16
    count = -(-units * 16 // most)
    out, at = [], 0
    for i in range(count):
        end = units * (i + 1) // count
        out.append((at * 16, (end - at) * 16))
        at = end
    return out


def in_vmem(shape, dtype):
    return pltpu.VMEM(shape, dtype)


def sigmoid(x):
    return 0.5 * jnp.tanh(0.5 * x) + 0.5


def gates_kernel(pitch, width, deep, gap, at_row, at_side, ids_ref, mid_ref, above_ref, below_ref, left_ref, right_ref, mask_ref, kernel_ref, bias_ref, fac_ref, zs_ref, own_ref, flat_ref, z_ref):
    depth = 6 * width
    rows = mid_ref.shape[0]
    cols = pitch - 2 * SIDE
    tall = rows + 2 * deep
    size_e = zs_ref.shape[0]
    begin = gap * pitch
    stop = begin + LEAD + tall * pitch
    if gap:
        for lo, hi in ((0, begin), (stop, size_e)):
            z_ref[8 + lo : 8 + hi, :] = jnp.zeros((hi - lo, 2 * width), F32)
            flat_ref[lo:hi, :] = jnp.zeros((hi - lo, 2 * width), BF)
    z_ref[0:8, :] = jnp.zeros((8, 2 * width), F32)
    z_ref[8 + size_e :, :] = jnp.zeros((8, 2 * width), F32)

    def put(at, value):
        size = value.shape[0]
        z_ref[8 + at : 8 + at + size, :] = value[:, : 2 * width].astype(F32)
        flat_ref[at : at + size, :] = value[:, 2 * width :]

    up, down, left, right = (ids_ref[1 + j].astype(F32) for j in range(4))

    def kept(value, *flags):
        value = value.astype(F32)
        for flag in flags:
            value = value * flag
        return value.astype(BF)

    def beside(ref, row, flag):
        if row < 0 or row >= tall:
            return jnp.zeros((SIDE, 4 * width), BF)
        flags = (flag, up) if row < deep else (flag, down) if row >= deep + rows else (flag,)
        return kept(ref[at_side + row], *flags)

    for row in range(tall + 1):
        put(begin + row * pitch, jnp.concatenate([beside(right_ref, row - 1, right), beside(left_ref, row, left)], 0))
    for row in range(tall):
        at = begin + LEAD + row * pitch
        if row < deep:
            put(at, kept(above_ref[at_row + row], up))
        elif row < deep + rows:
            put(at, mid_ref[row - deep])
        else:
            put(at, kept(below_ref[at_row + row - deep - rows], down))
    for start, size in chunks(size_e, 256):
        here = pl.ds(start, size)
        own_ref[here, :] = flat_ref[here, width:]
        for b in range(3):
            zs_ref[here, b * 2 * width : (b + 1) * 2 * width] = z_ref[
                7 + b + start : 7 + b + start + size, :
            ].astype(BF)
    cells = fac_ref.shape[0] - 2 * begin
    for start, size in chunks(cells, 480):
        start = start + begin
        total = bias_ref[...]
        for a in range(3):
            total = total + jnp.dot(
                zs_ref[pl.ds(start + a * pitch, size), :],
                kernel_ref[a * depth : (a + 1) * depth, :],
                preferred_element_type=F32,
            )
        here = pl.ds(start, size)
        mask = mask_ref[here, :].astype(F32)
        c_prev = flat_ref[pl.ds(start + pitch, size), :width].astype(F32)
        i = sigmoid(total[:, :width])
        f = sigmoid(total[:, width : 2 * width])
        g = jnp.tanh(total[:, 2 * width : 3 * width])
        o = sigmoid(total[:, 3 * width :])
        tc = jnp.tanh(f * c_prev + i * g)
        fac_ref[here, 0:width] = o * (1.0 - tc * tc)
        fac_ref[here, width : 2 * width] = mask * g * i * (1.0 - i)
        fac_ref[here, 2 * width : 3 * width] = mask * c_prev * f * (1.0 - f)
        fac_ref[here, 3 * width : 4 * width] = mask * i * (1.0 - g * g)
        fac_ref[here, 4 * width : 5 * width] = mask * tc * o * (1.0 - o)
        fac_ref[here, 5 * width : 6 * width] = f


def turn_kernel(kernel_ref, turned_ref):
    depth, ngate = kernel_ref.shape[0] // 3, kernel_ref.shape[1]
    for a in range(3):
        turned_ref[a * ngate : (a + 1) * ngate, :] = kernel_ref[a * depth : (a + 1) * depth, :].T


def step_kernel(step, group, layers, frames, pitch, rows, cols, width, *refs):
    ids_ref, kernel_t_ref = refs[0], refs[1]
    picks = picks_of(step, group, layers, frames)
    fac_refs = refs[2 : 2 + len(picks)]
    at = 2 + len(picks)
    tops = layers - 1 in group and step < frames
    own_ref = refs[at] if tops else None
    at += 1 if tops else 0
    has_inc, has_state, has_kept = needs_of(step, group, layers, frames)
    inc_refs = {}
    for f in picks:
        if frames - 1 - step + layers - f < layers:
            inc_refs[f] = refs[at]
            at += 1
    if has_state:
        dh_ref, dc_ref = refs[at : at + 2]
        at += 2
    if has_kept:
        at += 2
    dx_ref, dxi_ref, dgi_ref, dhn_ref, dcn_ref, d_ref, p_ref = refs[at:]
    margin = frames + layers - 1 - step
    size_d = LEAD + (rows + 2 * margin) * pitch
    size_z = LEAD + (rows + 2 * margin - 2) * pitch
    frame = ids_ref[0] - step
    ngate = 4 * width

    def point(fac_ref, top_frame, pick):
        start_frame = pick == frames - 1
        for start, size in chunks(size_d, 256):
            here = pl.ds(start, size)
            there = pl.ds(start + step * pitch, size)
            if tops and pick == top_frame:
                above = own_ref[pl.ds(start + (step + 1) * pitch, size), :].astype(F32)
            else:
                above = inc_refs[pick][here, :].astype(F32)
            dh = above
            if not start_frame:
                dh = dh + dh_ref[here, :]
            dc = dh * fac_ref[there, 0:width]
            if not start_frame:
                dc = dc + dc_ref[here, :]
            d_ref[here, 0:width] = (dc * fac_ref[there, width : 2 * width]).astype(BF)
            d_ref[here, width : 2 * width] = (dc * fac_ref[there, 2 * width : 3 * width]).astype(BF)
            d_ref[here, 2 * width : 3 * width] = (dc * fac_ref[there, 3 * width : 4 * width]).astype(BF)
            d_ref[here, 3 * width :] = (dh * fac_ref[there, 4 * width : 5 * width]).astype(BF)
            lo, hi = max(start, pitch), min(start + size, pitch + size_z)
            if hi > lo:
                rec = dc * fac_ref[there, 5 * width :]
                dcn_ref[lo - pitch : hi - pitch, :] = rec[lo - start : hi - start, :]

    top_frame = frames - 1 - step
    for number, pick in enumerate(picks):
        pl.when(frame == pick)(functools.partial(point, fac_refs[number], top_frame, pick))

    active = (frame >= picks[0]) & (frame <= picks[-1])

    @pl.when(active)
    def _():
        slot = pl.multiple_of(frame * (rows * cols), rows * cols)
        for row in range(rows):
            dgi_ref[pl.ds(slot + row * cols, cols), :] = d_ref[
                pl.ds(LEAD + (row + margin) * pitch, cols), :
            ]
        p_ref[0:8, :] = jnp.zeros((8, 6 * width), F32)
        p_ref[8 + size_z : 16 + size_z, :] = jnp.zeros((8, 6 * width), F32)
        for start, size in chunks(size_z, 448):
            total = None
            for a in range(3):
                part = jnp.dot(
                    d_ref[pl.ds(start + (2 - a) * pitch, size), :],
                    kernel_t_ref[a * ngate : (a + 1) * ngate, :],
                    preferred_element_type=F32,
                )
                total = part if total is None else total + part
            p_ref[pl.ds(8 + start, size), :] = total
        for start, size in chunks(size_z, 256):
            dz = (
                p_ref[pl.ds(8 + start, size), 2 * width : 4 * width]
                + p_ref[pl.ds(9 + start, size), 0 : 2 * width]
                + p_ref[pl.ds(7 + start, size), 4 * width :]
            )
            dx_ref[pl.ds(start, size), :] = dz[:, :width].astype(BF)
            dhn_ref[pl.ds(start, size), :] = dz[:, width:]
        for row in range(rows):
            dxi_ref[pl.ds(slot + row * cols, cols), :] = dx_ref[
                pl.ds(LEAD + (row + margin - 1) * pitch, cols), :
            ]


def picks_of(step, group, layers, frames):
    now = [frames - 1 - step + layers - 1 - layer for layer in group]
    return sorted(f for f in now if 0 <= f < frames)


def needs_of(step, group, layers, frames):
    has_inc = any(
        0 <= frames - 1 - step + layers - 1 - layer < frames for layer in group if layer < layers - 1
    )
    has_state = any(f < frames - 1 for f in picks_of(step, group, layers, frames))
    return has_inc, has_state, step > 0


def patch_kernel(pitch, rows, cols, edge, zs_ref, pt_ref, flat_ref):
    depth = zs_ref.shape[1]
    for a in range(3):
        for row in range(rows):
            flat_ref[row * cols : (row + 1) * cols, :] = zs_ref[
                pl.ds(LEAD + (edge + row + a) * pitch, cols), :
            ]
        pt_ref[a * depth : (a + 1) * depth, :] = flat_ref[...].T


def grad_kernel(cells, frame, count, begin, end, *refs):
    pts, dg_ref = refs[:count], refs[count]
    total_ref = None if begin else refs[count + 1]
    out_ref = refs[-1]
    block = 256
    for at in range(0, out_ref.shape[0], block):
        here = pl.ds(at, block)
        total = None if begin else total_ref[here, :]
        part = jnp.dot(
            pts[0][here, :], dg_ref[frame * cells : (frame + 1) * cells, :], preferred_element_type=F32
        )
        total = part if begin else total + part
        out_ref[here, :] = total.astype(out_ref.dtype)


def spec_v():
    return pl.BlockSpec(memory_space=pltpu.VMEM)


def spec_s():
    return pl.BlockSpec(memory_space=pltpu.SMEM)


def place_kernel(at_ref, come_ref, out_ref):
    for j in range(out_ref.shape[0]):
        out_ref[at_ref[j]] = come_ref[j]


RING = 4


def on_ring(own, ntile):
    def move(x, by):
        pairs = [(i, i // 16 * 16 + (i // RING + by) % RING * RING + i % RING) for i in range(ntile)]
        return lax.ppermute(x, "tile", pairs)

    return jnp.stack([own] + [move(own, h) for h in (1, -1, 2)])


def all_rows(near, ntile, tile):
    members = ntile // RING
    groups = [
        [plane * 16 + z * RING + y for plane in range(members // RING) for y in range(RING)] for z in range(RING)
    ]
    come = lax.all_to_all(
        jnp.tile(near, (members, 1, 1)), "tile", 0, 0, axis_index_groups=groups, tiled=True
    )
    z = tile // RING % RING
    at = [
        plane * 16 + (z - h) % RING * RING + y
        for plane in range(members // RING)
        for y in range(RING)
        for h in (0, 1, -1, 2)
    ]
    return pl.pallas_call(
        place_kernel,
        out_shape=in_vmem(come.shape, BF),
        in_specs=[spec_s(), spec_v()],
        out_specs=spec_v(),
        compiler_params=params(16),
        cost_estimate=pl.CostEstimate(flops=0, bytes_accessed=4 << 20, transcendentals=0),
    )(jnp.stack(at).astype(jnp.int32), come)


def on_device(layer_input, hidden_prev, cell_prev, out_cot, bias, master, moment1, moment2):
    frames, rows, cols, width = (layer_input.shape[i] for i in (1, 3, 4, 5))
    ngate = 4 * width
    layers = lax.axis_size("section")
    layer = lax.axis_index("section")
    ntile = lax.axis_size("tile")
    tile = lax.axis_index("tile")
    ncols = ntile // TILE_ROWS
    pitch = cols + 2 * SIDE
    edge = frames + layers - 1

    near = on_ring(master[0].astype(BF), ntile)
    kernel = all_rows(near, ntile, tile).reshape(-1, ngate)

    packed = jnp.concatenate(
        [layer_input[0, :, 0], hidden_prev[0, :, 0], cell_prev[0, :, 0].astype(BF), out_cot[:, 0]], -1
    )
    deeps = [edge + 1 - (frames - 1 - f) for f in range(frames)]
    grid_row, grid_col = tile // ncols, tile % ncols
    ids = jnp.stack(
        [
            frames - 1 + layers - 1 - layer,
            grid_row > 0,
            grid_row < TILE_ROWS - 1,
            grid_col > 0,
            grid_col < ncols - 1,
        ]
    ).astype(jnp.int32)

    def around(by, strip):
        return lax.ppermute(strip, "tile", [(i, by(i)) for i in range(ntile)])

    margins = {}
    for part in ((frames - 1,), tuple(range(frames - 1))):
        downs = jnp.concatenate([packed[f, rows - deeps[f] :] for f in part], 0)
        ups = jnp.concatenate([packed[f, : deeps[f]] for f in part], 0)
        downs, ups, _ = lax.optimization_barrier((downs, ups, near))
        above = around(lambda i: (i + ncols) % ntile, downs)
        below = around(lambda i: (i - ncols) % ntile, ups)
        talls, at = [], 0
        for f in part:
            talls.append(jnp.concatenate([above[at : at + deeps[f]], packed[f], below[at : at + deeps[f]]], 0))
            at += deeps[f]
        rights = jnp.concatenate([t[:, cols - SIDE :] for t in talls], 0)
        lefts = jnp.concatenate([t[:, :SIDE] for t in talls], 0)
        left = around(lambda i: i // ncols * ncols + (i + 1) % ncols, rights)
        right = around(lambda i: i // ncols * ncols + (i - 1) % ncols, lefts)
        for number, f in enumerate(part):
            ahead = part[:number]
            margins[f] = (
                (above, below, left, right),
                sum(deeps[g] for g in ahead),
                sum(rows + 2 * deeps[g] for g in ahead),
            )

    size_e = LEAD + (rows + 2 * edge + 2) * pitch
    size_d = LEAD + (rows + 2 * edge) * pitch
    cells = rows * cols

    at = jnp.arange(size_d, dtype=jnp.int32) - LEAD + SIDE
    row_at = at // pitch - edge + grid_row * rows
    col_at = at % pitch - SIDE + grid_col * cols
    inside = (row_at >= 0) & (row_at < TILE_ROWS * rows) & (col_at >= 0) & (col_at < ncols * cols)
    mask = jnp.broadcast_to(inside[:, None], (size_d, width)).astype(BF)

    facs, pts, owns = [None] * frames, [None] * frames, [None] * frames
    for f in reversed(range(frames)):
        gap = edge + 1 - deeps[f]
        strips, at_row, at_side = margins[f]
        facs[f], zs, owns[f] = pl.pallas_call(
            functools.partial(
                gates_kernel, pitch, width, deeps[f], gap, at_row, at_side
            ),
            out_shape=(
                in_vmem((size_d, 6 * width), F32),
                in_vmem((size_e, 6 * width), BF),
                in_vmem((size_e, width), BF),
            ),
            in_specs=[spec_s()] + [spec_v()] * 8,
            out_specs=(spec_v(),) * 3,
            scratch_shapes=[pltpu.VMEM((size_e, 2 * width), BF), pltpu.VMEM((size_e + 16, 2 * width), F32)],
            compiler_params=params(20),
            cost_estimate=pl.CostEstimate(
                flops=2 * size_d * 18 * width * ngate, bytes_accessed=10 << 20, transcendentals=size_d * 5 * width
            ),
        )(ids, packed[f], *strips, mask, kernel, bias)
        pts[f] = pl.pallas_call(
            functools.partial(patch_kernel, pitch, rows, cols, edge),
            out_shape=in_vmem((18 * width, cells), BF),
            in_specs=[spec_v()],
            out_specs=spec_v(),
            scratch_shapes=[pltpu.VMEM((cells, 6 * width), BF)],
            compiler_params=params(16),
            cost_estimate=pl.CostEstimate(flops=0, bytes_accessed=8 << 20, transcendentals=0),
        )(zs)
    kernel_t = pl.pallas_call(
        turn_kernel,
        out_shape=in_vmem((3 * ngate, 6 * width), BF),
        in_specs=[spec_v()],
        out_specs=spec_v(),
        compiler_params=params(16),
        cost_estimate=pl.CostEstimate(flops=0, bytes_accessed=4 << 20, transcendentals=0),
    )(kernel)

    steps = layers + frames - 1
    upper, lower = tuple(range(layers // 2, layers)), tuple(range(layers // 2))
    states = {upper: None, lower: None}
    sent = {}
    kept = None
    total = None
    for step in range(steps):
        margin = edge - step
        size_z = LEAD + (rows + 2 * margin - 2) * pitch
        fresh = {}
        for group in (upper, lower):
            picks = picks_of(step, group, layers, frames)
            if not picks:
                continue
            has_inc, has_state, has_kept = needs_of(step, group, layers, frames)
            args = [ids, kernel_t] + [facs[f] for f in picks]
            if layers - 1 in group and step < frames:
                args.append(owns[frames - 1 - step])
            if has_inc:
                above_of = [frames - 1 - step + layers - f for f in picks]
                args += [sent[i] for i in above_of if i < layers]
            if has_state:
                args += list(states[group])
            if has_kept:
                args += list(kept)
            dx, cots, dgates, dh_rec, dc_rec = pl.pallas_call(
                functools.partial(step_kernel, step, group, layers, frames, pitch, rows, cols, width),
                out_shape=(
                    jax.ShapeDtypeStruct((size_z, width), BF),
                    in_vmem((frames * cells, width), BF),
                    in_vmem((frames * cells, ngate), BF),
                    in_vmem((size_z, width), F32),
                    in_vmem((size_z, width), F32),
                ),
                in_specs=[spec_s()] + [spec_v()] * (len(args) - 1),
                out_specs=(spec_v(),) * 5,
                scratch_shapes=[
                    pltpu.VMEM((size_z + 2 * pitch, ngate), BF),
                    pltpu.VMEM((size_z + 16, 6 * width), F32),
                ],
                input_output_aliases={len(args) - 2: 1, len(args) - 1: 2} if has_kept else {},
                compiler_params=params(20),
                cost_estimate=pl.CostEstimate(
                    flops=2 * size_z * 18 * width * ngate, bytes_accessed=10 << 20, transcendentals=0
                ),
            )(*args)
            kept = (cots, dgates)
            states[group] = (dh_rec, dc_rec)
            for i in group:
                if i > 0 and 0 <= frames - 1 - step + layers - 1 - i < frames:
                    fresh[i] = lax.ppermute(dx, "section", [(i, i - 1)])
        sent = fresh
        if step >= layers - 1:
            f = frames - 1 - (step - layers + 1)
            end = step == steps - 1
            args = [pts[f], kept[1]] + ([] if total is None else [total])
            total = pl.pallas_call(
                functools.partial(grad_kernel, cells, f, 1, total is None, end),
                out_shape=in_vmem((18 * width, ngate), BF if end else F32),
                in_specs=[spec_v()] * len(args),
                out_specs=spec_v(),
                compiler_params=params(16),
                cost_estimate=pl.CostEstimate(
                    flops=2 * cells * 18 * width * ngate, bytes_accessed=4 << 20, transcendentals=0
                ),
            )(*args)
    cots = kept[0]
    total, cots = lax.optimization_barrier((total, cots))
    arrived = lax.all_to_all(total, "tile", 0, 0, tiled=True)
    arrived, cots = lax.optimization_barrier((arrived, cots))
    input_cot = cots.reshape(frames, rows, cols, width)
    grad_rows = jnp.sum(arrived.reshape(ntile, -1, ngate).astype(F32), 0)
    new_moment1 = 0.9 * moment1[0] + 0.1 * grad_rows
    new_moment2 = 0.999 * moment2[0] + 0.001 * grad_rows * grad_rows
    fix1 = 1.0 - 0.9**10
    fix2 = 1.0 - 0.999**10
    step_size = new_moment1 / fix1 / (jnp.sqrt(new_moment2 / fix2) + 1e-08)
    new_master = master[0] - 0.001 * step_size - 0.0001 * master[0]
    return (input_cot[None, :, None], new_master[None], new_moment1[None], new_moment2[None])


def solution(mesh):
    return jax.shard_map(
        on_device,
        mesh=mesh,
        in_specs=(
            P("section", None, "tile", None, None, None),
            P("section", None, "tile", None, None, None),
            P("section", None, "tile", None, None, None),
            P(None, "tile", None, None, None),
            P("section", None),
            P("section", "tile", None),
            P("section", "tile", None),
            P("section", "tile", None),
        ),
        out_specs=(
            P("section", None, "tile", None, None, None),
            P("section", "tile", None),
            P("section", "tile", None),
            P("section", "tile", None),
        ),
        check_vma=False,
    )
```

```python
import functools

import jax
import jax.numpy as jnp
from jax import lax
from jax.experimental import pallas as pl
from jax.experimental.pallas import tpu as pltpu
from jax.sharding import PartitionSpec as P

TILE_ROWS = 4
BF = jnp.bfloat16
F32 = jnp.float32
SIDE = 8
LEAD = 16


def params(mib):
    return pltpu.CompilerParams(vmem_limit_bytes=mib << 20)


def chunks(size, most):
    units = size // 16
    count = -(-units * 16 // most)
    out, at = [], 0
    for i in range(count):
        end = units * (i + 1) // count
        out.append((at * 16, (end - at) * 16))
        at = end
    return out


def in_vmem(shape, dtype):
    return pltpu.VMEM(shape, dtype)


def sigmoid(x):
    return 0.5 * jnp.tanh(0.5 * x) + 0.5


def gates_kernel(pitch, width, deep, gap, at_row, at_side, ids_ref, mid_ref, above_ref, below_ref, left_ref, right_ref, mask_ref, kernel_ref, bias_ref, fac_ref, zs_ref, own_ref, flat_ref, z_ref):
    depth = 6 * width
    rows = mid_ref.shape[0]
    cols = pitch - 2 * SIDE
    tall = rows + 2 * deep
    size_e = zs_ref.shape[0]
    begin = gap * pitch
    stop = begin + LEAD + tall * pitch
    if gap:
        for lo, hi in ((0, begin), (stop, size_e)):
            z_ref[8 + lo : 8 + hi, :] = jnp.zeros((hi - lo, 2 * width), F32)
            flat_ref[lo:hi, :] = jnp.zeros((hi - lo, 2 * width), BF)
    z_ref[0:8, :] = jnp.zeros((8, 2 * width), F32)
    z_ref[8 + size_e :, :] = jnp.zeros((8, 2 * width), F32)

    def put(at, value):
        size = value.shape[0]
        z_ref[8 + at : 8 + at + size, :] = value[:, : 2 * width].astype(F32)
        flat_ref[at : at + size, :] = value[:, 2 * width :]

    def beside(ref, row):
        if row < 0 or row >= tall:
            return jnp.zeros((SIDE, 4 * width), BF)
        if row < deep:
            return ref[at_side[0] + row]
        if row < deep + rows:
            return ref[at_side[1] + row - deep]
        return ref[at_side[2] + row - deep - rows]

    for row in range(tall + 1):
        put(begin + row * pitch, jnp.concatenate([beside(right_ref, row - 1), beside(left_ref, row)], 0))
    for row in range(tall):
        at = begin + LEAD + row * pitch
        if row < deep:
            put(at, above_ref[at_row + row])
        elif row < deep + rows:
            put(at, mid_ref[row - deep])
        else:
            put(at, below_ref[at_row + row - deep - rows])
    for start, size in chunks(size_e, 256):
        here = pl.ds(start, size)
        own_ref[here, :] = flat_ref[here, width:]
        for b in range(3):
            zs_ref[here, b * 2 * width : (b + 1) * 2 * width] = z_ref[
                7 + b + start : 7 + b + start + size, :
            ].astype(BF)
    cells = fac_ref.shape[0] - 2 * begin
    for start, size in chunks(cells, 480):
        start = start + begin
        total = bias_ref[...]
        for a in range(3):
            total = total + jnp.dot(
                zs_ref[pl.ds(start + a * pitch, size), :],
                kernel_ref[a * depth : (a + 1) * depth, :],
                preferred_element_type=F32,
            )
        here = pl.ds(start, size)
        mask = mask_ref[here, :].astype(F32)
        c_prev = flat_ref[pl.ds(start + pitch, size), :width].astype(F32)
        i = sigmoid(total[:, :width])
        f = sigmoid(total[:, width : 2 * width])
        g = jnp.tanh(total[:, 2 * width : 3 * width])
        o = sigmoid(total[:, 3 * width :])
        tc = jnp.tanh(f * c_prev + i * g)
        fac_ref[here, 0:width] = o * (1.0 - tc * tc)
        fac_ref[here, width : 2 * width] = mask * g * i * (1.0 - i)
        fac_ref[here, 2 * width : 3 * width] = mask * c_prev * f * (1.0 - f)
        fac_ref[here, 3 * width : 4 * width] = mask * i * (1.0 - g * g)
        fac_ref[here, 4 * width : 5 * width] = mask * tc * o * (1.0 - o)
        fac_ref[here, 5 * width : 6 * width] = f


def turn_kernel(kernel_ref, turned_ref):
    depth, ngate = kernel_ref.shape[0] // 3, kernel_ref.shape[1]
    for a in range(3):
        turned_ref[a * ngate : (a + 1) * ngate, :] = kernel_ref[a * depth : (a + 1) * depth, :].T


def step_kernel(step, group, layers, frames, pitch, rows, cols, width, *refs):
    ids_ref, kernel_t_ref = refs[0], refs[1]
    picks = picks_of(step, group, layers, frames)
    fac_refs = refs[2 : 2 + len(picks)]
    at = 2 + len(picks)
    tops = layers - 1 in group and step < frames
    own_ref = refs[at] if tops else None
    at += 1 if tops else 0
    has_inc, has_state, has_kept = needs_of(step, group, layers, frames)
    inc_refs = {}
    for f in picks:
        if frames - 1 - step + layers - f < layers:
            inc_refs[f] = refs[at]
            at += 1
    if has_state:
        dh_ref, dc_ref = refs[at : at + 2]
        at += 2
    if has_kept:
        at += 2
    dx_ref, dxi_ref, dgi_ref, dhn_ref, dcn_ref, d_ref, p_ref = refs[at:]
    margin = frames + layers - 1 - step
    size_d = LEAD + (rows + 2 * margin) * pitch
    size_z = LEAD + (rows + 2 * margin - 2) * pitch
    frame = ids_ref[0] - step
    ngate = 4 * width

    def point(fac_ref, top_frame, pick):
        start_frame = pick == frames - 1
        for start, size in chunks(size_d, 256):
            here = pl.ds(start, size)
            there = pl.ds(start + step * pitch, size)
            if tops and pick == top_frame:
                above = own_ref[pl.ds(start + (step + 1) * pitch, size), :].astype(F32)
            else:
                above = inc_refs[pick][here, :].astype(F32)
            dh = above
            if not start_frame:
                dh = dh + dh_ref[here, :]
            dc = dh * fac_ref[there, 0:width]
            if not start_frame:
                dc = dc + dc_ref[here, :]
            d_ref[here, 0:width] = (dc * fac_ref[there, width : 2 * width]).astype(BF)
            d_ref[here, width : 2 * width] = (dc * fac_ref[there, 2 * width : 3 * width]).astype(BF)
            d_ref[here, 2 * width : 3 * width] = (dc * fac_ref[there, 3 * width : 4 * width]).astype(BF)
            d_ref[here, 3 * width :] = (dh * fac_ref[there, 4 * width : 5 * width]).astype(BF)
            lo, hi = max(start, pitch), min(start + size, pitch + size_z)
            if hi > lo:
                rec = dc * fac_ref[there, 5 * width :]
                dcn_ref[lo - pitch : hi - pitch, :] = rec[lo - start : hi - start, :]

    top_frame = frames - 1 - step
    for number, pick in enumerate(picks):
        pl.when(frame == pick)(functools.partial(point, fac_refs[number], top_frame, pick))

    active = (frame >= picks[0]) & (frame <= picks[-1])

    @pl.when(active)
    def _():
        slot = pl.multiple_of(frame * (rows * cols), rows * cols)
        for row in range(rows):
            dgi_ref[pl.ds(slot + row * cols, cols), :] = d_ref[
                pl.ds(LEAD + (row + margin) * pitch, cols), :
            ]
        p_ref[0:8, :] = jnp.zeros((8, 6 * width), F32)
        p_ref[8 + size_z : 16 + size_z, :] = jnp.zeros((8, 6 * width), F32)
        for start, size in chunks(size_z, 448):
            total = None
            for a in range(3):
                part = jnp.dot(
                    d_ref[pl.ds(start + (2 - a) * pitch, size), :],
                    kernel_t_ref[a * ngate : (a + 1) * ngate, :],
                    preferred_element_type=F32,
                )
                total = part if total is None else total + part
            p_ref[pl.ds(8 + start, size), :] = total
        for start, size in chunks(size_z, 256):
            dz = (
                p_ref[pl.ds(8 + start, size), 2 * width : 4 * width]
                + p_ref[pl.ds(9 + start, size), 0 : 2 * width]
                + p_ref[pl.ds(7 + start, size), 4 * width :]
            )
            dx_ref[pl.ds(start, size), :] = dz[:, :width].astype(BF)
            dhn_ref[pl.ds(start, size), :] = dz[:, width:]
        for row in range(rows):
            dxi_ref[pl.ds(slot + row * cols, cols), :] = dx_ref[
                pl.ds(LEAD + (row + margin - 1) * pitch, cols), :
            ]


def picks_of(step, group, layers, frames):
    now = [frames - 1 - step + layers - 1 - layer for layer in group]
    return sorted(f for f in now if 0 <= f < frames)


def needs_of(step, group, layers, frames):
    has_inc = any(
        0 <= frames - 1 - step + layers - 1 - layer < frames for layer in group if layer < layers - 1
    )
    has_state = any(f < frames - 1 for f in picks_of(step, group, layers, frames))
    return has_inc, has_state, step > 0


def patch_kernel(pitch, rows, cols, edge, zs_ref, pt_ref, flat_ref):
    depth = zs_ref.shape[1]
    for a in range(3):
        for row in range(rows):
            flat_ref[row * cols : (row + 1) * cols, :] = zs_ref[
                pl.ds(LEAD + (edge + row + a) * pitch, cols), :
            ]
        pt_ref[a * depth : (a + 1) * depth, :] = flat_ref[...].T


def grad_kernel(cells, frame, count, begin, end, *refs):
    pts, dg_ref = refs[:count], refs[count]
    total_ref = None if begin else refs[count + 1]
    out_ref = refs[-1]
    block = 256
    for at in range(0, out_ref.shape[0], block):
        here = pl.ds(at, block)
        total = None if begin else total_ref[here, :]
        part = jnp.dot(
            pts[0][here, :], dg_ref[frame * cells : (frame + 1) * cells, :], preferred_element_type=F32
        )
        total = part if begin else total + part
        out_ref[here, :] = total.astype(out_ref.dtype)


def spec_v():
    return pl.BlockSpec(memory_space=pltpu.VMEM)


def spec_s():
    return pl.BlockSpec(memory_space=pltpu.SMEM)


def place_kernel(at_ref, come_ref, out_ref):
    for j in range(out_ref.shape[0]):
        out_ref[at_ref[j]] = come_ref[j]


RING = 4


def on_ring(own, ntile):
    def move(x, by):
        pairs = [(i, i // 16 * 16 + (i // RING + by) % RING * RING + i % RING) for i in range(ntile)]
        return lax.ppermute(x, "tile", pairs)

    return jnp.stack([own] + [move(own, h) for h in (1, -1, 2)])


def all_rows(near, ntile, tile):
    members = ntile // RING
    groups = [
        [plane * 16 + z * RING + y for plane in range(members // RING) for y in range(RING)] for z in range(RING)
    ]
    come = lax.all_to_all(
        jnp.tile(near, (members, 1, 1)), "tile", 0, 0, axis_index_groups=groups, tiled=True
    )
    z = tile // RING % RING
    at = [
        plane * 16 + (z - h) % RING * RING + y
        for plane in range(members // RING)
        for y in range(RING)
        for h in (0, 1, -1, 2)
    ]
    return pl.pallas_call(
        place_kernel,
        out_shape=in_vmem(come.shape, BF),
        in_specs=[spec_s(), spec_v()],
        out_specs=spec_v(),
        compiler_params=params(16),
        cost_estimate=pl.CostEstimate(flops=0, bytes_accessed=4 << 20, transcendentals=0),
    )(jnp.stack(at).astype(jnp.int32), come)


def on_device(layer_input, hidden_prev, cell_prev, out_cot, bias, master, moment1, moment2):
    frames, rows, cols, width = (layer_input.shape[i] for i in (1, 3, 4, 5))
    ngate = 4 * width
    layers = lax.axis_size("section")
    layer = lax.axis_index("section")
    ntile = lax.axis_size("tile")
    tile = lax.axis_index("tile")
    ncols = ntile // TILE_ROWS
    pitch = cols + 2 * SIDE
    edge = frames + layers - 1

    near = on_ring(master[0].astype(BF), ntile)
    kernel = all_rows(near, ntile, tile).reshape(-1, ngate)

    ids = (frames - 1 + layers - 1 - layer).astype(jnp.int32).reshape(1)
    packed = jnp.concatenate(
        [layer_input[0, :, 0], hidden_prev[0, :, 0], cell_prev[0, :, 0].astype(BF), out_cot[:, 0]], -1
    )
    deeps = [edge + 1 - (frames - 1 - f) for f in range(frames)]
    grid_row, grid_col = tile // ncols, tile % ncols

    def around(by, strip, keep):
        strip = jnp.where(keep, strip, jnp.zeros_like(strip))
        strip, _ = lax.optimization_barrier((strip, near))
        return lax.ppermute(strip, "tile", [(i, by(i)) for i in range(ntile)])

    downs = jnp.concatenate([packed[f, rows - deeps[f] :] for f in range(frames)], 0)
    ups = jnp.concatenate([packed[f, : deeps[f]] for f in range(frames)], 0)
    above = around(lambda i: (i + ncols) % ntile, downs, grid_row < TILE_ROWS - 1)
    below = around(lambda i: (i - ncols) % ntile, ups, grid_row > 0)
    mids = packed.reshape(frames * rows, cols, 4 * width)
    rights = jnp.concatenate([x[:, cols - SIDE :] for x in (above, mids, below)], 0)
    lefts = jnp.concatenate([x[:, :SIDE] for x in (above, mids, below)], 0)
    left = around(lambda i: i // ncols * ncols + (i + 1) % ncols, rights, grid_col < ncols - 1)
    right = around(lambda i: i // ncols * ncols + (i - 1) % ncols, lefts, grid_col > 0)

    size_e = LEAD + (rows + 2 * edge + 2) * pitch
    size_d = LEAD + (rows + 2 * edge) * pitch
    cells = rows * cols

    at = jnp.arange(size_d, dtype=jnp.int32) - LEAD + SIDE
    row_at = at // pitch - edge + grid_row * rows
    col_at = at % pitch - SIDE + grid_col * cols
    inside = (row_at >= 0) & (row_at < TILE_ROWS * rows) & (col_at >= 0) & (col_at < ncols * cols)
    mask = jnp.broadcast_to(inside[:, None], (size_d, width)).astype(BF)

    facs, pts, owns = [None] * frames, [None] * frames, [None] * frames
    for f in reversed(range(frames)):
        gap = edge + 1 - deeps[f]
        at_row = sum(deeps[:f])
        facs[f], zs, owns[f] = pl.pallas_call(
            functools.partial(
                gates_kernel, pitch, width, deeps[f], gap, at_row, (at_row, sum(deeps) + f * rows, sum(deeps) + frames * rows + at_row),
            ),
            out_shape=(
                in_vmem((size_d, 6 * width), F32),
                in_vmem((size_e, 6 * width), BF),
                in_vmem((size_e, width), BF),
            ),
            in_specs=[spec_s()] + [spec_v()] * 8,
            out_specs=(spec_v(),) * 3,
            scratch_shapes=[pltpu.VMEM((size_e, 2 * width), BF), pltpu.VMEM((size_e + 16, 2 * width), F32)],
            compiler_params=params(20),
            cost_estimate=pl.CostEstimate(
                flops=2 * size_d * 18 * width * ngate, bytes_accessed=10 << 20, transcendentals=size_d * 5 * width
            ),
        )(ids, packed[f], above, below, left, right, mask, kernel, bias)
        pts[f] = pl.pallas_call(
            functools.partial(patch_kernel, pitch, rows, cols, edge),
            out_shape=in_vmem((18 * width, cells), BF),
            in_specs=[spec_v()],
            out_specs=spec_v(),
            scratch_shapes=[pltpu.VMEM((cells, 6 * width), BF)],
            compiler_params=params(16),
            cost_estimate=pl.CostEstimate(flops=0, bytes_accessed=8 << 20, transcendentals=0),
        )(zs)
    kernel_t = pl.pallas_call(
        turn_kernel,
        out_shape=in_vmem((3 * ngate, 6 * width), BF),
        in_specs=[spec_v()],
        out_specs=spec_v(),
        compiler_params=params(16),
        cost_estimate=pl.CostEstimate(flops=0, bytes_accessed=4 << 20, transcendentals=0),
    )(kernel)

    steps = layers + frames - 1
    upper, lower = tuple(range(layers // 2, layers)), tuple(range(layers // 2))
    states = {upper: None, lower: None}
    sent = {}
    kept = None
    total = None
    for step in range(steps):
        margin = edge - step
        size_z = LEAD + (rows + 2 * margin - 2) * pitch
        fresh = {}
        for group in (upper, lower):
            picks = picks_of(step, group, layers, frames)
            if not picks:
                continue
            has_inc, has_state, has_kept = needs_of(step, group, layers, frames)
            args = [ids, kernel_t] + [facs[f] for f in picks]
            if layers - 1 in group and step < frames:
                args.append(owns[frames - 1 - step])
            if has_inc:
                above_of = [frames - 1 - step + layers - f for f in picks]
                args += [sent[i] for i in above_of if i < layers]
            if has_state:
                args += list(states[group])
            if has_kept:
                args += list(kept)
            dx, cots, dgates, dh_rec, dc_rec = pl.pallas_call(
                functools.partial(step_kernel, step, group, layers, frames, pitch, rows, cols, width),
                out_shape=(
                    jax.ShapeDtypeStruct((size_z, width), BF),
                    in_vmem((frames * cells, width), BF),
                    in_vmem((frames * cells, ngate), BF),
                    in_vmem((size_z, width), F32),
                    in_vmem((size_z, width), F32),
                ),
                in_specs=[spec_s()] + [spec_v()] * (len(args) - 1),
                out_specs=(spec_v(),) * 5,
                scratch_shapes=[
                    pltpu.VMEM((size_z + 2 * pitch, ngate), BF),
                    pltpu.VMEM((size_z + 16, 6 * width), F32),
                ],
                input_output_aliases={len(args) - 2: 1, len(args) - 1: 2} if has_kept else {},
                compiler_params=params(20),
                cost_estimate=pl.CostEstimate(
                    flops=2 * size_z * 18 * width * ngate, bytes_accessed=10 << 20, transcendentals=0
                ),
            )(*args)
            kept = (cots, dgates)
            states[group] = (dh_rec, dc_rec)
            for i in group:
                if i > 0 and 0 <= frames - 1 - step + layers - 1 - i < frames:
                    fresh[i] = lax.ppermute(dx, "section", [(i, i - 1)])
        sent = fresh
        if step >= layers - 1:
            f = frames - 1 - (step - layers + 1)
            end = step == steps - 1
            args = [pts[f], kept[1]] + ([] if total is None else [total])
            total = pl.pallas_call(
                functools.partial(grad_kernel, cells, f, 1, total is None, end),
                out_shape=in_vmem((18 * width, ngate), BF if end else F32),
                in_specs=[spec_v()] * len(args),
                out_specs=spec_v(),
                compiler_params=params(16),
                cost_estimate=pl.CostEstimate(
                    flops=2 * cells * 18 * width * ngate, bytes_accessed=4 << 20, transcendentals=0
                ),
            )(*args)
    cots = kept[0]
    total, cots = lax.optimization_barrier((total, cots))
    arrived = lax.all_to_all(total, "tile", 0, 0, tiled=True)
    arrived, cots = lax.optimization_barrier((arrived, cots))
    input_cot = cots.reshape(frames, rows, cols, width)
    grad_rows = jnp.sum(arrived.reshape(ntile, -1, ngate).astype(F32), 0)
    new_moment1 = 0.9 * moment1[0] + 0.1 * grad_rows
    new_moment2 = 0.999 * moment2[0] + 0.001 * grad_rows * grad_rows
    fix1 = 1.0 - 0.9**10
    fix2 = 1.0 - 0.999**10
    step_size = new_moment1 / fix1 / (jnp.sqrt(new_moment2 / fix2) + 1e-08)
    new_master = master[0] - 0.001 * step_size - 0.0001 * master[0]
    return (input_cot[None, :, None], new_master[None], new_moment1[None], new_moment2[None])


def solution(mesh):
    return jax.shard_map(
        on_device,
        mesh=mesh,
        in_specs=(
            P("section", None, "tile", None, None, None),
            P("section", None, "tile", None, None, None),
            P("section", None, "tile", None, None, None),
            P(None, "tile", None, None, None),
            P("section", None),
            P("section", "tile", None),
            P("section", "tile", None),
            P("section", "tile", None),
        ),
        out_specs=(
            P("section", None, "tile", None, None, None),
            P("section", "tile", None),
            P("section", "tile", None),
            P("section", "tile", None),
        ),
        check_vma=False,
    )
```

```python
import functools

import jax
import jax.numpy as jnp
from jax import lax
from jax.experimental import pallas as pl
from jax.experimental.pallas import tpu as pltpu
from jax.sharding import PartitionSpec as P

TILE_ROWS = 4
BF = jnp.bfloat16
F32 = jnp.float32
SIDE = 8
LEAD = 16


def params(mib):
    return pltpu.CompilerParams(vmem_limit_bytes=mib << 20)


def chunks(size, most):
    units = size // 16
    count = -(-units * 16 // most)
    out, at = [], 0
    for i in range(count):
        end = units * (i + 1) // count
        out.append((at * 16, (end - at) * 16))
        at = end
    return out


def in_vmem(shape, dtype):
    return pltpu.VMEM(shape, dtype)


def sigmoid(x):
    return 0.5 * jnp.tanh(0.5 * x) + 0.5


def gates_kernel(pitch, width, deep, gap, at_row, at_tip, at_side, ids_ref, mid_ref, above_ref, below_ref, left_ref, right_ref, left_tip_ref, right_tip_ref, mask_ref, kernel_ref, bias_ref, fac_ref, zs_ref, own_ref, flat_ref, z_ref):
    depth = 6 * width
    rows = mid_ref.shape[0]
    cols = pitch - 2 * SIDE
    tall = rows + 2 * deep
    size_e = zs_ref.shape[0]
    begin = gap * pitch
    stop = begin + LEAD + tall * pitch
    if gap:
        for lo, hi in ((0, begin), (stop, size_e)):
            z_ref[8 + lo : 8 + hi, :] = jnp.zeros((hi - lo, 2 * width), F32)
            flat_ref[lo:hi, :] = jnp.zeros((hi - lo, 2 * width), BF)
    z_ref[0:8, :] = jnp.zeros((8, 2 * width), F32)
    z_ref[8 + size_e :, :] = jnp.zeros((8, 2 * width), F32)

    def put(at, value):
        size = value.shape[0]
        z_ref[8 + at : 8 + at + size, :] = value[:, : 2 * width].astype(F32)
        flat_ref[at : at + size, :] = value[:, 2 * width :]

    def beside(side_ref, tip_ref, row):
        if row < 0 or row >= tall:
            return jnp.zeros((SIDE, 4 * width), BF)
        if row < deep:
            return tip_ref[at_row + row]
        if row < deep + rows:
            return side_ref[at_side + row - deep]
        return tip_ref[at_tip + row - deep - rows]

    for row in range(tall + 1):
        before = beside(right_ref, right_tip_ref, row - 1)
        after = beside(left_ref, left_tip_ref, row)
        put(begin + row * pitch, jnp.concatenate([before, after], 0))
    for row in range(tall):
        at = begin + LEAD + row * pitch
        if row < deep:
            put(at, above_ref[at_row + row])
        elif row < deep + rows:
            put(at, mid_ref[row - deep])
        else:
            put(at, below_ref[at_row + row - deep - rows])
    for start, size in chunks(size_e, 256):
        here = pl.ds(start, size)
        own_ref[here, :] = flat_ref[here, width:]
        for b in range(3):
            zs_ref[here, b * 2 * width : (b + 1) * 2 * width] = z_ref[
                7 + b + start : 7 + b + start + size, :
            ].astype(BF)
    cells = fac_ref.shape[0] - 2 * begin
    for start, size in chunks(cells, 480):
        start = start + begin
        total = bias_ref[...]
        for a in range(3):
            total = total + jnp.dot(
                zs_ref[pl.ds(start + a * pitch, size), :],
                kernel_ref[a * depth : (a + 1) * depth, :],
                preferred_element_type=F32,
            )
        here = pl.ds(start, size)
        mask = mask_ref[here, :].astype(F32)
        c_prev = flat_ref[pl.ds(start + pitch, size), :width].astype(F32)
        i = sigmoid(total[:, :width])
        f = sigmoid(total[:, width : 2 * width])
        g = jnp.tanh(total[:, 2 * width : 3 * width])
        o = sigmoid(total[:, 3 * width :])
        tc = jnp.tanh(f * c_prev + i * g)
        fac_ref[here, 0:width] = o * (1.0 - tc * tc)
        fac_ref[here, width : 2 * width] = mask * g * i * (1.0 - i)
        fac_ref[here, 2 * width : 3 * width] = mask * c_prev * f * (1.0 - f)
        fac_ref[here, 3 * width : 4 * width] = mask * i * (1.0 - g * g)
        fac_ref[here, 4 * width : 5 * width] = mask * tc * o * (1.0 - o)
        fac_ref[here, 5 * width : 6 * width] = f


def turn_kernel(kernel_ref, turned_ref):
    depth, ngate = kernel_ref.shape[0] // 3, kernel_ref.shape[1]
    for a in range(3):
        turned_ref[a * ngate : (a + 1) * ngate, :] = kernel_ref[a * depth : (a + 1) * depth, :].T


def step_kernel(step, group, layers, frames, pitch, rows, cols, width, *refs):
    ids_ref, kernel_t_ref = refs[0], refs[1]
    picks = picks_of(step, group, layers, frames)
    fac_refs = refs[2 : 2 + len(picks)]
    at = 2 + len(picks)
    tops = layers - 1 in group and step < frames
    own_ref = refs[at] if tops else None
    at += 1 if tops else 0
    has_inc, has_state, has_kept = needs_of(step, group, layers, frames)
    inc_refs = {}
    for f in picks:
        if frames - 1 - step + layers - f < layers:
            inc_refs[f] = refs[at]
            at += 1
    if has_state:
        dh_ref, dc_ref = refs[at : at + 2]
        at += 2
    if has_kept:
        at += 2
    dx_ref, dxi_ref, dgi_ref, dhn_ref, dcn_ref, d_ref, p_ref = refs[at:]
    margin = frames + layers - 1 - step
    size_d = LEAD + (rows + 2 * margin) * pitch
    size_z = LEAD + (rows + 2 * margin - 2) * pitch
    frame = ids_ref[0] - step
    ngate = 4 * width

    def point(fac_ref, top_frame, pick):
        start_frame = pick == frames - 1
        for start, size in chunks(size_d, 256):
            here = pl.ds(start, size)
            there = pl.ds(start + step * pitch, size)
            if tops and pick == top_frame:
                above = own_ref[pl.ds(start + (step + 1) * pitch, size), :].astype(F32)
            else:
                above = inc_refs[pick][here, :].astype(F32)
            dh = above
            if not start_frame:
                dh = dh + dh_ref[here, :]
            dc = dh * fac_ref[there, 0:width]
            if not start_frame:
                dc = dc + dc_ref[here, :]
            d_ref[here, 0:width] = (dc * fac_ref[there, width : 2 * width]).astype(BF)
            d_ref[here, width : 2 * width] = (dc * fac_ref[there, 2 * width : 3 * width]).astype(BF)
            d_ref[here, 2 * width : 3 * width] = (dc * fac_ref[there, 3 * width : 4 * width]).astype(BF)
            d_ref[here, 3 * width :] = (dh * fac_ref[there, 4 * width : 5 * width]).astype(BF)
            lo, hi = max(start, pitch), min(start + size, pitch + size_z)
            if hi > lo:
                rec = dc * fac_ref[there, 5 * width :]
                dcn_ref[lo - pitch : hi - pitch, :] = rec[lo - start : hi - start, :]

    top_frame = frames - 1 - step
    for number, pick in enumerate(picks):
        pl.when(frame == pick)(functools.partial(point, fac_refs[number], top_frame, pick))

    active = (frame >= picks[0]) & (frame <= picks[-1])

    @pl.when(active)
    def _():
        slot = pl.multiple_of(frame * (rows * cols), rows * cols)
        for row in range(rows):
            dgi_ref[pl.ds(slot + row * cols, cols), :] = d_ref[
                pl.ds(LEAD + (row + margin) * pitch, cols), :
            ]
        p_ref[0:8, :] = jnp.zeros((8, 6 * width), F32)
        p_ref[8 + size_z : 16 + size_z, :] = jnp.zeros((8, 6 * width), F32)
        for start, size in chunks(size_z, 448):
            total = None
            for a in range(3):
                part = jnp.dot(
                    d_ref[pl.ds(start + (2 - a) * pitch, size), :],
                    kernel_t_ref[a * ngate : (a + 1) * ngate, :],
                    preferred_element_type=F32,
                )
                total = part if total is None else total + part
            p_ref[pl.ds(8 + start, size), :] = total
        for start, size in chunks(size_z, 256):
            dz = (
                p_ref[pl.ds(8 + start, size), 2 * width : 4 * width]
                + p_ref[pl.ds(9 + start, size), 0 : 2 * width]
                + p_ref[pl.ds(7 + start, size), 4 * width :]
            )
            dx_ref[pl.ds(start, size), :] = dz[:, :width].astype(BF)
            dhn_ref[pl.ds(start, size), :] = dz[:, width:]
        for row in range(rows):
            dxi_ref[pl.ds(slot + row * cols, cols), :] = dx_ref[
                pl.ds(LEAD + (row + margin - 1) * pitch, cols), :
            ]


def picks_of(step, group, layers, frames):
    now = [frames - 1 - step + layers - 1 - layer for layer in group]
    return sorted(f for f in now if 0 <= f < frames)


def needs_of(step, group, layers, frames):
    has_inc = any(
        0 <= frames - 1 - step + layers - 1 - layer < frames for layer in group if layer < layers - 1
    )
    has_state = any(f < frames - 1 for f in picks_of(step, group, layers, frames))
    return has_inc, has_state, step > 0


def patch_kernel(pitch, rows, cols, edge, zs_ref, pt_ref, flat_ref):
    depth = zs_ref.shape[1]
    for a in range(3):
        for row in range(rows):
            flat_ref[row * cols : (row + 1) * cols, :] = zs_ref[
                pl.ds(LEAD + (edge + row + a) * pitch, cols), :
            ]
        pt_ref[a * depth : (a + 1) * depth, :] = flat_ref[...].T


def grad_kernel(cells, frame, count, begin, end, *refs):
    pts, dg_ref = refs[:count], refs[count]
    total_ref = None if begin else refs[count + 1]
    out_ref = refs[-1]
    block = 256
    for at in range(0, out_ref.shape[0], block):
        here = pl.ds(at, block)
        total = None if begin else total_ref[here, :]
        part = jnp.dot(
            pts[0][here, :], dg_ref[frame * cells : (frame + 1) * cells, :], preferred_element_type=F32
        )
        total = part if begin else total + part
        out_ref[here, :] = total.astype(out_ref.dtype)


def spec_v():
    return pl.BlockSpec(memory_space=pltpu.VMEM)


def spec_s():
    return pl.BlockSpec(memory_space=pltpu.SMEM)


def place_kernel(at_ref, come_ref, out_ref):
    for j in range(out_ref.shape[0]):
        out_ref[at_ref[j]] = come_ref[j]


RING = 4


def on_ring(own, ntile):
    def move(x, by):
        pairs = [(i, i // 16 * 16 + (i // RING + by) % RING * RING + i % RING) for i in range(ntile)]
        return lax.ppermute(x, "tile", pairs)

    return jnp.stack([own] + [move(own, h) for h in (1, -1, 2)])


def all_rows(near, ntile, tile):
    members = ntile // RING
    groups = [
        [plane * 16 + z * RING + y for plane in range(members // RING) for y in range(RING)] for z in range(RING)
    ]
    come = lax.all_to_all(
        jnp.tile(near, (members, 1, 1)), "tile", 0, 0, axis_index_groups=groups, tiled=True
    )
    z = tile // RING % RING
    at = [
        plane * 16 + (z - h) % RING * RING + y
        for plane in range(members // RING)
        for y in range(RING)
        for h in (0, 1, -1, 2)
    ]
    return pl.pallas_call(
        place_kernel,
        out_shape=in_vmem(come.shape, BF),
        in_specs=[spec_s(), spec_v()],
        out_specs=spec_v(),
        compiler_params=params(16),
        cost_estimate=pl.CostEstimate(flops=0, bytes_accessed=4 << 20, transcendentals=0),
    )(jnp.stack(at).astype(jnp.int32), come)


def on_device(layer_input, hidden_prev, cell_prev, out_cot, bias, master, moment1, moment2):
    frames, rows, cols, width = (layer_input.shape[i] for i in (1, 3, 4, 5))
    ngate = 4 * width
    layers = lax.axis_size("section")
    layer = lax.axis_index("section")
    ntile = lax.axis_size("tile")
    tile = lax.axis_index("tile")
    ncols = ntile // TILE_ROWS
    pitch = cols + 2 * SIDE
    edge = frames + layers - 1

    near = on_ring(master[0].astype(BF), ntile)
    kernel = all_rows(near, ntile, tile).reshape(-1, ngate)

    ids = (frames - 1 + layers - 1 - layer).astype(jnp.int32).reshape(1)
    packed = jnp.concatenate(
        [layer_input[0, :, 0], hidden_prev[0, :, 0], cell_prev[0, :, 0].astype(BF), out_cot[:, 0]], -1
    )
    deeps = [edge + 1 - (frames - 1 - f) for f in range(frames)]
    grid_row, grid_col = tile // ncols, tile % ncols

    def around(by, strip, keep):
        got = lax.ppermute(strip, "tile", [(i, by(i)) for i in range(ntile)])
        return jnp.where(keep, got, jnp.zeros_like(got))

    to_right = lambda i: i // ncols * ncols + (i + 1) % ncols
    to_left = lambda i: i // ncols * ncols + (i - 1) % ncols
    downs = jnp.concatenate([packed[f, rows - deeps[f] :] for f in range(frames)], 0)
    ups = jnp.concatenate([packed[f, : deeps[f]] for f in range(frames)], 0)
    mids = packed.reshape(frames * rows, cols, 4 * width)
    mid_right, mid_left = mids[:, cols - SIDE :], mids[:, :SIDE]
    downs, ups, mid_right, mid_left, _ = lax.optimization_barrier((downs, ups, mid_right, mid_left, near))
    above = around(lambda i: (i + ncols) % ntile, downs, grid_row > 0)
    below = around(lambda i: (i - ncols) % ntile, ups, grid_row < TILE_ROWS - 1)
    left = around(to_right, mid_right, grid_col > 0)
    right = around(to_left, mid_left, grid_col < ncols - 1)
    late, _ = lax.optimization_barrier(
        ((layer_input[0, :, 0], hidden_prev[0, :, 0], cell_prev[0, :, 0], out_cot[:, 0]), (above, below))
    )
    tiles = jnp.concatenate([x.astype(BF) for x in late], -1)
    tips = jnp.concatenate([above, below], 0)
    left_tips = around(to_right, tips[:, cols - SIDE :], grid_col > 0)
    right_tips = around(to_left, tips[:, :SIDE], grid_col < ncols - 1)

    size_e = LEAD + (rows + 2 * edge + 2) * pitch
    size_d = LEAD + (rows + 2 * edge) * pitch
    cells = rows * cols

    at = jnp.arange(size_d, dtype=jnp.int32) - LEAD + SIDE
    at, _ = lax.optimization_barrier((at, tiles))
    row_at = at // pitch - edge + grid_row * rows
    col_at = at % pitch - SIDE + grid_col * cols
    inside = (row_at >= 0) & (row_at < TILE_ROWS * rows) & (col_at >= 0) & (col_at < ncols * cols)
    mask = jnp.broadcast_to(inside[:, None], (size_d, width)).astype(BF)

    facs, pts, owns = [None] * frames, [None] * frames, [None] * frames
    for f in reversed(range(frames)):
        gap = edge + 1 - deeps[f]
        at_row = sum(deeps[:f])
        facs[f], zs, owns[f] = pl.pallas_call(
            functools.partial(
                gates_kernel, pitch, width, deeps[f], gap, at_row, sum(deeps) + at_row, f * rows
            ),
            out_shape=(
                in_vmem((size_d, 6 * width), F32),
                in_vmem((size_e, 6 * width), BF),
                in_vmem((size_e, width), BF),
            ),
            in_specs=[spec_s()] + [spec_v()] * 10,
            out_specs=(spec_v(),) * 3,
            scratch_shapes=[pltpu.VMEM((size_e, 2 * width), BF), pltpu.VMEM((size_e + 16, 2 * width), F32)],
            compiler_params=params(20),
            cost_estimate=pl.CostEstimate(
                flops=2 * size_d * 18 * width * ngate, bytes_accessed=10 << 20, transcendentals=size_d * 5 * width
            ),
        )(ids, tiles[f], above, below, left, right, left_tips, right_tips, mask, kernel, bias)
        pts[f] = pl.pallas_call(
            functools.partial(patch_kernel, pitch, rows, cols, edge),
            out_shape=in_vmem((18 * width, cells), BF),
            in_specs=[spec_v()],
            out_specs=spec_v(),
            scratch_shapes=[pltpu.VMEM((cells, 6 * width), BF)],
            compiler_params=params(16),
            cost_estimate=pl.CostEstimate(flops=0, bytes_accessed=8 << 20, transcendentals=0),
        )(zs)
    kernel_t = pl.pallas_call(
        turn_kernel,
        out_shape=in_vmem((3 * ngate, 6 * width), BF),
        in_specs=[spec_v()],
        out_specs=spec_v(),
        compiler_params=params(16),
        cost_estimate=pl.CostEstimate(flops=0, bytes_accessed=4 << 20, transcendentals=0),
    )(kernel)

    steps = layers + frames - 1
    upper, lower = tuple(range(layers // 2, layers)), tuple(range(layers // 2))
    states = {upper: None, lower: None}
    sent = {}
    kept = None
    total = None
    for step in range(steps):
        margin = edge - step
        size_z = LEAD + (rows + 2 * margin - 2) * pitch
        fresh = {}
        for group in (upper, lower):
            picks = picks_of(step, group, layers, frames)
            if not picks:
                continue
            has_inc, has_state, has_kept = needs_of(step, group, layers, frames)
            args = [ids, kernel_t] + [facs[f] for f in picks]
            if layers - 1 in group and step < frames:
                args.append(owns[frames - 1 - step])
            if has_inc:
                above_of = [frames - 1 - step + layers - f for f in picks]
                args += [sent[i] for i in above_of if i < layers]
            if has_state:
                args += list(states[group])
            if has_kept:
                args += list(kept)
            dx, cots, dgates, dh_rec, dc_rec = pl.pallas_call(
                functools.partial(step_kernel, step, group, layers, frames, pitch, rows, cols, width),
                out_shape=(
                    jax.ShapeDtypeStruct((size_z, width), BF),
                    in_vmem((frames * cells, width), BF),
                    in_vmem((frames * cells, ngate), BF),
                    in_vmem((size_z, width), F32),
                    in_vmem((size_z, width), F32),
                ),
                in_specs=[spec_s()] + [spec_v()] * (len(args) - 1),
                out_specs=(spec_v(),) * 5,
                scratch_shapes=[
                    pltpu.VMEM((size_z + 2 * pitch, ngate), BF),
                    pltpu.VMEM((size_z + 16, 6 * width), F32),
                ],
                input_output_aliases={len(args) - 2: 1, len(args) - 1: 2} if has_kept else {},
                compiler_params=params(20),
                cost_estimate=pl.CostEstimate(
                    flops=2 * size_z * 18 * width * ngate, bytes_accessed=10 << 20, transcendentals=0
                ),
            )(*args)
            kept = (cots, dgates)
            states[group] = (dh_rec, dc_rec)
            for i in group:
                if i > 0 and 0 <= frames - 1 - step + layers - 1 - i < frames:
                    fresh[i] = lax.ppermute(dx, "section", [(i, i - 1)])
        sent = fresh
        if step >= layers - 1:
            f = frames - 1 - (step - layers + 1)
            end = step == steps - 1
            args = [pts[f], kept[1]] + ([] if total is None else [total])
            total = pl.pallas_call(
                functools.partial(grad_kernel, cells, f, 1, total is None, end),
                out_shape=in_vmem((18 * width, ngate), BF if end else F32),
                in_specs=[spec_v()] * len(args),
                out_specs=spec_v(),
                compiler_params=params(16),
                cost_estimate=pl.CostEstimate(
                    flops=2 * cells * 18 * width * ngate, bytes_accessed=4 << 20, transcendentals=0
                ),
            )(*args)
    cots = kept[0]
    total, cots = lax.optimization_barrier((total, cots))
    arrived = lax.all_to_all(total, "tile", 0, 0, tiled=True)
    arrived, cots = lax.optimization_barrier((arrived, cots))
    input_cot = cots.reshape(frames, rows, cols, width)
    grad_rows = jnp.sum(arrived.reshape(ntile, -1, ngate).astype(F32), 0)
    new_moment1 = 0.9 * moment1[0] + 0.1 * grad_rows
    new_moment2 = 0.999 * moment2[0] + 0.001 * grad_rows * grad_rows
    fix1 = 1.0 - 0.9**10
    fix2 = 1.0 - 0.999**10
    step_size = new_moment1 / fix1 / (jnp.sqrt(new_moment2 / fix2) + 1e-08)
    new_master = master[0] - 0.001 * step_size - 0.0001 * master[0]
    return (input_cot[None, :, None], new_master[None], new_moment1[None], new_moment2[None])


def solution(mesh):
    return jax.shard_map(
        on_device,
        mesh=mesh,
        in_specs=(
            P("section", None, "tile", None, None, None),
            P("section", None, "tile", None, None, None),
            P("section", None, "tile", None, None, None),
            P(None, "tile", None, None, None),
            P("section", None),
            P("section", "tile", None),
            P("section", "tile", None),
            P("section", "tile", None),
        ),
        out_specs=(
            P("section", None, "tile", None, None, None),
            P("section", "tile", None),
            P("section", "tile", None),
            P("section", "tile", None),
        ),
        check_vma=False,
    )
```

```python
import functools

import jax
import jax.numpy as jnp
from jax import lax
from jax.experimental import pallas as pl
from jax.experimental.pallas import tpu as pltpu
from jax.sharding import PartitionSpec as P

TILE_ROWS = 4
BF = jnp.bfloat16
F32 = jnp.float32
SIDE = 8
LEAD = 16


def params(mib):
    return pltpu.CompilerParams(vmem_limit_bytes=mib << 20)


def chunks(size, most):
    units = size // 16
    count = -(-units * 16 // most)
    out, at = [], 0
    for i in range(count):
        end = units * (i + 1) // count
        out.append((at * 16, (end - at) * 16))
        at = end
    return out


def in_vmem(shape, dtype):
    return pltpu.VMEM(shape, dtype)


def sigmoid(x):
    return 0.5 * jnp.tanh(0.5 * x) + 0.5


def gates_kernel(pitch, width, deep, gap, at_row, at_tip, at_side, ids_ref, mid_ref, above_ref, below_ref, left_ref, right_ref, left_tip_ref, right_tip_ref, mask_ref, kernel_ref, bias_ref, fac_ref, zs_ref, own_ref, flat_ref, z_ref):
    depth = 6 * width
    rows = mid_ref.shape[0]
    cols = pitch - 2 * SIDE
    tall = rows + 2 * deep
    size_e = zs_ref.shape[0]
    begin = gap * pitch
    stop = begin + LEAD + tall * pitch
    if gap:
        for lo, hi in ((0, begin), (stop, size_e)):
            z_ref[8 + lo : 8 + hi, :] = jnp.zeros((hi - lo, 2 * width), F32)
            zs_ref[lo:hi, 2 * width : 4 * width] = jnp.zeros((hi - lo, 2 * width), BF)
            flat_ref[lo:hi, :] = jnp.zeros((hi - lo, width), BF)
            own_ref[lo:hi, :] = jnp.zeros((hi - lo, width), BF)
    z_ref[0:8, :] = jnp.zeros((8, 2 * width), F32)
    z_ref[8 + size_e :, :] = jnp.zeros((8, 2 * width), F32)

    def put(at, value):
        size = value.shape[0]
        z_ref[8 + at : 8 + at + size, :] = value[:, : 2 * width].astype(F32)
        zs_ref[at : at + size, 2 * width : 4 * width] = value[:, : 2 * width]
        flat_ref[at : at + size, :] = value[:, 2 * width : 3 * width]
        own_ref[at : at + size, :] = value[:, 3 * width :]

    def beside(side_ref, tip_ref, row):
        if row < 0 or row >= tall:
            return jnp.zeros((SIDE, 4 * width), BF)
        if row < deep:
            return tip_ref[at_row + row]
        if row < deep + rows:
            return side_ref[at_side + row - deep]
        return tip_ref[at_tip + row - deep - rows]

    for row in range(tall + 1):
        before = beside(right_ref, right_tip_ref, row - 1)
        after = beside(left_ref, left_tip_ref, row)
        put(begin + row * pitch, jnp.concatenate([before, after], 0))
    for row in range(tall):
        at = begin + LEAD + row * pitch
        if row < deep:
            put(at, above_ref[at_row + row])
        elif row < deep + rows:
            put(at, mid_ref[row - deep])
        else:
            put(at, below_ref[at_row + row - deep - rows])
    for start, size in chunks(size_e, 256):
        here = pl.ds(start, size)
        for b in (0, 2):
            zs_ref[here, b * 2 * width : (b + 1) * 2 * width] = z_ref[
                7 + b + start : 7 + b + start + size, :
            ].astype(BF)
    cells = fac_ref.shape[0] - 2 * begin
    for start, size in chunks(cells, 480):
        start = start + begin
        total = bias_ref[...]
        for a in range(3):
            total = total + jnp.dot(
                zs_ref[pl.ds(start + a * pitch, size), :],
                kernel_ref[a * depth : (a + 1) * depth, :],
                preferred_element_type=F32,
            )
        here = pl.ds(start, size)
        mask = mask_ref[here, :].astype(F32)
        c_prev = flat_ref[pl.ds(start + pitch, size), :].astype(F32)
        i = sigmoid(total[:, :width])
        f = sigmoid(total[:, width : 2 * width])
        g = jnp.tanh(total[:, 2 * width : 3 * width])
        o = sigmoid(total[:, 3 * width :])
        tc = jnp.tanh(f * c_prev + i * g)
        fac_ref[here, 0:width] = o * (1.0 - tc * tc)
        fac_ref[here, width : 2 * width] = mask * g * i * (1.0 - i)
        fac_ref[here, 2 * width : 3 * width] = mask * c_prev * f * (1.0 - f)
        fac_ref[here, 3 * width : 4 * width] = mask * i * (1.0 - g * g)
        fac_ref[here, 4 * width : 5 * width] = mask * tc * o * (1.0 - o)
        fac_ref[here, 5 * width : 6 * width] = f


def turn_kernel(kernel_ref, turned_ref):
    depth, ngate = kernel_ref.shape[0] // 3, kernel_ref.shape[1]
    for a in range(3):
        turned_ref[a * ngate : (a + 1) * ngate, :] = kernel_ref[a * depth : (a + 1) * depth, :].T


def step_kernel(step, group, layers, frames, pitch, rows, cols, width, *refs):
    ids_ref, kernel_t_ref = refs[0], refs[1]
    picks = picks_of(step, group, layers, frames)
    fac_refs = refs[2 : 2 + len(picks)]
    at = 2 + len(picks)
    tops = layers - 1 in group and step < frames
    own_ref = refs[at] if tops else None
    at += 1 if tops else 0
    has_inc, has_state, has_kept = needs_of(step, group, layers, frames)
    inc_refs = {}
    for f in picks:
        if frames - 1 - step + layers - f < layers:
            inc_refs[f] = refs[at]
            at += 1
    if has_state:
        dh_ref, dc_ref = refs[at : at + 2]
        at += 2
    if has_kept:
        at += 2
    dx_ref, dxi_ref, dgi_ref, dhn_ref, dcn_ref, d_ref, p_ref = refs[at:]
    margin = frames + layers - 1 - step
    size_d = LEAD + (rows + 2 * margin) * pitch
    size_z = LEAD + (rows + 2 * margin - 2) * pitch
    frame = ids_ref[0] - step
    ngate = 4 * width

    def point(fac_ref, top_frame, pick):
        start_frame = pick == frames - 1
        for start, size in chunks(size_d, 256):
            here = pl.ds(start, size)
            there = pl.ds(start + step * pitch, size)
            if tops and pick == top_frame:
                above = own_ref[pl.ds(start + (step + 1) * pitch, size), :].astype(F32)
            else:
                above = inc_refs[pick][here, :].astype(F32)
            dh = above
            if not start_frame:
                dh = dh + dh_ref[here, :]
            dc = dh * fac_ref[there, 0:width]
            if not start_frame:
                dc = dc + dc_ref[here, :]
            d_ref[here, 0:width] = (dc * fac_ref[there, width : 2 * width]).astype(BF)
            d_ref[here, width : 2 * width] = (dc * fac_ref[there, 2 * width : 3 * width]).astype(BF)
            d_ref[here, 2 * width : 3 * width] = (dc * fac_ref[there, 3 * width : 4 * width]).astype(BF)
            d_ref[here, 3 * width :] = (dh * fac_ref[there, 4 * width : 5 * width]).astype(BF)
            lo, hi = max(start, pitch), min(start + size, pitch + size_z)
            if hi > lo:
                rec = dc * fac_ref[there, 5 * width :]
                dcn_ref[lo - pitch : hi - pitch, :] = rec[lo - start : hi - start, :]

    top_frame = frames - 1 - step
    for number, pick in enumerate(picks):
        pl.when(frame == pick)(functools.partial(point, fac_refs[number], top_frame, pick))

    active = (frame >= picks[0]) & (frame <= picks[-1])

    @pl.when(active)
    def _():
        slot = pl.multiple_of(frame * (rows * cols), rows * cols)
        for row in range(rows):
            dgi_ref[pl.ds(slot + row * cols, cols), :] = d_ref[
                pl.ds(LEAD + (row + margin) * pitch, cols), :
            ]
        p_ref[0:8, :] = jnp.zeros((8, 6 * width), F32)
        p_ref[8 + size_z : 16 + size_z, :] = jnp.zeros((8, 6 * width), F32)
        for start, size in chunks(size_z, 448):
            total = None
            for a in range(3):
                part = jnp.dot(
                    d_ref[pl.ds(start + (2 - a) * pitch, size), :],
                    kernel_t_ref[a * ngate : (a + 1) * ngate, :],
                    preferred_element_type=F32,
                )
                total = part if total is None else total + part
            p_ref[pl.ds(8 + start, size), :] = total
        for start, size in chunks(size_z, 256):
            dz = (
                p_ref[pl.ds(8 + start, size), 2 * width : 4 * width]
                + p_ref[pl.ds(9 + start, size), 0 : 2 * width]
                + p_ref[pl.ds(7 + start, size), 4 * width :]
            )
            dx_ref[pl.ds(start, size), :] = dz[:, :width].astype(BF)
            dhn_ref[pl.ds(start, size), :] = dz[:, width:]
        for row in range(rows):
            dxi_ref[pl.ds(slot + row * cols, cols), :] = dx_ref[
                pl.ds(LEAD + (row + margin - 1) * pitch, cols), :
            ]


def picks_of(step, group, layers, frames):
    now = [frames - 1 - step + layers - 1 - layer for layer in group]
    return sorted(f for f in now if 0 <= f < frames)


def needs_of(step, group, layers, frames):
    has_inc = any(
        0 <= frames - 1 - step + layers - 1 - layer < frames for layer in group if layer < layers - 1
    )
    has_state = any(f < frames - 1 for f in picks_of(step, group, layers, frames))
    return has_inc, has_state, step > 0


def patch_kernel(pitch, rows, cols, edge, zs_ref, pt_ref, flat_ref):
    depth = zs_ref.shape[1]
    for a in range(3):
        for row in range(rows):
            flat_ref[row * cols : (row + 1) * cols, :] = zs_ref[
                pl.ds(LEAD + (edge + row + a) * pitch, cols), :
            ]
        pt_ref[a * depth : (a + 1) * depth, :] = flat_ref[...].T


def grad_kernel(cells, frame, count, begin, end, *refs):
    pts, dg_ref = refs[:count], refs[count]
    total_ref = None if begin else refs[count + 1]
    out_ref = refs[-1]
    block = 256
    for at in range(0, out_ref.shape[0], block):
        here = pl.ds(at, block)
        total = None if begin else total_ref[here, :]
        part = jnp.dot(
            pts[0][here, :], dg_ref[frame * cells : (frame + 1) * cells, :], preferred_element_type=F32
        )
        total = part if begin else total + part
        out_ref[here, :] = total.astype(out_ref.dtype)


def spec_v():
    return pl.BlockSpec(memory_space=pltpu.VMEM)


def spec_s():
    return pl.BlockSpec(memory_space=pltpu.SMEM)


def place_kernel(at_ref, come_ref, out_ref):
    for j in range(out_ref.shape[0]):
        out_ref[at_ref[j]] = come_ref[j]


RING = 4


def on_ring(own, ntile):
    def move(x, by):
        pairs = [(i, i // 16 * 16 + (i // RING + by) % RING * RING + i % RING) for i in range(ntile)]
        return lax.ppermute(x, "tile", pairs)

    return jnp.stack([own] + [move(own, h) for h in (1, -1, 2)])


def all_rows(near, ntile, tile):
    members = ntile // RING
    groups = [
        [plane * 16 + z * RING + y for plane in range(members // RING) for y in range(RING)] for z in range(RING)
    ]
    come = lax.all_to_all(
        jnp.tile(near, (members, 1, 1)), "tile", 0, 0, axis_index_groups=groups, tiled=True
    )
    z = tile // RING % RING
    at = [
        plane * 16 + (z - h) % RING * RING + y
        for plane in range(members // RING)
        for y in range(RING)
        for h in (0, 1, -1, 2)
    ]
    return pl.pallas_call(
        place_kernel,
        out_shape=in_vmem(come.shape, BF),
        in_specs=[spec_s(), spec_v()],
        out_specs=spec_v(),
        compiler_params=params(16),
        cost_estimate=pl.CostEstimate(flops=0, bytes_accessed=4 << 20, transcendentals=0),
    )(jnp.stack(at).astype(jnp.int32), come)


def on_device(layer_input, hidden_prev, cell_prev, out_cot, bias, master, moment1, moment2):
    frames, rows, cols, width = (layer_input.shape[i] for i in (1, 3, 4, 5))
    ngate = 4 * width
    layers = lax.axis_size("section")
    layer = lax.axis_index("section")
    ntile = lax.axis_size("tile")
    tile = lax.axis_index("tile")
    ncols = ntile // TILE_ROWS
    pitch = cols + 2 * SIDE
    edge = frames + layers - 1

    near = on_ring(master[0].astype(BF), ntile)
    kernel = all_rows(near, ntile, tile).reshape(-1, ngate)

    ids = (frames - 1 + layers - 1 - layer).astype(jnp.int32).reshape(1)
    packed = jnp.concatenate(
        [layer_input[0, :, 0], hidden_prev[0, :, 0], cell_prev[0, :, 0].astype(BF), out_cot[:, 0]], -1
    )
    deeps = [edge + 1 - (frames - 1 - f) for f in range(frames)]
    grid_row, grid_col = tile // ncols, tile % ncols

    def around(by, strip, keep):
        got = lax.ppermute(strip, "tile", [(i, by(i)) for i in range(ntile)])
        return jnp.where(keep, got, jnp.zeros_like(got))

    to_right = lambda i: i // ncols * ncols + (i + 1) % ncols
    to_left = lambda i: i // ncols * ncols + (i - 1) % ncols
    downs = jnp.concatenate([packed[f, rows - deeps[f] :] for f in range(frames)], 0)
    ups = jnp.concatenate([packed[f, : deeps[f]] for f in range(frames)], 0)
    mids = packed.reshape(frames * rows, cols, 4 * width)
    mid_right, mid_left = mids[:, cols - SIDE :], mids[:, :SIDE]
    downs, ups, mid_right, mid_left, _ = lax.optimization_barrier((downs, ups, mid_right, mid_left, near))
    above = around(lambda i: (i + ncols) % ntile, downs, grid_row > 0)
    below = around(lambda i: (i - ncols) % ntile, ups, grid_row < TILE_ROWS - 1)
    left = around(to_right, mid_right, grid_col > 0)
    right = around(to_left, mid_left, grid_col < ncols - 1)
    late, _ = lax.optimization_barrier(
        ((layer_input[0, :, 0], hidden_prev[0, :, 0], cell_prev[0, :, 0], out_cot[:, 0]), (above, below))
    )
    tiles = jnp.concatenate([x.astype(BF) for x in late], -1)
    tips = jnp.concatenate([above, below], 0)
    left_tips = around(to_right, tips[:, cols - SIDE :], grid_col > 0)
    right_tips = around(to_left, tips[:, :SIDE], grid_col < ncols - 1)

    size_e = LEAD + (rows + 2 * edge + 2) * pitch
    size_d = LEAD + (rows + 2 * edge) * pitch
    cells = rows * cols

    at = jnp.arange(size_d, dtype=jnp.int32) - LEAD + SIDE
    at, _ = lax.optimization_barrier((at, tiles))
    row_at = at // pitch - edge + grid_row * rows
    col_at = at % pitch - SIDE + grid_col * cols
    inside = (row_at >= 0) & (row_at < TILE_ROWS * rows) & (col_at >= 0) & (col_at < ncols * cols)
    mask = jnp.broadcast_to(inside[:, None], (size_d, width)).astype(BF)

    facs, pts, owns = [None] * frames, [None] * frames, [None] * frames
    for f in reversed(range(frames)):
        gap = edge + 1 - deeps[f]
        at_row = sum(deeps[:f])
        facs[f], zs, owns[f] = pl.pallas_call(
            functools.partial(
                gates_kernel, pitch, width, deeps[f], gap, at_row, sum(deeps) + at_row, f * rows
            ),
            out_shape=(
                in_vmem((size_d, 6 * width), F32),
                in_vmem((size_e, 6 * width), BF),
                in_vmem((size_e, width), BF),
            ),
            in_specs=[spec_s()] + [spec_v()] * 10,
            out_specs=(spec_v(),) * 3,
            scratch_shapes=[pltpu.VMEM((size_e, width), BF), pltpu.VMEM((size_e + 16, 2 * width), F32)],
            compiler_params=params(20),
            cost_estimate=pl.CostEstimate(
                flops=2 * size_d * 18 * width * ngate, bytes_accessed=10 << 20, transcendentals=size_d * 5 * width
            ),
        )(ids, tiles[f], above, below, left, right, left_tips, right_tips, mask, kernel, bias)
        pts[f] = pl.pallas_call(
            functools.partial(patch_kernel, pitch, rows, cols, edge),
            out_shape=in_vmem((18 * width, cells), BF),
            in_specs=[spec_v()],
            out_specs=spec_v(),
            scratch_shapes=[pltpu.VMEM((cells, 6 * width), BF)],
            compiler_params=params(16),
            cost_estimate=pl.CostEstimate(flops=0, bytes_accessed=8 << 20, transcendentals=0),
        )(zs)
    kernel_t = pl.pallas_call(
        turn_kernel,
        out_shape=in_vmem((3 * ngate, 6 * width), BF),
        in_specs=[spec_v()],
        out_specs=spec_v(),
        compiler_params=params(16),
        cost_estimate=pl.CostEstimate(flops=0, bytes_accessed=4 << 20, transcendentals=0),
    )(kernel)

    steps = layers + frames - 1
    upper, lower = tuple(range(layers // 2, layers)), tuple(range(layers // 2))
    states = {upper: None, lower: None}
    sent = {}
    kept = None
    total = None
    for step in range(steps):
        margin = edge - step
        size_z = LEAD + (rows + 2 * margin - 2) * pitch
        fresh = {}
        for group in (upper, lower):
            picks = picks_of(step, group, layers, frames)
            if not picks:
                continue
            has_inc, has_state, has_kept = needs_of(step, group, layers, frames)
            args = [ids, kernel_t] + [facs[f] for f in picks]
            if layers - 1 in group and step < frames:
                args.append(owns[frames - 1 - step])
            if has_inc:
                above_of = [frames - 1 - step + layers - f for f in picks]
                args += [sent[i] for i in above_of if i < layers]
            if has_state:
                args += list(states[group])
            if has_kept:
                args += list(kept)
            dx, cots, dgates, dh_rec, dc_rec = pl.pallas_call(
                functools.partial(step_kernel, step, group, layers, frames, pitch, rows, cols, width),
                out_shape=(
                    jax.ShapeDtypeStruct((size_z, width), BF),
                    in_vmem((frames * cells, width), BF),
                    in_vmem((frames * cells, ngate), BF),
                    in_vmem((size_z, width), F32),
                    in_vmem((size_z, width), F32),
                ),
                in_specs=[spec_s()] + [spec_v()] * (len(args) - 1),
                out_specs=(spec_v(),) * 5,
                scratch_shapes=[
                    pltpu.VMEM((size_z + 2 * pitch, ngate), BF),
                    pltpu.VMEM((size_z + 16, 6 * width), F32),
                ],
                input_output_aliases={len(args) - 2: 1, len(args) - 1: 2} if has_kept else {},
                compiler_params=params(20),
                cost_estimate=pl.CostEstimate(
                    flops=2 * size_z * 18 * width * ngate, bytes_accessed=10 << 20, transcendentals=0
                ),
            )(*args)
            kept = (cots, dgates)
            states[group] = (dh_rec, dc_rec)
            for i in group:
                if i > 0 and 0 <= frames - 1 - step + layers - 1 - i < frames:
                    fresh[i] = lax.ppermute(dx, "section", [(i, i - 1)])
        sent = fresh
        if step >= layers - 1:
            f = frames - 1 - (step - layers + 1)
            end = step == steps - 1
            args = [pts[f], kept[1]] + ([] if total is None else [total])
            total = pl.pallas_call(
                functools.partial(grad_kernel, cells, f, 1, total is None, end),
                out_shape=in_vmem((18 * width, ngate), BF if end else F32),
                in_specs=[spec_v()] * len(args),
                out_specs=spec_v(),
                compiler_params=params(16),
                cost_estimate=pl.CostEstimate(
                    flops=2 * cells * 18 * width * ngate, bytes_accessed=4 << 20, transcendentals=0
                ),
            )(*args)
    cots = kept[0]
    total, cots = lax.optimization_barrier((total, cots))
    arrived = lax.all_to_all(total, "tile", 0, 0, tiled=True)
    arrived, cots = lax.optimization_barrier((arrived, cots))
    input_cot = cots.reshape(frames, rows, cols, width)
    grad_rows = jnp.sum(arrived.reshape(ntile, -1, ngate).astype(F32), 0)
    new_moment1 = 0.9 * moment1[0] + 0.1 * grad_rows
    new_moment2 = 0.999 * moment2[0] + 0.001 * grad_rows * grad_rows
    fix1 = 1.0 - 0.9**10
    fix2 = 1.0 - 0.999**10
    step_size = new_moment1 / fix1 / (jnp.sqrt(new_moment2 / fix2) + 1e-08)
    new_master = master[0] - 0.001 * step_size - 0.0001 * master[0]
    return (input_cot[None, :, None], new_master[None], new_moment1[None], new_moment2[None])


def solution(mesh):
    return jax.shard_map(
        on_device,
        mesh=mesh,
        in_specs=(
            P("section", None, "tile", None, None, None),
            P("section", None, "tile", None, None, None),
            P("section", None, "tile", None, None, None),
            P(None, "tile", None, None, None),
            P("section", None),
            P("section", "tile", None),
            P("section", "tile", None),
            P("section", "tile", None),
        ),
        out_specs=(
            P("section", None, "tile", None, None, None),
            P("section", "tile", None),
            P("section", "tile", None),
            P("section", "tile", None),
        ),
        check_vma=False,
    )
```

```python
import functools

import jax
import jax.numpy as jnp
from jax import lax
from jax.experimental import pallas as pl
from jax.experimental.pallas import tpu as pltpu
from jax.sharding import PartitionSpec as P

TILE_ROWS = 4
BF = jnp.bfloat16
F32 = jnp.float32
SIDE = 8
LEAD = 16


def params(mib):
    return pltpu.CompilerParams(vmem_limit_bytes=mib << 20)


def chunks(size, most):
    units = size // 16
    count = -(-units * 16 // most)
    out, at = [], 0
    for i in range(count):
        end = units * (i + 1) // count
        out.append((at * 16, (end - at) * 16))
        at = end
    return out


def in_vmem(shape, dtype):
    return pltpu.VMEM(shape, dtype)


def sigmoid(x):
    return 0.5 * jnp.tanh(0.5 * x) + 0.5


def gates_kernel(pitch, width, deep, gap, at_row, at_tip, at_side, ids_ref, mid_ref, above_ref, below_ref, left_ref, right_ref, left_tip_ref, right_tip_ref, mask_ref, kernel_ref, bias_ref, fac_ref, zs_ref, own_ref, flat_ref, z_ref):
    depth = 6 * width
    rows = mid_ref.shape[0]
    cols = pitch - 2 * SIDE
    tall = rows + 2 * deep
    size_e = zs_ref.shape[0]
    begin = gap * pitch
    stop = begin + LEAD + tall * pitch
    if gap:
        for lo, hi in ((0, begin), (stop, size_e)):
            z_ref[8 + lo : 8 + hi, :] = jnp.zeros((hi - lo, 2 * width), F32)
            zs_ref[lo:hi, 2 * width : 4 * width] = jnp.zeros((hi - lo, 2 * width), BF)
            flat_ref[lo:hi, :] = jnp.zeros((hi - lo, width), BF)
            own_ref[lo:hi, :] = jnp.zeros((hi - lo, width), BF)
    z_ref[0:8, :] = jnp.zeros((8, 2 * width), F32)
    z_ref[8 + size_e :, :] = jnp.zeros((8, 2 * width), F32)

    def put(at, value):
        size = value.shape[0]
        z_ref[8 + at : 8 + at + size, :] = value[:, : 2 * width].astype(F32)
        zs_ref[at : at + size, 2 * width : 4 * width] = value[:, : 2 * width]
        flat_ref[at : at + size, :] = value[:, 2 * width : 3 * width]
        own_ref[at : at + size, :] = value[:, 3 * width :]

    def beside(side_ref, tip_ref, row):
        if row < 0 or row >= tall:
            return jnp.zeros((SIDE, 4 * width), BF)
        if row < deep:
            return tip_ref[at_row + row]
        if row < deep + rows:
            return side_ref[at_side + row - deep]
        return tip_ref[at_tip + row - deep - rows]

    for row in range(tall + 1):
        before = beside(right_ref, right_tip_ref, row - 1)
        after = beside(left_ref, left_tip_ref, row)
        put(begin + row * pitch, jnp.concatenate([before, after], 0))
    for row in range(tall):
        at = begin + LEAD + row * pitch
        if row < deep:
            put(at, above_ref[at_row + row])
        elif row < deep + rows:
            put(at, mid_ref[row - deep])
        else:
            put(at, below_ref[at_row + row - deep - rows])
    for start, size in chunks(size_e, 256):
        here = pl.ds(start, size)
        for b in (0, 2):
            zs_ref[here, b * 2 * width : (b + 1) * 2 * width] = z_ref[
                7 + b + start : 7 + b + start + size, :
            ].astype(BF)
    cells = fac_ref.shape[0] - 2 * begin
    for start, size in chunks(cells, 480):
        start = start + begin
        total = bias_ref[...]
        for a in range(3):
            total = total + jnp.dot(
                zs_ref[pl.ds(start + a * pitch, size), :],
                kernel_ref[a * depth : (a + 1) * depth, :],
                preferred_element_type=F32,
            )
        here = pl.ds(start, size)
        mask = mask_ref[here, :].astype(F32)
        c_prev = flat_ref[pl.ds(start + pitch, size), :].astype(F32)
        i = sigmoid(total[:, :width])
        f = sigmoid(total[:, width : 2 * width])
        g = jnp.tanh(total[:, 2 * width : 3 * width])
        o = sigmoid(total[:, 3 * width :])
        tc = jnp.tanh(f * c_prev + i * g)
        fac_ref[here, 0:width] = o * (1.0 - tc * tc)
        fac_ref[here, width : 2 * width] = mask * g * i * (1.0 - i)
        fac_ref[here, 2 * width : 3 * width] = mask * c_prev * f * (1.0 - f)
        fac_ref[here, 3 * width : 4 * width] = mask * i * (1.0 - g * g)
        fac_ref[here, 4 * width : 5 * width] = mask * tc * o * (1.0 - o)
        fac_ref[here, 5 * width : 6 * width] = f


def turn_kernel(kernel_ref, turned_ref):
    depth, ngate = kernel_ref.shape[0] // 3, kernel_ref.shape[1]
    for a in range(3):
        turned_ref[a * ngate : (a + 1) * ngate, :] = kernel_ref[a * depth : (a + 1) * depth, :].T


def step_kernel(step, group, layers, frames, pitch, rows, cols, width, *refs):
    ids_ref, kernel_t_ref = refs[0], refs[1]
    picks = picks_of(step, group, layers, frames)
    fac_refs = refs[2 : 2 + len(picks)]
    at = 2 + len(picks)
    tops = layers - 1 in group and step < frames
    own_ref = refs[at] if tops else None
    at += 1 if tops else 0
    has_inc, has_state, has_kept = needs_of(step, group, layers, frames)
    inc_refs = {}
    for f in picks:
        if frames - 1 - step + layers - f < layers:
            inc_refs[f] = refs[at]
            at += 1
    if has_state:
        dh_ref, dc_ref = refs[at : at + 2]
        at += 2
    if has_kept:
        at += 2
    last = picks == [0]
    dx_ref, dxi_ref, dgi_ref = refs[at : at + 3]
    dhn_ref, dcn_ref = (None, None) if last else refs[at + 3 : at + 5]
    d_ref, p_ref = refs[-2:]
    part = width if last else 2 * width
    margin = frames + layers - 1 - step
    size_d = LEAD + (rows + 2 * margin) * pitch
    size_z = LEAD + (rows + 2 * margin - 2) * pitch
    frame = ids_ref[0] - step
    ngate = 4 * width

    def point(fac_ref, top_frame, pick):
        start_frame = pick == frames - 1
        for start, size in chunks(size_d, 256):
            here = pl.ds(start, size)
            there = pl.ds(start + step * pitch, size)
            if tops and pick == top_frame:
                above = own_ref[pl.ds(start + (step + 1) * pitch, size), :].astype(F32)
            else:
                above = inc_refs[pick][here, :].astype(F32)
            dh = above
            if not start_frame:
                dh = dh + dh_ref[here, :]
            dc = dh * fac_ref[there, 0:width]
            if not start_frame:
                dc = dc + dc_ref[here, :]
            d_ref[here, 0:width] = (dc * fac_ref[there, width : 2 * width]).astype(BF)
            d_ref[here, width : 2 * width] = (dc * fac_ref[there, 2 * width : 3 * width]).astype(BF)
            d_ref[here, 2 * width : 3 * width] = (dc * fac_ref[there, 3 * width : 4 * width]).astype(BF)
            d_ref[here, 3 * width :] = (dh * fac_ref[there, 4 * width : 5 * width]).astype(BF)
            lo, hi = max(start, pitch), min(start + size, pitch + size_z)
            if hi > lo and not last:
                rec = dc * fac_ref[there, 5 * width :]
                dcn_ref[lo - pitch : hi - pitch, :] = rec[lo - start : hi - start, :]

    top_frame = frames - 1 - step
    for number, pick in enumerate(picks):
        pl.when(frame == pick)(functools.partial(point, fac_refs[number], top_frame, pick))

    active = (frame >= picks[0]) & (frame <= picks[-1])

    @pl.when(active)
    def _():
        slot = pl.multiple_of(frame * (rows * cols), rows * cols)
        for row in range(rows):
            dgi_ref[pl.ds(slot + row * cols, cols), :] = d_ref[
                pl.ds(LEAD + (row + margin) * pitch, cols), :
            ]
        p_ref[0:8, :] = jnp.zeros((8, 3 * part), F32)
        p_ref[8 + size_z : 16 + size_z, :] = jnp.zeros((8, 3 * part), F32)
        def turned(a):
            here = slice(a * ngate, (a + 1) * ngate)
            if not last:
                return kernel_t_ref[here, :]
            return jnp.concatenate(
                [kernel_t_ref[here, b * 2 * width : b * 2 * width + width] for b in range(3)], 1
            )

        for start, size in chunks(size_z, 448):
            total = None
            for a in range(3):
                term = jnp.dot(
                    d_ref[pl.ds(start + (2 - a) * pitch, size), :], turned(a), preferred_element_type=F32
                )
                total = term if total is None else total + term
            p_ref[pl.ds(8 + start, size), :] = total
        for start, size in chunks(size_z, 256):
            dz = (
                p_ref[pl.ds(8 + start, size), part : 2 * part]
                + p_ref[pl.ds(9 + start, size), 0:part]
                + p_ref[pl.ds(7 + start, size), 2 * part :]
            )
            dx_ref[pl.ds(start, size), :] = dz[:, :width].astype(BF)
            if not last:
                dhn_ref[pl.ds(start, size), :] = dz[:, width:]
        for row in range(rows):
            dxi_ref[pl.ds(slot + row * cols, cols), :] = dx_ref[
                pl.ds(LEAD + (row + margin - 1) * pitch, cols), :
            ]


def picks_of(step, group, layers, frames):
    now = [frames - 1 - step + layers - 1 - layer for layer in group]
    return sorted(f for f in now if 0 <= f < frames)


def needs_of(step, group, layers, frames):
    has_inc = any(
        0 <= frames - 1 - step + layers - 1 - layer < frames for layer in group if layer < layers - 1
    )
    has_state = any(f < frames - 1 for f in picks_of(step, group, layers, frames))
    return has_inc, has_state, step > 0


def patch_kernel(pitch, rows, cols, edge, zs_ref, pt_ref, flat_ref):
    depth = zs_ref.shape[1]
    for a in range(3):
        for row in range(rows):
            flat_ref[row * cols : (row + 1) * cols, :] = zs_ref[
                pl.ds(LEAD + (edge + row + a) * pitch, cols), :
            ]
        pt_ref[a * depth : (a + 1) * depth, :] = flat_ref[...].T


def grad_kernel(cells, frame, count, begin, end, *refs):
    pts, dg_ref = refs[:count], refs[count]
    total_ref = None if begin else refs[count + 1]
    out_ref = refs[-1]
    block = 256
    for at in range(0, out_ref.shape[0], block):
        here = pl.ds(at, block)
        total = None if begin else total_ref[here, :]
        part = jnp.dot(
            pts[0][here, :], dg_ref[frame * cells : (frame + 1) * cells, :], preferred_element_type=F32
        )
        total = part if begin else total + part
        out_ref[here, :] = total.astype(out_ref.dtype)


def spec_v():
    return pl.BlockSpec(memory_space=pltpu.VMEM)


def spec_s():
    return pl.BlockSpec(memory_space=pltpu.SMEM)


def place_kernel(at_ref, come_ref, out_ref):
    for j in range(out_ref.shape[0]):
        out_ref[at_ref[j]] = come_ref[j]


RING = 4


def on_ring(own, ntile):
    def move(x, by):
        pairs = [(i, i // 16 * 16 + (i // RING + by) % RING * RING + i % RING) for i in range(ntile)]
        return lax.ppermute(x, "tile", pairs)

    return jnp.stack([own] + [move(own, h) for h in (1, -1, 2)])


def all_rows(near, ntile, tile):
    members = ntile // RING
    groups = [
        [plane * 16 + z * RING + y for plane in range(members // RING) for y in range(RING)] for z in range(RING)
    ]
    come = lax.all_to_all(
        jnp.tile(near, (members, 1, 1)), "tile", 0, 0, axis_index_groups=groups, tiled=True
    )
    z = tile // RING % RING
    at = [
        plane * 16 + (z - h) % RING * RING + y
        for plane in range(members // RING)
        for y in range(RING)
        for h in (0, 1, -1, 2)
    ]
    return pl.pallas_call(
        place_kernel,
        out_shape=in_vmem(come.shape, BF),
        in_specs=[spec_s(), spec_v()],
        out_specs=spec_v(),
        compiler_params=params(16),
        cost_estimate=pl.CostEstimate(flops=0, bytes_accessed=4 << 20, transcendentals=0),
    )(jnp.stack(at).astype(jnp.int32), come)


def on_device(layer_input, hidden_prev, cell_prev, out_cot, bias, master, moment1, moment2):
    frames, rows, cols, width = (layer_input.shape[i] for i in (1, 3, 4, 5))
    ngate = 4 * width
    layers = lax.axis_size("section")
    layer = lax.axis_index("section")
    ntile = lax.axis_size("tile")
    tile = lax.axis_index("tile")
    ncols = ntile // TILE_ROWS
    pitch = cols + 2 * SIDE
    edge = frames + layers - 1

    near = on_ring(master[0].astype(BF), ntile)
    kernel = all_rows(near, ntile, tile).reshape(-1, ngate)

    ids = (frames - 1 + layers - 1 - layer).astype(jnp.int32).reshape(1)
    packed = jnp.concatenate(
        [layer_input[0, :, 0], hidden_prev[0, :, 0], cell_prev[0, :, 0].astype(BF), out_cot[:, 0]], -1
    )
    deeps = [edge + 1 - (frames - 1 - f) for f in range(frames)]
    grid_row, grid_col = tile // ncols, tile % ncols

    def around(by, strip, keep):
        got = lax.ppermute(strip, "tile", [(i, by(i)) for i in range(ntile)])
        return jnp.where(keep, got, jnp.zeros_like(got))

    to_right = lambda i: i // ncols * ncols + (i + 1) % ncols
    to_left = lambda i: i // ncols * ncols + (i - 1) % ncols
    downs = jnp.concatenate([packed[f, rows - deeps[f] :] for f in range(frames)], 0)
    ups = jnp.concatenate([packed[f, : deeps[f]] for f in range(frames)], 0)
    mids = packed.reshape(frames * rows, cols, 4 * width)
    mid_right, mid_left = mids[:, cols - SIDE :], mids[:, :SIDE]
    downs, ups, mid_right, mid_left, _ = lax.optimization_barrier((downs, ups, mid_right, mid_left, near))
    above = around(lambda i: (i + ncols) % ntile, downs, grid_row > 0)
    below = around(lambda i: (i - ncols) % ntile, ups, grid_row < TILE_ROWS - 1)
    left = around(to_right, mid_right, grid_col > 0)
    right = around(to_left, mid_left, grid_col < ncols - 1)
    late, _ = lax.optimization_barrier(
        ((layer_input[0, :, 0], hidden_prev[0, :, 0], cell_prev[0, :, 0], out_cot[:, 0]), (above, below))
    )
    tiles = jnp.concatenate([x.astype(BF) for x in late], -1)
    tips = jnp.concatenate([above, below], 0)
    left_tips = around(to_right, tips[:, cols - SIDE :], grid_col > 0)
    right_tips = around(to_left, tips[:, :SIDE], grid_col < ncols - 1)

    size_e = LEAD + (rows + 2 * edge + 2) * pitch
    size_d = LEAD + (rows + 2 * edge) * pitch
    cells = rows * cols

    at = jnp.arange(size_d, dtype=jnp.int32) - LEAD + SIDE
    at, _ = lax.optimization_barrier((at, tiles))
    row_at = at // pitch - edge + grid_row * rows
    col_at = at % pitch - SIDE + grid_col * cols
    inside = (row_at >= 0) & (row_at < TILE_ROWS * rows) & (col_at >= 0) & (col_at < ncols * cols)
    mask = jnp.broadcast_to(inside[:, None], (size_d, width)).astype(BF)

    facs, pts, owns = [None] * frames, [None] * frames, [None] * frames
    for f in reversed(range(frames)):
        gap = edge + 1 - deeps[f]
        at_row = sum(deeps[:f])
        facs[f], zs, owns[f] = pl.pallas_call(
            functools.partial(
                gates_kernel, pitch, width, deeps[f], gap, at_row, sum(deeps) + at_row, f * rows
            ),
            out_shape=(
                in_vmem((size_d, 6 * width), F32),
                in_vmem((size_e, 6 * width), BF),
                in_vmem((size_e, width), BF),
            ),
            in_specs=[spec_s()] + [spec_v()] * 10,
            out_specs=(spec_v(),) * 3,
            scratch_shapes=[pltpu.VMEM((size_e, width), BF), pltpu.VMEM((size_e + 16, 2 * width), F32)],
            compiler_params=params(20),
            cost_estimate=pl.CostEstimate(
                flops=2 * size_d * 18 * width * ngate, bytes_accessed=10 << 20, transcendentals=size_d * 5 * width
            ),
        )(ids, tiles[f], above, below, left, right, left_tips, right_tips, mask, kernel, bias)
        pts[f] = pl.pallas_call(
            functools.partial(patch_kernel, pitch, rows, cols, edge),
            out_shape=in_vmem((18 * width, cells), BF),
            in_specs=[spec_v()],
            out_specs=spec_v(),
            scratch_shapes=[pltpu.VMEM((cells, 6 * width), BF)],
            compiler_params=params(16),
            cost_estimate=pl.CostEstimate(flops=0, bytes_accessed=8 << 20, transcendentals=0),
        )(zs)
    kernel_t = pl.pallas_call(
        turn_kernel,
        out_shape=in_vmem((3 * ngate, 6 * width), BF),
        in_specs=[spec_v()],
        out_specs=spec_v(),
        compiler_params=params(16),
        cost_estimate=pl.CostEstimate(flops=0, bytes_accessed=4 << 20, transcendentals=0),
    )(kernel)

    steps = layers + frames - 1
    upper, lower = tuple(range(layers // 2, layers)), tuple(range(layers // 2))
    states = {upper: None, lower: None}
    sent = {}
    kept = None
    total = None
    for step in range(steps):
        margin = edge - step
        size_z = LEAD + (rows + 2 * margin - 2) * pitch
        fresh = {}
        for group in (upper, lower):
            picks = picks_of(step, group, layers, frames)
            if not picks:
                continue
            has_inc, has_state, has_kept = needs_of(step, group, layers, frames)
            args = [ids, kernel_t] + [facs[f] for f in picks]
            if layers - 1 in group and step < frames:
                args.append(owns[frames - 1 - step])
            if has_inc:
                above_of = [frames - 1 - step + layers - f for f in picks]
                args += [sent[i] for i in above_of if i < layers]
            if has_state:
                args += list(states[group])
            if has_kept:
                args += list(kept)
            last = picks == [0]
            dx, cots, dgates, *state = pl.pallas_call(
                functools.partial(step_kernel, step, group, layers, frames, pitch, rows, cols, width),
                out_shape=(
                    jax.ShapeDtypeStruct((size_z, width), BF),
                    in_vmem((frames * cells, width), BF),
                    in_vmem((frames * cells, ngate), BF),
                )
                + (in_vmem((size_z, width), F32),) * (0 if last else 2),
                in_specs=[spec_s()] + [spec_v()] * (len(args) - 1),
                out_specs=(spec_v(),) * (3 if last else 5),
                scratch_shapes=[
                    pltpu.VMEM((size_z + 2 * pitch, ngate), BF),
                    pltpu.VMEM((size_z + 16, (3 if last else 6) * width), F32),
                ],
                input_output_aliases={len(args) - 2: 1, len(args) - 1: 2} if has_kept else {},
                compiler_params=params(20),
                cost_estimate=pl.CostEstimate(
                    flops=2 * size_z * 18 * width * ngate, bytes_accessed=10 << 20, transcendentals=0
                ),
            )(*args)
            kept = (cots, dgates)
            states[group] = tuple(state)
            for i in group:
                if i > 0 and 0 <= frames - 1 - step + layers - 1 - i < frames:
                    fresh[i] = lax.ppermute(dx, "section", [(i, i - 1)])
        sent = fresh
        if step >= layers - 1:
            f = frames - 1 - (step - layers + 1)
            end = step == steps - 1
            args = [pts[f], kept[1]] + ([] if total is None else [total])
            total = pl.pallas_call(
                functools.partial(grad_kernel, cells, f, 1, total is None, end),
                out_shape=in_vmem((18 * width, ngate), BF if end else F32),
                in_specs=[spec_v()] * len(args),
                out_specs=spec_v(),
                compiler_params=params(16),
                cost_estimate=pl.CostEstimate(
                    flops=2 * cells * 18 * width * ngate, bytes_accessed=4 << 20, transcendentals=0
                ),
            )(*args)
    cots = kept[0]
    total, cots = lax.optimization_barrier((total, cots))
    arrived = lax.all_to_all(total, "tile", 0, 0, tiled=True)
    arrived, cots = lax.optimization_barrier((arrived, cots))
    input_cot = cots.reshape(frames, rows, cols, width)
    grad_rows = jnp.sum(arrived.reshape(ntile, -1, ngate).astype(F32), 0)
    new_moment1 = 0.9 * moment1[0] + 0.1 * grad_rows
    new_moment2 = 0.999 * moment2[0] + 0.001 * grad_rows * grad_rows
    fix1 = 1.0 - 0.9**10
    fix2 = 1.0 - 0.999**10
    step_size = new_moment1 / fix1 / (jnp.sqrt(new_moment2 / fix2) + 1e-08)
    new_master = master[0] - 0.001 * step_size - 0.0001 * master[0]
    return (input_cot[None, :, None], new_master[None], new_moment1[None], new_moment2[None])


def solution(mesh):
    return jax.shard_map(
        on_device,
        mesh=mesh,
        in_specs=(
            P("section", None, "tile", None, None, None),
            P("section", None, "tile", None, None, None),
            P("section", None, "tile", None, None, None),
            P(None, "tile", None, None, None),
            P("section", None),
            P("section", "tile", None),
            P("section", "tile", None),
            P("section", "tile", None),
        ),
        out_specs=(
            P("section", None, "tile", None, None, None),
            P("section", "tile", None),
            P("section", "tile", None),
            P("section", "tile", None),
        ),
        check_vma=False,
    )
```

```python
import functools

import jax
import jax.numpy as jnp
from jax import lax
from jax.experimental import pallas as pl
from jax.experimental.pallas import tpu as pltpu
from jax.sharding import PartitionSpec as P

TILE_ROWS = 4
BF = jnp.bfloat16
F32 = jnp.float32
SIDE = 8
LEAD = 16


def params(mib):
    return pltpu.CompilerParams(vmem_limit_bytes=mib << 20)


def chunks(size, most):
    units = size // 16
    count = -(-units * 16 // most)
    out, at = [], 0
    for i in range(count):
        end = units * (i + 1) // count
        out.append((at * 16, (end - at) * 16))
        at = end
    return out


def in_vmem(shape, dtype):
    return pltpu.VMEM(shape, dtype)


def sigmoid(x):
    return 0.5 * jnp.tanh(0.5 * x) + 0.5


def gates_kernel(pitch, width, deep, gap, at_row, at_tip, at_side, ids_ref, mid_ref, above_ref, below_ref, left_ref, right_ref, left_tip_ref, right_tip_ref, mask_ref, kernel_ref, bias_ref, fac_ref, zs_ref, own_ref, flat_ref, z_ref):
    depth = 6 * width
    rows = mid_ref.shape[0]
    cols = pitch - 2 * SIDE
    tall = rows + 2 * deep
    size_e = zs_ref.shape[0]
    begin = gap * pitch
    stop = begin + LEAD + tall * pitch
    if gap:
        for lo, hi in ((0, begin), (stop, size_e)):
            z_ref[8 + lo : 8 + hi, :] = jnp.zeros((hi - lo, 2 * width), F32)
            zs_ref[lo:hi, 2 * width : 4 * width] = jnp.zeros((hi - lo, 2 * width), BF)
            flat_ref[lo:hi, :] = jnp.zeros((hi - lo, width), BF)
            own_ref[lo:hi, :] = jnp.zeros((hi - lo, width), BF)
    z_ref[0:8, :] = jnp.zeros((8, 2 * width), F32)
    z_ref[8 + size_e :, :] = jnp.zeros((8, 2 * width), F32)

    def put(at, value):
        size = value.shape[0]
        z_ref[8 + at : 8 + at + size, :] = value[:, : 2 * width].astype(F32)
        zs_ref[at : at + size, 2 * width : 4 * width] = value[:, : 2 * width]
        flat_ref[at : at + size, :] = value[:, 2 * width : 3 * width]
        own_ref[at : at + size, :] = value[:, 3 * width :]

    def beside(side_ref, tip_ref, row):
        if row < 0 or row >= tall:
            return jnp.zeros((SIDE, 4 * width), BF)
        if row < deep:
            return tip_ref[at_row + row]
        if row < deep + rows:
            return side_ref[at_side + row - deep]
        return tip_ref[at_tip + row - deep - rows]

    for row in range(tall + 1):
        before = beside(right_ref, right_tip_ref, row - 1)
        after = beside(left_ref, left_tip_ref, row)
        put(begin + row * pitch, jnp.concatenate([before, after], 0))
    for row in range(tall):
        at = begin + LEAD + row * pitch
        if row < deep:
            put(at, above_ref[at_row + row])
        elif row < deep + rows:
            put(at, mid_ref[row - deep])
        else:
            put(at, below_ref[at_row + row - deep - rows])
    for start, size in chunks(size_e, 256):
        here = pl.ds(start, size)
        for b in (0, 2):
            zs_ref[here, b * 2 * width : (b + 1) * 2 * width] = z_ref[
                7 + b + start : 7 + b + start + size, :
            ].astype(BF)
    cells = fac_ref.shape[0] - 2 * begin
    for start, size in chunks(cells, 480):
        start = start + begin
        total = bias_ref[...]
        for a in range(3):
            total = total + jnp.dot(
                zs_ref[pl.ds(start + a * pitch, size), :],
                kernel_ref[a * depth : (a + 1) * depth, :],
                preferred_element_type=F32,
            )
        here = pl.ds(start, size)
        mask = mask_ref[here, :].astype(F32)
        c_prev = flat_ref[pl.ds(start + pitch, size), :].astype(F32)
        i = sigmoid(total[:, :width])
        f = sigmoid(total[:, width : 2 * width])
        g = jnp.tanh(total[:, 2 * width : 3 * width])
        o = sigmoid(total[:, 3 * width :])
        tc = jnp.tanh(f * c_prev + i * g)
        fac_ref[here, 0:width] = o * (1.0 - tc * tc)
        fac_ref[here, width : 2 * width] = mask * g * i * (1.0 - i)
        fac_ref[here, 2 * width : 3 * width] = mask * c_prev * f * (1.0 - f)
        fac_ref[here, 3 * width : 4 * width] = mask * i * (1.0 - g * g)
        fac_ref[here, 4 * width : 5 * width] = mask * tc * o * (1.0 - o)
        fac_ref[here, 5 * width : 6 * width] = f


def turn_kernel(kernel_ref, turned_ref):
    depth, ngate = kernel_ref.shape[0] // 3, kernel_ref.shape[1]
    for a in range(3):
        turned_ref[a * ngate : (a + 1) * ngate, :] = kernel_ref[a * depth : (a + 1) * depth, :].T


def step_kernel(step, group, layers, frames, pitch, rows, cols, width, *refs):
    ids_ref, kernel_t_ref = refs[0], refs[1]
    picks = picks_of(step, group, layers, frames)
    fac_refs = refs[2 : 2 + len(picks)]
    at = 2 + len(picks)
    tops = layers - 1 in group and step < frames
    own_ref = refs[at] if tops else None
    at += 1 if tops else 0
    has_inc, has_state, has_kept = needs_of(step, group, layers, frames)
    inc_refs = {}
    for f in picks:
        if frames - 1 - step + layers - f < layers:
            inc_refs[f] = refs[at]
            at += 1
    if has_state:
        dh_ref, dc_ref = refs[at : at + 2]
        at += 2
    if has_kept:
        at += 2
    last = picks == [0]
    dx_ref, dxi_ref, dgi_ref = refs[at : at + 3]
    dhn_ref, dcn_ref = (None, None) if last else refs[at + 3 : at + 5]
    d_ref, p_ref = refs[-2:]
    part = width if last else 2 * width
    margin = frames + layers - 1 - step
    size_d = LEAD + (rows + 2 * margin) * pitch
    size_z = LEAD + (rows + 2 * margin - 2) * pitch
    frame = ids_ref[0] - step
    ngate = 4 * width

    def point(fac_ref, top_frame, pick):
        start_frame = pick == frames - 1
        for start, size in chunks(size_d, 256):
            here = pl.ds(start, size)
            there = pl.ds(start + step * pitch, size)
            if tops and pick == top_frame:
                above = own_ref[pl.ds(start + (step + 1) * pitch, size), :].astype(F32)
            else:
                above = inc_refs[pick][here, :].astype(F32)
            dh = above
            if not start_frame:
                dh = dh + dh_ref[here, :]
            dc = dh * fac_ref[there, 0:width]
            if not start_frame:
                dc = dc + dc_ref[here, :]
            d_ref[here, 0:width] = (dc * fac_ref[there, width : 2 * width]).astype(BF)
            d_ref[here, width : 2 * width] = (dc * fac_ref[there, 2 * width : 3 * width]).astype(BF)
            d_ref[here, 2 * width : 3 * width] = (dc * fac_ref[there, 3 * width : 4 * width]).astype(BF)
            d_ref[here, 3 * width :] = (dh * fac_ref[there, 4 * width : 5 * width]).astype(BF)
            lo, hi = max(start, pitch), min(start + size, pitch + size_z)
            if hi > lo and not last:
                rec = dc * fac_ref[there, 5 * width :]
                dcn_ref[lo - pitch : hi - pitch, :] = rec[lo - start : hi - start, :]

    top_frame = frames - 1 - step
    for number, pick in enumerate(picks):
        pl.when(frame == pick)(functools.partial(point, fac_refs[number], top_frame, pick))

    active = (frame >= picks[0]) & (frame <= picks[-1])

    @pl.when(active)
    def _():
        slot = pl.multiple_of(frame * (rows * cols), rows * cols)
        for row in range(rows):
            dgi_ref[pl.ds(slot + row * cols, cols), :] = d_ref[
                pl.ds(LEAD + (row + margin) * pitch, cols), :
            ]
        p_ref[0:8, :] = jnp.zeros((8, 3 * part), F32)
        p_ref[8 + size_z : 16 + size_z, :] = jnp.zeros((8, 3 * part), F32)
        def turned(a):
            here = slice(a * ngate, (a + 1) * ngate)
            if not last:
                return kernel_t_ref[here, :]
            return jnp.concatenate(
                [kernel_t_ref[here, b * 2 * width : b * 2 * width + width] for b in range(3)], 1
            )

        for start, size in chunks(size_z, 448):
            total = None
            for a in range(3):
                term = jnp.dot(
                    d_ref[pl.ds(start + (2 - a) * pitch, size), :], turned(a), preferred_element_type=F32
                )
                total = term if total is None else total + term
            p_ref[pl.ds(8 + start, size), :] = total
        for start, size in chunks(size_z, 256):
            dz = (
                p_ref[pl.ds(8 + start, size), part : 2 * part]
                + p_ref[pl.ds(9 + start, size), 0:part]
                + p_ref[pl.ds(7 + start, size), 2 * part :]
            )
            dx_ref[pl.ds(start, size), :] = dz[:, :width].astype(BF)
            if not last:
                dhn_ref[pl.ds(start, size), :] = dz[:, width:]
        for row in range(rows):
            dxi_ref[pl.ds(slot + row * cols, cols), :] = dx_ref[
                pl.ds(LEAD + (row + margin - 1) * pitch, cols), :
            ]


def picks_of(step, group, layers, frames):
    now = [frames - 1 - step + layers - 1 - layer for layer in group]
    return sorted(f for f in now if 0 <= f < frames)


def needs_of(step, group, layers, frames):
    has_inc = any(
        0 <= frames - 1 - step + layers - 1 - layer < frames for layer in group if layer < layers - 1
    )
    has_state = any(f < frames - 1 for f in picks_of(step, group, layers, frames))
    return has_inc, has_state, step > 0


def patch_kernel(pitch, rows, cols, edge, zs_ref, pt_ref, flat_ref):
    depth = zs_ref.shape[1]
    for a in range(3):
        for row in range(rows):
            flat_ref[row * cols : (row + 1) * cols, :] = zs_ref[
                pl.ds(LEAD + (edge + row + a) * pitch, cols), :
            ]
        pt_ref[a * depth : (a + 1) * depth, :] = flat_ref[...].T


def grad_kernel(cells, frame, count, begin, end, *refs):
    pts, dg_ref = refs[:count], refs[count]
    total_ref = None if begin else refs[count + 1]
    out_ref = refs[-1]
    block = 256
    for at in range(0, out_ref.shape[0], block):
        here = pl.ds(at, block)
        total = None if begin else total_ref[here, :]
        part = jnp.dot(
            pts[0][here, :], dg_ref[frame * cells : (frame + 1) * cells, :], preferred_element_type=F32
        )
        total = part if begin else total + part
        out_ref[here, :] = total.astype(out_ref.dtype)


def spec_v():
    return pl.BlockSpec(memory_space=pltpu.VMEM)


def spec_s():
    return pl.BlockSpec(memory_space=pltpu.SMEM)


def place_kernel(at_ref, come_ref, out_ref):
    for j in range(out_ref.shape[0]):
        out_ref[at_ref[j]] = come_ref[j]


RING = 4


def on_ring(own, ntile):
    def move(x, by):
        pairs = [(i, i // 16 * 16 + (i // RING + by) % RING * RING + i % RING) for i in range(ntile)]
        return lax.ppermute(x, "tile", pairs)

    return jnp.stack([own] + [move(own, h) for h in (1, -1, 2)])


def all_rows(near, ntile, tile):
    members = ntile // RING
    groups = [
        [plane * 16 + z * RING + y for plane in range(members // RING) for y in range(RING)] for z in range(RING)
    ]
    come = lax.all_to_all(
        jnp.tile(near, (members, 1, 1)), "tile", 0, 0, axis_index_groups=groups, tiled=True
    )
    z = tile // RING % RING
    at = [
        plane * 16 + (z - h) % RING * RING + y
        for plane in range(members // RING)
        for y in range(RING)
        for h in (0, 1, -1, 2)
    ]
    return pl.pallas_call(
        place_kernel,
        out_shape=in_vmem(come.shape, BF),
        in_specs=[spec_s(), spec_v()],
        out_specs=spec_v(),
        compiler_params=params(16),
        cost_estimate=pl.CostEstimate(flops=0, bytes_accessed=4 << 20, transcendentals=0),
    )(jnp.stack(at).astype(jnp.int32), come)


def on_device(layer_input, hidden_prev, cell_prev, out_cot, bias, master, moment1, moment2):
    frames, rows, cols, width = (layer_input.shape[i] for i in (1, 3, 4, 5))
    ngate = 4 * width
    layers = lax.axis_size("section")
    layer = lax.axis_index("section")
    ntile = lax.axis_size("tile")
    tile = lax.axis_index("tile")
    ncols = ntile // TILE_ROWS
    pitch = cols + 2 * SIDE
    edge = frames + layers - 1

    near = on_ring(master[0].astype(BF), ntile)
    kernel = all_rows(near, ntile, tile).reshape(-1, ngate)

    ids = (frames - 1 + layers - 1 - layer).astype(jnp.int32).reshape(1)
    packed = jnp.concatenate(
        [layer_input[0, :, 0], hidden_prev[0, :, 0], cell_prev[0, :, 0].astype(BF), out_cot[:, 0]], -1
    )
    deeps = [edge + 1 - (frames - 1 - f) for f in range(frames)]
    grid_row, grid_col = tile // ncols, tile % ncols

    def around(by, strip, keep):
        got = lax.ppermute(strip, "tile", [(i, by(i)) for i in range(ntile)])
        return jnp.where(keep, got, jnp.zeros_like(got))

    to_right = lambda i: i // ncols * ncols + (i + 1) % ncols
    to_left = lambda i: i // ncols * ncols + (i - 1) % ncols
    downs = jnp.concatenate([packed[f, rows - deeps[f] :] for f in range(frames)], 0)
    ups = jnp.concatenate([packed[f, : deeps[f]] for f in range(frames)], 0)
    mids = packed.reshape(frames * rows, cols, 4 * width)
    mid_right, mid_left = mids[:, cols - SIDE :], mids[:, :SIDE]
    downs, ups, mid_right, mid_left, _ = lax.optimization_barrier((downs, ups, mid_right, mid_left, near))
    above = around(lambda i: (i + ncols) % ntile, downs, grid_row > 0)
    below = around(lambda i: (i - ncols) % ntile, ups, grid_row < TILE_ROWS - 1)
    left = around(to_right, mid_right, grid_col > 0)
    right = around(to_left, mid_left, grid_col < ncols - 1)
    late, _ = lax.optimization_barrier(
        ((layer_input[0, :, 0], hidden_prev[0, :, 0], cell_prev[0, :, 0], out_cot[:, 0]), (above, below))
    )
    tiles = jnp.concatenate([x.astype(BF) for x in late], -1)
    tips = jnp.concatenate([above, below], 0)
    left_tips = around(to_right, tips[:, cols - SIDE :], grid_col > 0)
    right_tips = around(to_left, tips[:, :SIDE], grid_col < ncols - 1)

    size_e = LEAD + (rows + 2 * edge + 2) * pitch
    size_d = LEAD + (rows + 2 * edge) * pitch
    cells = rows * cols

    at = jnp.arange(size_d, dtype=jnp.int32) - LEAD + SIDE
    at, _ = lax.optimization_barrier((at, tiles))
    row_at = at // pitch - edge + grid_row * rows
    col_at = at % pitch - SIDE + grid_col * cols
    inside = (row_at >= 0) & (row_at < TILE_ROWS * rows) & (col_at >= 0) & (col_at < ncols * cols)
    mask = jnp.broadcast_to(inside[:, None], (size_d, width)).astype(BF)

    facs, pts, owns = [None] * frames, [None] * frames, [None] * frames
    for f in reversed(range(frames)):
        gap = edge + 1 - deeps[f]
        at_row = sum(deeps[:f])
        facs[f], zs, owns[f] = pl.pallas_call(
            functools.partial(
                gates_kernel, pitch, width, deeps[f], gap, at_row, sum(deeps) + at_row, f * rows
            ),
            out_shape=(
                in_vmem((size_d, 6 * width), F32),
                in_vmem((size_e, 6 * width), BF),
                in_vmem((size_e, width), BF),
            ),
            in_specs=[spec_s()] + [spec_v()] * 10,
            out_specs=(spec_v(),) * 3,
            scratch_shapes=[pltpu.VMEM((size_e, width), BF), pltpu.VMEM((size_e + 16, 2 * width), F32)],
            compiler_params=params(20),
            cost_estimate=pl.CostEstimate(
                flops=2 * size_d * 18 * width * ngate, bytes_accessed=10 << 20, transcendentals=size_d * 5 * width
            ),
        )(ids, tiles[f], above, below, left, right, left_tips, right_tips, mask, kernel, bias)
        pts[f] = pl.pallas_call(
            functools.partial(patch_kernel, pitch, rows, cols, edge),
            out_shape=in_vmem((18 * width, cells), BF),
            in_specs=[spec_v()],
            out_specs=spec_v(),
            scratch_shapes=[pltpu.VMEM((cells, 6 * width), BF)],
            compiler_params=params(16),
            cost_estimate=pl.CostEstimate(flops=0, bytes_accessed=8 << 20, transcendentals=0),
        )(zs)
    kernel_t = pl.pallas_call(
        turn_kernel,
        out_shape=in_vmem((3 * ngate, 6 * width), BF),
        in_specs=[spec_v()],
        out_specs=spec_v(),
        compiler_params=params(16),
        cost_estimate=pl.CostEstimate(flops=0, bytes_accessed=4 << 20, transcendentals=0),
    )(kernel)

    steps = layers + frames - 1
    upper, lower = tuple(range(layers // 2, layers)), tuple(range(layers // 2))
    states = {upper: None, lower: None}
    sent = {}
    kept = None
    total = None
    for step in range(steps):
        margin = edge - step
        size_z = LEAD + (rows + 2 * margin - 2) * pitch
        fresh = {}
        for group in (upper, lower):
            picks = picks_of(step, group, layers, frames)
            if not picks:
                continue
            has_inc, has_state, has_kept = needs_of(step, group, layers, frames)
            args = [ids, kernel_t] + [facs[f] for f in picks]
            if layers - 1 in group and step < frames:
                args.append(owns[frames - 1 - step])
            if has_inc:
                above_of = [frames - 1 - step + layers - f for f in picks]
                args += [sent[i] for i in above_of if i < layers]
            if has_state:
                args += list(states[group])
            if has_kept:
                args += list(kept)
            last = picks == [0]
            dx, cots, dgates, *state = pl.pallas_call(
                functools.partial(step_kernel, step, group, layers, frames, pitch, rows, cols, width),
                out_shape=(
                    jax.ShapeDtypeStruct((size_z, width), BF),
                    in_vmem((frames * cells, width), BF),
                    in_vmem((frames * cells, ngate), BF),
                )
                + (in_vmem((size_z, width), F32),) * (0 if last else 2),
                in_specs=[spec_s()] + [spec_v()] * (len(args) - 1),
                out_specs=(spec_v(),) * (3 if last else 5),
                scratch_shapes=[
                    pltpu.VMEM((size_z + 2 * pitch, ngate), BF),
                    pltpu.VMEM((size_z + 16, (3 if last else 6) * width), F32),
                ],
                input_output_aliases={len(args) - 2: 1, len(args) - 1: 2} if has_kept else {},
                compiler_params=params(20),
                cost_estimate=pl.CostEstimate(
                    flops=2 * size_z * 18 * width * ngate, bytes_accessed=10 << 20, transcendentals=0
                ),
            )(*args)
            kept = (cots, dgates)
            states[group] = tuple(state)
            for i in group:
                if i > 0 and 0 <= frames - 1 - step + layers - 1 - i < frames:
                    fresh[i] = lax.ppermute(dx, "section", [(i, i - 1)])
        sent = fresh
        if step >= layers - 1:
            f = frames - 1 - (step - layers + 1)
            end = step == steps - 1
            args = [pts[f], kept[1]] + ([] if total is None else [total])
            total = pl.pallas_call(
                functools.partial(grad_kernel, cells, f, 1, total is None, end),
                out_shape=in_vmem((18 * width, ngate), BF if end else F32),
                in_specs=[spec_v()] * len(args),
                out_specs=spec_v(),
                compiler_params=params(16),
                cost_estimate=pl.CostEstimate(
                    flops=2 * cells * 18 * width * ngate, bytes_accessed=4 << 20, transcendentals=0
                ),
            )(*args)
    cots = kept[0]
    arrived = lax.all_to_all(total, "tile", 0, 0, tiled=True)
    input_cot = cots.reshape(frames, rows, cols, width)
    grad_rows = jnp.sum(arrived.reshape(ntile, -1, ngate).astype(F32), 0)
    new_moment1 = 0.9 * moment1[0] + 0.1 * grad_rows
    new_moment2 = 0.999 * moment2[0] + 0.001 * grad_rows * grad_rows
    fix1 = 1.0 - 0.9**10
    fix2 = 1.0 - 0.999**10
    step_size = new_moment1 / fix1 / (jnp.sqrt(new_moment2 / fix2) + 1e-08)
    new_master = master[0] - 0.001 * step_size - 0.0001 * master[0]
    return (input_cot[None, :, None], new_master[None], new_moment1[None], new_moment2[None])


def solution(mesh):
    return jax.shard_map(
        on_device,
        mesh=mesh,
        in_specs=(
            P("section", None, "tile", None, None, None),
            P("section", None, "tile", None, None, None),
            P("section", None, "tile", None, None, None),
            P(None, "tile", None, None, None),
            P("section", None),
            P("section", "tile", None),
            P("section", "tile", None),
            P("section", "tile", None),
        ),
        out_specs=(
            P("section", None, "tile", None, None, None),
            P("section", "tile", None),
            P("section", "tile", None),
            P("section", "tile", None),
        ),
        check_vma=False,
    )
```
